32 devices in a mesh: section: 2 (over core), dp: 16 (over z, y, x).
Axes of the slice: x: 2, y: 2, z: 4, core: 2. Of those that a mesh axis runs over, the one named last changes fastest.
Arguments:
- tokens: bfloat16 [32, 196, 768], P('dp'), may hold values from -6 to 6
- patch_mask: int32 [32, 196], P('dp'), may hold values from 0 to 1, as said below
- cotangent: bfloat16 [2, 32, 196, 768], P('section', 'dp'), may hold values from -6 to 6
- in_weight: bfloat16 [2, 768, 2304], P('section'), may hold values from -0.21875 to 0.21875
- out_weight: bfloat16 [2, 768, 768], P('section'), may hold values from -1.75 to 1.75
- up_weight: bfloat16 [2, 768, 3072], P('section'), may hold values from -0.21875 to 0.21875
- down_weight: bfloat16 [2, 3072, 768], P('section'), may hold values from -0.109375 to 0.109375
- gains: float32 [2, 4, 768], P('section'), may hold values from 0.1 to 1.9
- biases: float32 [2, 5, 768], P('section'), may hold values from -1.8 to 1.8
- up_bias: float32 [2, 3072], P('section'), may hold values from -1.8 to 1.8
- down_bias: float32 [2, 768], P('section'), may hold values from -1.8 to 1.8
Outputs:
- block_outputs: bfloat16 [2, 32, 196, 768], P('section', 'dp')
- token_grads: float32 [2, 32, 196, 768], P('section', 'dp')
- in_grad: float32 [2, 768, 2304], P('section', None, 'dp')
- out_grad: float32 [2, 768, 768], P('section', None, 'dp')
- up_grad: float32 [2, 768, 3072], P('section', None, 'dp')
- down_grad: float32 [2, 3072, 768], P('section', None, 'dp')
- gain_grad: float32 [2, 4, 768], P('section', None, 'dp')
- bias_grad: float32 [2, 5, 768], P('section', None, 'dp')
- up_bias_grad: float32 [2, 3072], P('section', 'dp')
- down_bias_grad: float32 [2, 768], P('section', 'dp')
The draws below stay inside these ranges and needn't reach their ends.
Inputs may be any that keep to these rules, and one draw needn't show every extreme that they name: `patch_mask`: each image masks between 59 and 117 of its 196 patches; some image masks exactly 59 and another exactly 117.
All inputs are finite; a program needn't handle non-finite values.
Results may differ from the reference program's by a relative error of at most 0.012.
Values may be sent and summed in bfloat16 or wider, within the bound.
No kernel may reach another device: no remote copies, remote signals or barrier semaphores. Data moves between devices by JAX's collectives and lax.ppermute only.
A program may use at most 256 MiB of HBM per device.

```python
import jax
import jax.numpy as jnp
from jax import lax

D = 768
HEADS = 12
HEAD_DIM = 64
FF = 3072
P_SIZE = 196
IMAGES = 32
MASK_LO = 59
MASK_HI = 117


def draw_patch_mask(key, part):
    key = jax.random.fold_in(key, 11)
    key_count, key_pick, key_other, key_order = jax.random.split(key, 4)
    counts = jax.random.randint(key_count, (IMAGES,), MASK_LO, MASK_HI + 1)
    lowest_image = jax.random.randint(key_pick, (), 0, IMAGES)
    highest_image = (lowest_image + 1 + jax.random.randint(key_other, (), 0, IMAGES - 1)) % IMAGES
    positions = jnp.arange(IMAGES)
    counts = jnp.where(positions == lowest_image, MASK_LO, counts)
    counts = jnp.where(positions == highest_image, MASK_HI, counts)
    orderings = jax.vmap(lambda single: jax.random.permutation(single, P_SIZE))(jax.random.split(key_order, IMAGES))
    return (orderings < counts[:, None]).astype(jnp.int32)


def shard_levels(rng, extent, shards, low, high):
    def one(dim, parts):
        steps = jax.random.uniform(jax.random.fold_in(jax.random.fold_in(rng, 6), dim), (parts,), jnp.float32, low / len(shards), high / len(shards))
        return jnp.repeat(jnp.exp(steps), extent[dim] // parts).reshape((-1,) + (1,) * (len(extent) - dim - 1))

    level = one(*shards[0])
    for cut in shards[1:]:
        level = level * one(*cut)
    return level


def noise(own_key, dims, scale, bound, cuts=(), kind=jnp.bfloat16):
    entries = jax.random.normal(own_key, dims, jnp.float32) * scale
    if len(cuts) > 0:
        entries = shard_levels(own_key, dims, cuts, -0.22, 0.18) * entries
    return jnp.clip(entries, min=-bound, max=bound).astype(kind)


def setup_inputs(seed: int = 0) -> dict:
    key_of = jax.random.split(jax.random.key(seed), 12)
    return {
        "tokens": noise(key_of[0], (IMAGES, P_SIZE, D), 1.0, 6.0, ((0, 16),)),
        "patch_mask": draw_patch_mask(jax.random.fold_in(key_of[11], 71), 0),
        "cotangent": noise(key_of[2], (2, IMAGES, P_SIZE, D), 1.0, 6.0, ((0, 2), (1, 16))),
        "in_weight": noise(key_of[3], (2, D, 3 * D), D ** -0.5, 0.21875, ((0, 2),)),
        "out_weight": noise(key_of[4], (2, D, D), (D // 64) ** -0.5, 1.75, ((0, 2),)),
        "up_weight": noise(key_of[5], (2, D, FF), D ** -0.5, 0.21875, ((0, 2),)),
        "down_weight": noise(key_of[6], (2, FF, D), FF ** -0.5, 0.109375, ((0, 2),)),
        "gains": jnp.clip(1.0 + 0.18 * jax.random.normal(key_of[7], (2, 4, D), jnp.float32), 0.1, 1.9),
        "biases": noise(key_of[8], (2, 5, D), 0.3, 1.8, ((0, 2),), jnp.float32),
        "up_bias": noise(key_of[9], (2, FF), 0.3, 1.8, ((0, 2),), jnp.float32),
        "down_bias": noise(key_of[10], (2, D), 0.3, 1.8, ((0, 2),), jnp.float32),
    }


@jax.custom_vjp
def low(v):
    return lax.optimization_barrier(v.astype(jnp.bfloat16)).astype(jnp.float32)

@jax.custom_vjp
def low_back(v):
    return v

def low_keep(v):
    return (low(v), None)

def low_pass(kept, grad):
    return (grad,)

def back_keep(v):
    return (v, None)

def back_low(kept, grad):
    return (low(grad),)
low.defvjp(low_keep, low_pass)
low_back.defvjp(back_keep, back_low)
epsilon = 1e-06

def layer_norm(states, gain, shift):
    centre = states - lax.optimization_barrier(jnp.mean(states, axis=-1, keepdims=True))
    spread = lax.optimization_barrier(jnp.mean(centre * centre, axis=-1, keepdims=True))
    return centre * lax.rsqrt(spread + epsilon) * gain + shift

def project(left, right):
    return jnp.einsum('bpd,de->bpe', left, right, precision=lax.Precision.HIGHEST)

def block(states, query_rows, key_rows, in_weight, out_weight, up_weight, down_weight, gains, biases, up_bias, down_bias):
    images, patches, width = states.shape
    normed = low(layer_norm(states, gains[0], biases[0]))
    joined_bias = jnp.concatenate([biases[1], jnp.zeros_like(biases[1]), biases[2]])
    projected = low_back(low(project(normed, in_weight) + joined_bias))
    pieces = projected.reshape(images, patches, 3, HEADS, HEAD_DIM)
    queries = pieces[:, :, 0]
    keys_all = pieces[:, :, 1]
    values_all = pieces[:, :, 2]
    scores = low_back(jnp.einsum('bqhd,bkhd->bhqk', queries, keys_all, precision=lax.Precision.HIGHEST))
    logits = jnp.where(key_rows[:, None, None, :] > 0, scores * HEAD_DIM ** (-0.5), -1e+30)
    probs = low(jax.nn.softmax(logits, axis=-1))
    mixed = jnp.einsum('bhqk,bkhd->bqhd', probs, values_all, precision=lax.Precision.HIGHEST)
    mixed = low_back(low(mixed.reshape(images, patches, width)))
    attended = low_back(project(mixed, out_weight) + biases[3])
    middle = states + gains[1] * attended * query_rows[..., None]
    hidden_in = low(layer_norm(middle, gains[2], biases[4]))
    hidden = low_back(project(hidden_in, up_weight) + up_bias)
    activated = low(jax.nn.gelu(hidden, approximate=False))
    lowered = low_back(project(activated, down_weight) + down_bias)
    return middle + gains[3] * lowered * query_rows[..., None]

def reference(tokens, patch_mask, cotangent, in_weight, out_weight, up_weight, down_weight, gains, biases, up_bias, down_bias):
    params = tuple((item.astype(jnp.float32) for item in (in_weight, out_weight, up_weight, down_weight, gains, biases, up_bias, down_bias)))
    images = tokens.shape[0]
    group = 1
    for option in range(1, 17):
        if images % option == 0:
            group = option
    count = images // group
    token_groups = tokens.astype(jnp.float32).reshape(count, group, P_SIZE, D)
    mask_groups = patch_mask.astype(jnp.float32).reshape(count, group, P_SIZE)
    cot_groups = cotangent.astype(jnp.float32).reshape(2, count, group, P_SIZE, D).transpose(1, 0, 2, 3, 4)

    def forward(token_block, masked, *weights):
        visible = 1.0 - masked
        first_block = [item[0] for item in weights]
        second_block = [item[1] for item in weights]
        encoded = block(token_block, visible, visible, *first_block)
        latent = low_back(low(encoded))
        regressor_in = jnp.where(masked[..., None] > 0, token_block, latent)
        regressed = block(regressor_in, masked, jnp.ones_like(masked), *second_block)
        return (encoded * visible[..., None], regressed * masked[..., None])

    def step(totals, inputs):
        token_block, masked, cot_block = inputs
        outputs, pullback = jax.vjp(lambda first_arg, *weights: forward(first_arg, masked, *weights), token_block, *params)
        grads = pullback((cot_block[0], cot_block[1]))
        totals = tuple((left + right for left, right in zip(totals, grads[1:])))
        token_grad = grads[0]
        split_grad = jnp.stack([token_grad * (1.0 - masked)[..., None], token_grad * masked[..., None]])
        return (totals, (jnp.stack(outputs), split_grad))
    init = tuple((jnp.zeros_like(item) for item in params))
    totals, (outputs, token_grads) = lax.scan(step, init, (token_groups, mask_groups, cot_groups))
    outputs = outputs.transpose(1, 0, 2, 3, 4).reshape(2, images, P_SIZE, D).astype(jnp.bfloat16)
    token_grads = token_grads.transpose(1, 0, 2, 3, 4).reshape(2, images, P_SIZE, D)
    return (outputs, token_grads, totals[0], totals[1], totals[2], totals[3], totals[4], totals[5], totals[6], totals[7])
```

```python
import functools

import jax
import jax.numpy as jnp
from jax import lax
from jax.experimental import pallas as pl
from jax.experimental.pallas import tpu as pltpu
from jax.sharding import PartitionSpec as P

HEADS = 12
HEAD_DIM = 64
PAIRS = HEADS // 2
LANES = 2 * HEAD_DIM
MASK_LO = 59
MASK_HI = 117
TILE = 768
MIB = 2**20

epsilon = 1e-06
f32 = jnp.float32
bf16 = jnp.bfloat16
ANY = pl.BlockSpec(memory_space=pl.ANY)
SMEM = pl.BlockSpec(memory_space=pltpu.SMEM)
VMEM = pl.BlockSpec(memory_space=pltpu.VMEM)


def up16(count):
    return -(-count // 16) * 16


class Rows:
    def __init__(self, first, images, patches):
        most = patches - MASK_LO if first else MASK_HI
        self.first = first
        self.images = images
        self.patches = patches
        self.top = up16(most)
        self.rest = 0 if first else up16(patches - self.top)
        self.keys = self.top + self.rest
        self.queries = images * self.top
        self.total = images * self.keys


def dot(left, right):
    return jnp.dot(left, right, preferred_element_type=f32)


def dot_nt(left, right):
    return lax.dot_general(left, right, (((1,), (1,)), ((), ())), preferred_element_type=f32)


def dot_tn(left, right):
    return lax.dot_general(left, right, (((0,), (0,)), ((), ())), preferred_element_type=f32)


def iota(shape, dim):
    return lax.broadcasted_iota(jnp.int32, shape, dim)


def sort_rows(mask_ref, rows):
    masked = mask_ref[...].astype(f32)
    flag = 1.0 - masked if rows.first else masked
    n = rows.patches
    tri = jnp.where(iota((n, n), 0) <= iota((n, n), 1), 1.0, 0.0).astype(bf16)
    upto = dot(flag.astype(bf16), tri)
    count = jnp.sum(flag, axis=1, keepdims=True)
    at = iota(flag.shape, 1).astype(f32)
    place = jnp.where(flag > 0, upto - 1.0, count + at - upto)
    return flag, place, count


def pick(place, image, start, length):
    slots = iota((length, place.shape[1]), 0).astype(f32) + float(start)
    return jnp.where(slots == place[image : image + 1, :], 1.0, 0.0)


def valid_rows(count, rows):
    parts = [
        jnp.where(iota((rows.top, 1), 0).astype(f32) < count[b : b + 1, :], 1.0, 0.0)
        for b in range(rows.images)
    ]
    return jnp.concatenate(parts, axis=0)


def normed(states):
    centre = states - jnp.mean(states, axis=-1, keepdims=True)
    spread = jnp.mean(centre * centre, axis=-1, keepdims=True)
    scale = lax.rsqrt(spread + epsilon)
    return centre * scale, scale


def norm_back(grad, unit, scale, gain):
    inner = grad * gain
    along = jnp.mean(inner * unit, axis=-1, keepdims=True)
    return scale * (inner - jnp.mean(inner, axis=-1, keepdims=True) - unit * along)


def gelu_parts(values):
    size = jnp.abs(values) * (0.5**0.5)
    t = 1.0 / (1.0 + 0.3275911 * size)
    series = t * (
        0.254829592
        + t * (-0.284496736 + t * (1.421413741 + t * (-1.453152027 + t * 1.061405429)))
    )
    decay = jnp.exp(-0.5 * values * values)
    upper = 0.5 * series * decay
    below = jnp.where(values < 0, upper, 1.0 - upper)
    return below, decay * 0.3989422804014327


def total(values):
    return jnp.sum(values, axis=0, keepdims=True)


def key_rows(ref, image, lanes, rows):
    block = ref[image * rows.top : (image + 1) * rows.top, lanes]
    if rows.rest == 0:
        return block
    start = rows.queries + image * rows.rest
    return jnp.concatenate([block, ref[start : start + rows.rest, lanes]], axis=0)


class Copies:
    def __init__(self, sems):
        self.sems = sems
        self.used = 0

    def start(self, source, target):
        copy = pltpu.make_async_copy(source, target, self.sems.at[self.used])
        self.used += 1
        copy.start()
        return copy


SAVED = ("xs", "h1", "qkv", "p", "o", "a", "x1", "h2", "gp", "gl", "y")


def saved_shapes(rows, width, hidden):
    return {
        "xs": ((rows.total, width), bf16),
        "h1": ((rows.total, width), bf16),
        "qkv": ((rows.total, 3 * width), bf16),
        "p": ((rows.images * HEADS, rows.top, rows.keys), bf16),
        "o": ((rows.queries, width), bf16),
        "a": ((rows.queries, width), bf16),
        "x1": ((rows.queries, width), f32),
        "h2": ((rows.queries, width), bf16),
        "gp": ((rows.queries, hidden), bf16),
        "gl": ((rows.queries, hidden), bf16),
        "y": ((rows.queries, width), bf16),
    }


def forward_kernel(rows, n_in, *refs):
    (where_ref, mask_ref, tok_ref, lat_ref, gains_ref, biases_ref, upb_ref, downb_ref) = refs[:8]
    w_in, w_out, w_up, w_down = refs[8:12]
    result = refs[n_in]
    saved = dict(zip(SAVED, refs[n_in + 1 : n_in + 1 + len(SAVED)]))
    scratch = refs[n_in + 1 + len(SAVED) :]
    wi, wo, wu, wd = scratch[:4]
    held = dict(zip(SAVED, scratch[4 : 4 + len(SAVED)]))
    res, sems = scratch[4 + len(SAVED) :]
    width = wo.shape[0]
    images, top, queries = rows.images, rows.top, rows.queries
    scale = HEAD_DIM**-0.5

    @pl.when(where_ref[0] == (0 if rows.first else 1))
    def _():
        copies = Copies(sems)
        get_in = copies.start(w_in.at[0], wi)
        get_out = copies.start(w_out.at[0], wo)
        get_up = copies.start(w_up.at[0], wu)
        get_down = copies.start(w_down.at[0], wd)
        puts = []

        def put(name):
            puts.append(copies.start(held[name], saved[name]))

        flag, place, count = sort_rows(mask_ref, rows)

        def states_of(b, start, length):
            chosen = pick(place, b, start, length)
            if rows.first:
                return dot(chosen.astype(bf16), tok_ref[b])
            from_tokens = (chosen * flag[b : b + 1, :]).astype(bf16)
            from_latent = (chosen * (1.0 - flag[b : b + 1, :])).astype(bf16)
            return dot(from_tokens, tok_ref[b]) + dot(from_latent, lat_ref[b])

        pieces = [states_of(b, 0, top) for b in range(images)]
        if rows.rest:
            pieces += [states_of(b, top, rows.rest) for b in range(images)]
        states = jnp.concatenate(pieces, axis=0)
        held["xs"][...] = states.astype(bf16)
        put("xs")
        unit, _ = normed(states)
        h1 = (unit * gains_ref[0, 0:1, :] + biases_ref[0, 0:1, :]).astype(bf16)
        held["h1"][...] = h1
        put("h1")
        qkv = held["qkv"]
        get_in.wait()
        qkv[0:queries, 0:width] = (dot(h1[:queries], wi[:, :width]) + biases_ref[0, 1:2, :]).astype(
            bf16
        )
        if rows.rest:
            qkv[queries:, 0:width] = jnp.zeros((rows.total - queries, width), bf16)
        qkv[:, width : 2 * width] = dot(h1, wi[:, width : 2 * width]).astype(bf16)
        qkv[:, 2 * width :] = (dot(h1, wi[:, 2 * width :]) + biases_ref[0, 2:3, :]).astype(bf16)
        put("qkv")
        lane = iota((1, LANES), 1)
        sides = [(lane < HEAD_DIM), (lane >= HEAD_DIM)]
        masks = [jnp.where(side, 1.0, 0.0).astype(bf16) for side in sides]

        @pl.loop(0, PAIRS)
        def _(pair):
            lo = pl.multiple_of(pair * LANES, LANES)
            for b in range(images):
                q = qkv[b * top : (b + 1) * top, pl.ds(lo, LANES)]
                k = key_rows(qkv, b, pl.ds(width + lo, LANES), rows)
                v = key_rows(qkv, b, pl.ds(2 * width + lo, LANES), rows)
                at = iota((1, rows.keys), 1).astype(f32)
                if rows.first:
                    usable = at < count[b : b + 1, :]
                else:
                    usable = at < float(rows.patches)
                mixed = []
                for side in range(2):
                    raw = dot_nt(q * masks[side], k)
                    logits = jnp.where(usable, raw * scale, -1e30)
                    grown = jnp.exp(logits - jnp.max(logits, axis=-1, keepdims=True))
                    p = (grown * (1.0 / jnp.sum(grown, axis=-1, keepdims=True))).astype(bf16)
                    held["p"][(b * 2 + side) * PAIRS + pair] = p
                    mixed.append(dot(p, v))
                held["o"][b * top : (b + 1) * top, pl.ds(lo, LANES)] = jnp.where(
                    sides[0], mixed[0], mixed[1]
                ).astype(bf16)

        put("p")
        put("o")
        get_out.wait()
        a = dot(held["o"][...], wo[...]) + biases_ref[0, 3:4, :]
        held["a"][...] = a.astype(bf16)
        put("a")
        usable_rows = valid_rows(count, rows)
        x1 = states[:queries] + gains_ref[0, 1:2, :] * a * usable_rows
        held["x1"][...] = x1
        put("x1")
        unit, _ = normed(x1)
        h2 = (unit * gains_ref[0, 2:3, :] + biases_ref[0, 4:5, :]).astype(bf16)
        held["h2"][...] = h2
        put("h2")
        get_up.wait()
        get_down.wait()
        y = jnp.zeros((queries, width), f32)
        for start in range(0, wu.shape[1], TILE):
            cols = slice(start, start + TILE)
            u = dot(h2, wu[:, cols]) + upb_ref[:, cols]
            below, density = gelu_parts(u)
            gl = (u * below).astype(bf16)
            held["gl"][:, cols] = gl
            held["gp"][:, cols] = (below + u * density).astype(bf16)
            y = y + dot(gl, wd[cols, :])
        put("gl")
        put("gp")
        y = y + downb_ref[...]
        held["y"][...] = y.astype(bf16)
        put("y")
        x2 = (x1 + gains_ref[0, 3:4, :] * y * usable_rows).astype(bf16)
        for b in range(images):
            chosen = (pick(place, b, 0, top) * flag[b : b + 1, :]).astype(bf16)
            res[b] = dot_tn(chosen, x2[b * top : (b + 1) * top]).astype(bf16)
        puts.append(copies.start(res, result.at[0]))
        for copy in puts:
            copy.wait()


def forward(rows, where, mask, tokens, latent, weights, before):
    w_in, w_out, w_up, w_down, gains, biases, up_bias, down_bias = weights
    width, hidden = w_up.shape[1:]
    shapes = saved_shapes(rows, width, hidden)
    operands = [where, mask, tokens, latent, gains, biases, up_bias, down_bias]
    operands += [w_in, w_out, w_up, w_down]
    in_specs = [SMEM] + [VMEM] * 7 + [ANY] * 4
    aliases = {}
    if before is not None:
        aliases[len(operands)] = 0
        operands.append(before)
        in_specs.append(ANY)
    outs = [jax.ShapeDtypeStruct((1,) + tokens.shape, bf16)]
    outs += [jax.ShapeDtypeStruct(*shapes[name]) for name in SAVED]
    results = pl.pallas_call(
        functools.partial(forward_kernel, rows, len(operands)),
        out_shape=outs,
        in_specs=in_specs,
        out_specs=[ANY] * len(outs),
        scratch_shapes=[pltpu.VMEM(w.shape[1:], bf16) for w in (w_in, w_out, w_up, w_down)]
        + [pltpu.VMEM(*shapes[name]) for name in SAVED]
        + [pltpu.VMEM(tokens.shape, bf16), pltpu.SemaphoreType.DMA((20,))],
        input_output_aliases=aliases,
        compiler_params=pltpu.CompilerParams(vmem_limit_bytes=52 * MIB),
        cost_estimate=pl.CostEstimate(
            flops=2 * rows.queries * 12 * width * width,
            bytes_accessed=12 * 2 * width * width,
            transcendentals=0,
        ),
        name="forward_first" if rows.first else "forward_second",
    )(*operands)
    return results[0], dict(zip(SAVED, results[1:]))


def split_store(bit, keep, send, tile, shards, base, order):
    height = tile.shape[0] // shards
    for own in range(2):

        @pl.when(bit == own)
        def _():
            for d in range(shards):
                x, y, z = d & 1, (d >> 1) & 1, d >> 2
                mine, slot = (x, 2 * z + y) if order == 0 else (y, 2 * z + x)
                target = keep if mine == own else send
                target[slot - base] = tile[d * height : (d + 1) * height]


def bit_of(where_ref, order):
    return (where_ref[1] >> order) & 1


def down_kernel(rows, order, *refs):
    where_ref, mask_ref, cot_ref, ret_ref, gains_ref, y_ref, gl_ref = refs[:7]
    outs = refs[7:-1]
    if order is None:
        plain, g_out, dy_out, vec = outs
    else:
        keep, send, g_out, dy_out, vec = outs
    turned = refs[-1]
    images, top = rows.images, rows.top

    @pl.when(where_ref[0] == (0 if rows.first else 1))
    def _():
        @pl.when(pl.program_id(0) == 0)
        def _():
            flag, place, count = sort_rows(mask_ref, rows)
            pieces = []
            for b in range(images):
                chosen = (pick(place, b, 0, top) * flag[b : b + 1, :]).astype(bf16)
                piece = dot(chosen, cot_ref[0, b])
                if rows.first:
                    piece = piece + dot(chosen, ret_ref[b])
                pieces.append(piece)
            grad = jnp.concatenate(pieces, axis=0)
            g_out[...] = grad
            dy = (grad * gains_ref[0, 3:4, :] * valid_rows(count, rows)).astype(bf16)
            dy_out[...] = dy
            vec[...] = jnp.zeros(vec.shape, f32)
            vec[0:1, :] = total(grad * y_ref[...].astype(f32))
            vec[1:2, :] = total(dy.astype(f32))
            turned[...] = dy.T

        tile = dot(turned[...], gl_ref[...]).astype(bf16)
        if order is None:
            plain[...] = tile
        else:
            split_store(bit_of(where_ref, order), keep, send, tile, 16, 0, order)


def grad_outs(order, shards, full, block, index):
    if order is None:
        return [jax.ShapeDtypeStruct(full, bf16)], [pl.BlockSpec(block, index)]
    return [jax.ShapeDtypeStruct(shards, bf16)] * 2, None


def whole(shape):
    return pl.BlockSpec(shape, lambda *_: (0,) * len(shape))


def down_back(rows, order, where, mask, cot, returned, gains, saved):
    queries, width = saved["y"].shape
    hidden = saved["gl"].shape[1]
    if order is None:
        grads = [jax.ShapeDtypeStruct((width, hidden), bf16)]
        specs = [pl.BlockSpec((width, TILE), lambda t: (0, t))]
    else:
        grads = [jax.ShapeDtypeStruct((8, width // 16, hidden), bf16)] * 2
        specs = [pl.BlockSpec((8, width // 16, TILE), lambda t: (0, 0, t))] * 2
    vectors = [
        jax.ShapeDtypeStruct((queries, width), f32),
        jax.ShapeDtypeStruct((queries, width), bf16),
        jax.ShapeDtypeStruct((8, width), f32),
    ]
    return pl.pallas_call(
        functools.partial(down_kernel, rows, order),
        grid=(hidden // TILE,),
        out_shape=grads + vectors,
        in_specs=[SMEM]
        + [whole(a.shape) for a in (mask, cot, returned, gains, saved["y"])]
        + [pl.BlockSpec((queries, TILE), lambda t: (0, t))],
        out_specs=specs + [whole(v.shape) for v in vectors],
        scratch_shapes=[pltpu.VMEM((width, queries), bf16)],
        compiler_params=pltpu.CompilerParams(vmem_limit_bytes=40 * MIB),
        cost_estimate=pl.CostEstimate(
            flops=2 * queries * hidden * width, bytes_accessed=4 * hidden * width, transcendentals=0
        ),
        name="down_grad",
    )(where, mask, cot, returned, gains, saved["y"], saved["gl"])


def up_kernel(rows, order, *refs):
    where_ref, dy_ref, gp_ref, h2_ref, down_ref, up_ref = refs[:6]
    if order is None:
        plain, upb_out, dh2_out = refs[6:]
    else:
        keep, send, upb_out, dh2_out = refs[6:]
    step = pl.program_id(0)

    @pl.when(where_ref[0] == (0 if rows.first else 1))
    def _():
        dgl = dot_nt(dy_ref[...], down_ref[0])
        du = (dgl * gp_ref[...].astype(f32)).astype(bf16)
        upb_out[...] = total(du.astype(f32))
        tile = dot_tn(du, h2_ref[...]).astype(bf16)
        if order is None:
            plain[...] = tile
        else:
            split_store(bit_of(where_ref, order), keep, send, tile, 4, 0, order)
        part = dot_nt(du, up_ref[0])

        @pl.when(step == 0)
        def _():
            dh2_out[...] = part

        @pl.when(step > 0)
        def _():
            dh2_out[...] += part


def up_back(rows, order, where, dy, saved, w_down, w_up):
    queries, width = dy.shape
    hidden = w_up.shape[2]
    if order is None:
        grads = [jax.ShapeDtypeStruct((hidden, width), bf16)]
        specs = [pl.BlockSpec((TILE, width), lambda t: (t, 0))]
    else:
        grads = [jax.ShapeDtypeStruct((8, hidden // 16, width), bf16)] * 2
        specs = [pl.BlockSpec((2, hidden // 16, width), lambda t: (t, 0, 0))] * 2
    vectors = [
        jax.ShapeDtypeStruct((1, hidden), f32),
        jax.ShapeDtypeStruct((queries, width), f32),
    ]
    return pl.pallas_call(
        functools.partial(up_kernel, rows, order),
        grid=(hidden // TILE,),
        out_shape=grads + vectors,
        in_specs=[
            SMEM,
            whole(dy.shape),
            pl.BlockSpec((queries, TILE), lambda t: (0, t)),
            whole(dy.shape),
            pl.BlockSpec((1, TILE, width), lambda t: (0, t, 0)),
            pl.BlockSpec((1, width, TILE), lambda t: (0, 0, t)),
        ],
        out_specs=specs + [pl.BlockSpec((1, TILE), lambda t: (0, t)), whole((queries, width))],
        compiler_params=pltpu.CompilerParams(vmem_limit_bytes=40 * MIB),
        cost_estimate=pl.CostEstimate(
            flops=6 * queries * hidden * width, bytes_accessed=6 * hidden * width, transcendentals=0
        ),
        name="up_grad",
    )(where, dy, saved["gp"], saved["h2"], w_down, w_up)


ATTEND = ("dh2", "x1", "g", "a", "o", "w_out", "qkv", "p", "w_in", "xs")


def attend_kernel(rows, order, n_in, n_out, *refs):
    where_ref, mask_ref, gains_ref, biases_ref, vec_ref, upb_ref = refs[:6]
    source = dict(zip(ATTEND, refs[6:16]))
    outs = refs[n_in : n_in + n_out]
    dqkv_out, token_out, ret_out, vec_out = outs[-4:]
    scratch = refs[n_in + n_out :]
    held = dict(zip(ATTEND, scratch[: len(ATTEND)]))
    dqkv, tok_buf, ret_buf, vec_buf = scratch[len(ATTEND) : len(ATTEND) + 4]
    halves = scratch[len(ATTEND) + 4 : -1]
    sems = scratch[-1]
    images, top, queries = rows.images, rows.top, rows.queries
    width = held["w_out"].shape[0]
    scale = HEAD_DIM**-0.5

    @pl.when(where_ref[0] == (0 if rows.first else 1))
    def _():
        copies = Copies(sems)
        gets = {}
        for name in ATTEND:
            ref = source[name]
            gets[name] = copies.start(ref.at[0] if name in ("w_in", "w_out") else ref, held[name])
        puts = []
        flag, place, count = sort_rows(mask_ref, rows)
        usable_rows = valid_rows(count, rows)
        for name in ("dh2", "x1", "g"):
            gets[name].wait()
        unit, spread = normed(held["x1"][...])
        dh2 = held["dh2"][...]
        gain_two = total(dh2 * unit)
        bias_two = total(dh2)
        dx1 = held["g"][...] + norm_back(dh2, unit, spread, gains_ref[0, 2:3, :])
        da = (dx1 * gains_ref[0, 1:2, :] * usable_rows).astype(bf16)
        for name in ("a", "o", "w_out"):
            gets[name].wait()
        scale_one = total(dx1 * held["a"][...].astype(f32) * usable_rows)
        out_bias = total(da.astype(f32))
        tile = dot_tn(da, held["o"][...]).astype(bf16)
        if order is None:
            halves[0][...] = tile
        else:
            split_store(bit_of(where_ref, order), halves[0], halves[1], tile, 16, 0, order)
        for half, out in zip(halves, outs):
            puts.append(copies.start(half, out))
        do_ref = held["o"]
        do_ref[...] = dot_nt(da, held["w_out"][...]).astype(bf16)
        for name in ("qkv", "p"):
            gets[name].wait()
        qkv = held["qkv"]
        lane = iota((1, LANES), 1)
        sides = [(lane < HEAD_DIM), (lane >= HEAD_DIM)]
        masks = [jnp.where(side, 1.0, 0.0).astype(bf16) for side in sides]
        if rows.rest:
            dqkv[queries:, 0:width] = jnp.zeros((rows.total - queries, width), bf16)

        @pl.loop(0, PAIRS)
        def _(pair):
            lo = pl.multiple_of(pair * LANES, LANES)
            for b in range(images):
                q = qkv[b * top : (b + 1) * top, pl.ds(lo, LANES)]
                k = key_rows(qkv, b, pl.ds(width + lo, LANES), rows)
                v = key_rows(qkv, b, pl.ds(2 * width + lo, LANES), rows)
                do = do_ref[b * top : (b + 1) * top, pl.ds(lo, LANES)]
                parts = []
                for side in range(2):
                    p = held["p"][(b * 2 + side) * PAIRS + pair]
                    wide = p.astype(f32)
                    dp = dot_nt(do * masks[side], v)
                    inner = jnp.sum(wide * dp, axis=-1, keepdims=True)
                    draw = (wide * (dp - inner) * scale).astype(bf16)
                    parts.append((dot(draw, k), dot_tn(draw, q), dot_tn(p, do)))
                for at in range(3):
                    merged = jnp.where(sides[0], parts[0][at], parts[1][at]).astype(bf16)
                    lanes = pl.ds(at * width + lo, LANES)
                    dqkv[b * top : (b + 1) * top, lanes] = merged[:top]
                    if rows.rest and at > 0:
                        start = queries + b * rows.rest
                        dqkv[start : start + rows.rest, lanes] = merged[top:]

        puts.append(copies.start(dqkv, dqkv_out))
        gets["w_in"].wait()
        gets["xs"].wait()
        dh1 = jnp.zeros((rows.total, width), f32)
        for at in range(3):
            cols = slice(at * width, (at + 1) * width)
            dh1 = dh1 + dot_nt(dqkv[:, cols], held["w_in"][:, cols])
        unit, spread = normed(held["xs"][...].astype(f32))
        dx = norm_back(dh1, unit, spread, gains_ref[0, 0:1, :])
        if rows.rest:
            rest = dx[queries:]
        dx = dx[:queries] + dx1
        high = dx.astype(bf16)
        low = (dx - high.astype(f32)).astype(bf16)
        for b in range(images):
            chosen = pick(place, b, 0, top)
            mine = (chosen * flag[b : b + 1, :]).astype(bf16)
            part = slice(b * top, (b + 1) * top)
            tok_buf[b] = dot_tn(mine, high[part]) + dot_tn(mine, low[part])
            if not rows.first:
                other = (chosen * (1.0 - flag[b : b + 1, :])).astype(bf16)
                back = dot_tn(other, high[part])
                tail = pick(place, b, top, rows.rest).astype(bf16)
                part = slice(b * rows.rest, (b + 1) * rows.rest)
                back = back + dot_tn(tail, rest[part].astype(bf16))
                ret_buf[b] = back.astype(bf16)
        puts.append(copies.start(tok_buf, token_out.at[0]))
        if not rows.first:
            puts.append(copies.start(ret_buf, ret_out))
        vec_buf[...] = jnp.zeros(vec_buf.shape, f32)
        vec_buf[0:1, :] = total(dh1 * unit)
        vec_buf[1:2, :] = scale_one
        vec_buf[2:3, :] = gain_two
        vec_buf[3:4, :] = vec_ref[0:1, :]
        vec_buf[4:5, :] = total(dh1)
        vec_buf[5:6, :] = total(dqkv[:, 0:width].astype(f32))
        vec_buf[6:7, :] = total(dqkv[:, 2 * width :].astype(f32))
        vec_buf[7:8, :] = out_bias
        vec_buf[8:9, :] = bias_two
        vec_buf[9:10, :] = vec_ref[1:2, :]
        for at in range(upb_ref.shape[1] // width):
            vec_buf[10 + at : 11 + at, :] = upb_ref[:, at * width : (at + 1) * width]
        puts.append(copies.start(vec_buf, vec_out))
        for copy in puts:
            copy.wait()


def attend_back(rows, order, where, mask, weights, vec, upb, dh2, grad, saved, token_before):
    w_in, w_out, _, _, gains, biases, _, _ = weights
    queries, width = dh2.shape
    shape = (rows.images, rows.patches, width)
    values = dict(saved, dh2=dh2, g=grad, w_in=w_in, w_out=w_out)
    operands = [where, mask, gains, biases, vec, upb] + [values[name] for name in ATTEND]
    in_specs = [SMEM] + [VMEM] * 5 + [ANY] * len(ATTEND)
    if order is None:
        grads = [jax.ShapeDtypeStruct((width, width), bf16)]
    else:
        grads = [jax.ShapeDtypeStruct((8, width // 16, width), bf16)] * 2
    outs = grads + [
        jax.ShapeDtypeStruct((rows.total, 3 * width), bf16),
        jax.ShapeDtypeStruct((1,) + shape, f32),
        jax.ShapeDtypeStruct(shape, bf16),
        jax.ShapeDtypeStruct((16, width), f32),
    ]
    aliases = {}
    if token_before is not None:
        aliases[len(operands)] = len(grads) + 1
        operands.append(token_before)
        in_specs.append(ANY)
    held = [
        pltpu.VMEM(values[n].shape[1:] if n in ("w_in", "w_out") else values[n].shape, values[n].dtype)
        for n in ATTEND
    ]
    return pl.pallas_call(
        functools.partial(attend_kernel, rows, order, len(operands), len(outs)),
        out_shape=outs,
        in_specs=in_specs,
        out_specs=[ANY] * len(outs),
        scratch_shapes=held
        + [
            pltpu.VMEM((rows.total, 3 * width), bf16),
            pltpu.VMEM(shape, f32),
            pltpu.VMEM(shape, bf16),
            pltpu.VMEM((16, width), f32),
        ]
        + [pltpu.VMEM(g.shape, g.dtype) for g in grads]
        + [pltpu.SemaphoreType.DMA((20,))],
        input_output_aliases=aliases,
        compiler_params=pltpu.CompilerParams(vmem_limit_bytes=52 * MIB),
        cost_estimate=pl.CostEstimate(
            flops=2 * rows.total * 6 * width * width,
            bytes_accessed=16 * width * width,
            transcendentals=0,
        ),
        name="attend_back",
    )(*operands)


def in_kernel(rows, order, where_ref, dqkv_ref, h1_ref, *outs):
    @pl.when(where_ref[0] == (0 if rows.first else 1))
    def _():
        tile = dot_tn(dqkv_ref[...], h1_ref[...]).astype(bf16)
        if order is None:
            outs[0][...] = tile
        else:
            split_store(bit_of(where_ref, order), outs[0], outs[1], tile, 8, 0, order)


def in_back(rows, order, where, dqkv, h1):
    tall, wide = dqkv.shape
    width = h1.shape[1]
    half = wide // 2
    if order is None:
        grads = [jax.ShapeDtypeStruct((wide, width), bf16)]
        specs = [pl.BlockSpec((half, width), lambda t: (t, 0))]
    else:
        grads = [jax.ShapeDtypeStruct((8, wide // 16, width), bf16)] * 2
        specs = [pl.BlockSpec((4, wide // 16, width), lambda t: (t, 0, 0))] * 2
    return pl.pallas_call(
        functools.partial(in_kernel, rows, order),
        grid=(2,),
        out_shape=grads,
        in_specs=[SMEM, pl.BlockSpec((tall, half), lambda t: (0, t)), whole(h1.shape)],
        out_specs=specs,
        compiler_params=pltpu.CompilerParams(vmem_limit_bytes=40 * MIB),
        cost_estimate=pl.CostEstimate(
            flops=2 * tall * wide * width, bytes_accessed=4 * wide * width, transcendentals=0
        ),
        name="in_grad",
    )(where, dqkv, h1)


def wide_sum(*terms):
    result = terms[0].astype(f32)
    for term in terms[1:]:
        result = result + term.astype(f32)
    return result


def swap(value, by, count):
    return lax.ppermute(value, "dp", [(i, i ^ by) for i in range(count)])


def line_sum(parts, z, stride, count):
    length = parts.shape[0]
    right = left = None

    def part(at):
        return lax.dynamic_index_in_dim(parts, jnp.clip(at, 0, length - 1), 0, keepdims=False)

    for t in range(length - 1):
        ahead = length - 1 - t
        to_right, to_left = part(z + ahead), part(z - ahead)
        if t > 0:
            to_right = wide_sum(to_right, right).astype(bf16)
            to_left = wide_sum(to_left, left).astype(bf16)
        pairs = [
            (i, i + stride)
            for i in range(count)
            if i // stride % length <= t and i // stride % length < length - 1
        ]
        back = [(count - 1 - i, count - 1 - j) for i, j in pairs]
        right = lax.ppermute(to_right, "dp", pairs)
        left = lax.ppermute(to_left, "dp", back)
    return wide_sum(part(z), right, left)


def half_of(parts, bit, axis):
    keep = lax.dynamic_index_in_dim(parts, bit, axis, keepdims=False)
    send = lax.dynamic_index_in_dim(parts, 1 - bit, axis, keepdims=False)
    return keep, send


def on_device(
    tokens,
    patch_mask,
    cotangent,
    in_weight,
    out_weight,
    up_weight,
    down_weight,
    gains,
    biases,
    up_bias,
    down_bias,
):
    weights = (in_weight, out_weight, up_weight, down_weight, gains, biases, up_bias, down_bias)
    images, patches, width = tokens.shape
    hidden = up_weight.shape[2]
    count = lax.axis_size("dp")
    section = lax.axis_index("section")
    place = lax.axis_index("dp")
    is_first = section == 0
    where = jnp.stack([section, place]).astype(jnp.int32)
    small = count == 16
    orders = {"down": 0, "up": 1, "out": 0, "in": 1} if small else dict.fromkeys(
        ("down", "up", "out", "in")
    )
    rows = [Rows(True, images, patches), Rows(False, images, patches)]

    result, kept_first = forward(rows[0], where, patch_mask, tokens, tokens, weights, None)
    latent = lax.ppermute(result[0], "section", [(0, 1)])
    result, kept_second = forward(rows[1], where, patch_mask, tokens, latent, weights, result)
    kept = [kept_first, kept_second]

    grads = [None, None]
    vectors = [None, None]
    returned = latent
    token_grads = None
    for phase in (1, 0):
        layout, saved = rows[phase], kept[phase]
        pairs = [(phase * count + i, phase * count + (i ^ 1)) for i in range(count)]
        cross = [(phase * count + i, phase * count + (i ^ 2)) for i in range(count)]

        def first_exchange(halves, order):
            if order is None:
                return halves
            keep, send = halves
            got = lax.ppermute(send, ("section", "dp"), cross if order else pairs)
            return [keep, got]

        *halves, grad, dy, vec = down_back(
            layout, orders["down"], where, patch_mask, cotangent, returned, gains, saved
        )
        mine = {"down": first_exchange(halves, orders["down"])}
        *halves, upb, dh2 = up_back(
            layout, orders["up"], where, dy, saved, down_weight, up_weight
        )
        mine["up"] = first_exchange(halves, orders["up"])
        *halves, dqkv, token_grads, back, vec = attend_back(
            layout, orders["out"], where, patch_mask, weights, vec, upb, dh2, grad, saved, token_grads
        )
        if phase == 1:
            returned = lax.ppermute(back, "section", [(1, 0)])
        mine["out"] = first_exchange(halves, orders["out"])
        halves = in_back(layout, orders["in"], where, dqkv, saved["h1"])
        mine["in"] = first_exchange(halves, orders["in"])
        grads[phase] = mine
        vectors[phase] = vec

    vec = jnp.where(is_first, vectors[0], vectors[1])
    finals = {}
    if small:
        x, y, z = place & 1, (place >> 1) & 1, place >> 2
        for name in ("down", "up", "out", "in"):
            merged = jnp.where(
                is_first, wide_sum(*grads[0][name]), wide_sum(*grads[1][name])
            ).astype(bf16)
            first = orders[name]
            second_bit, step = (y, 2) if first == 0 else (x, 1)
            shape = merged.shape[1:]
            merged = merged.reshape((4, 2) + shape)
            if name in ("down", "up"):
                part = line_sum(merged, z, 4, count).astype(bf16)
                keep, send = half_of(part, second_bit, 0)
                finals[name] = wide_sum(keep, swap(send, step, count))
            else:
                keep, send = half_of(merged, second_bit, 1)
                part = wide_sum(keep, swap(send, step, count)).astype(bf16)
                finals[name] = line_sum(part, z, 4, count)
        for by in (1, 2, 4, 8):
            vec = vec + swap(vec, by, count)
    else:
        for name in ("down", "up", "out", "in"):
            merged = jnp.where(is_first, grads[0][name][0], grads[1][name][0])
            finals[name] = lax.psum_scatter(
                merged.astype(f32), "dp", scatter_dimension=0, tiled=True
            )
        vec = lax.psum(vec, "dp")

    def columns(values):
        size = values.shape[-1] // count
        return lax.dynamic_slice_in_dim(values, place * size, size, values.ndim - 1)

    return (
        result,
        token_grads,
        finals["in"].T[None],
        finals["out"].T[None],
        finals["up"].T[None],
        finals["down"].T[None],
        columns(vec[0:4])[None],
        columns(vec[4:9])[None],
        columns(vec[10:14].reshape(1, hidden)),
        columns(vec[9:10]),
    )


def solution(mesh):
    return jax.shard_map(
        on_device,
        mesh=mesh,
        in_specs=(
            P("dp", None, None),
            P("dp", None),
            P("section", "dp", None, None),
            P("section", None, None),
            P("section", None, None),
            P("section", None, None),
            P("section", None, None),
            P("section", None, None),
            P("section", None, None),
            P("section", None),
            P("section", None),
        ),
        out_specs=(
            P("section", "dp", None, None),
            P("section", "dp", None, None),
            P("section", None, "dp"),
            P("section", None, "dp"),
            P("section", None, "dp"),
            P("section", None, "dp"),
            P("section", None, "dp"),
            P("section", None, "dp"),
            P("section", "dp"),
            P("section", "dp"),
        ),
        check_vma=False,
    )
```

```python
import functools

import jax
import jax.numpy as jnp
from jax import lax
from jax.experimental import pallas as pl
from jax.experimental.pallas import tpu as pltpu
from jax.sharding import PartitionSpec as P

HEADS = 12
HEAD_DIM = 64
PAIRS = HEADS // 2
LANES = 2 * HEAD_DIM
MASK_LO = 59
MASK_HI = 117
TILE = 768
MIB = 2**20

epsilon = 1e-06
f32 = jnp.float32
bf16 = jnp.bfloat16
ANY = pl.BlockSpec(memory_space=pl.ANY)
SMEM = pl.BlockSpec(memory_space=pltpu.SMEM)
VMEM = pl.BlockSpec(memory_space=pltpu.VMEM)
COST = pl.CostEstimate(flops=1000, bytes_accessed=1000, transcendentals=0)


def up16(count):
    return -(-count // 16) * 16


class Rows:
    def __init__(self, first, images, patches):
        most = patches - MASK_LO if first else MASK_HI
        self.first = first
        self.images = images
        self.patches = patches
        self.top = up16(most)
        self.rest = 0 if first else up16(patches - self.top)
        self.keys = self.top + self.rest
        self.queries = images * self.top
        self.total = images * self.keys


def dot(left, right):
    return jnp.dot(left, right, preferred_element_type=f32)


def dot_nt(left, right):
    return lax.dot_general(left, right, (((1,), (1,)), ((), ())), preferred_element_type=f32)


def dot_tn(left, right):
    return lax.dot_general(left, right, (((0,), (0,)), ((), ())), preferred_element_type=f32)


def iota(shape, dim):
    return lax.broadcasted_iota(jnp.int32, shape, dim)


def sort_rows(mask_ref, rows):
    masked = mask_ref[...].astype(f32)
    flag = 1.0 - masked if rows.first else masked
    n = rows.patches
    tri = jnp.where(iota((n, n), 0) <= iota((n, n), 1), 1.0, 0.0).astype(bf16)
    upto = dot(flag.astype(bf16), tri)
    count = jnp.sum(flag, axis=1, keepdims=True)
    at = iota(flag.shape, 1).astype(f32)
    place = jnp.where(flag > 0, upto - 1.0, count + at - upto)
    return flag, place, count


def pick(place, image, start, length):
    slots = iota((length, place.shape[1]), 0).astype(f32) + float(start)
    return jnp.where(slots == place[image : image + 1, :], 1.0, 0.0)


def valid_rows(count, rows):
    parts = [
        jnp.where(iota((rows.top, 1), 0).astype(f32) < count[b : b + 1, :], 1.0, 0.0)
        for b in range(rows.images)
    ]
    return jnp.concatenate(parts, axis=0)


def normed(states):
    centre = states - jnp.mean(states, axis=-1, keepdims=True)
    spread = jnp.mean(centre * centre, axis=-1, keepdims=True)
    scale = lax.rsqrt(spread + epsilon)
    return centre * scale, scale


def norm_back(grad, unit, scale, gain):
    inner = grad * gain
    along = jnp.mean(inner * unit, axis=-1, keepdims=True)
    return scale * (inner - jnp.mean(inner, axis=-1, keepdims=True) - unit * along)


def gelu_parts(values):
    size = jnp.abs(values) * (0.5**0.5)
    t = 1.0 / (1.0 + 0.3275911 * size)
    series = t * (
        0.254829592
        + t * (-0.284496736 + t * (1.421413741 + t * (-1.453152027 + t * 1.061405429)))
    )
    decay = jnp.exp(-0.5 * values * values)
    upper = 0.5 * series * decay
    below = jnp.where(values < 0, upper, 1.0 - upper)
    return below, decay * 0.3989422804014327


def total(values):
    return jnp.sum(values, axis=0, keepdims=True)


def key_rows(ref, image, lanes, rows):
    block = ref[image * rows.top : (image + 1) * rows.top, lanes]
    if rows.rest == 0:
        return block
    start = rows.queries + image * rows.rest
    return jnp.concatenate([block, ref[start : start + rows.rest, lanes]], axis=0)


class Copies:
    def __init__(self, sems):
        self.sems = sems
        self.used = 0

    def start(self, source, target):
        copy = pltpu.make_async_copy(source, target, self.sems.at[self.used])
        self.used += 1
        copy.start()
        return copy


SAVED = ("xs", "h1", "qkv", "p", "o", "a", "x1", "h2", "gp", "gl", "y")


def saved_shapes(rows, width, hidden):
    return {
        "xs": ((rows.total, width), bf16),
        "h1": ((rows.total, width), bf16),
        "qkv": ((rows.total, 3 * width), bf16),
        "p": ((rows.images * HEADS, rows.top, rows.keys), bf16),
        "o": ((rows.queries, width), bf16),
        "a": ((rows.queries, width), bf16),
        "x1": ((rows.queries, width), f32),
        "h2": ((rows.queries, width), bf16),
        "gp": ((rows.queries, hidden), bf16),
        "gl": ((rows.queries, hidden), bf16),
        "y": ((rows.queries, width), bf16),
    }


def forward_kernel(rows, n_in, *refs):
    where_ref, mask_ref, tok_ref, lat_ref, gains_ref, biases_ref, upb_ref, downb_ref = refs[:8]
    w_in, w_out, w_up, w_down = refs[8:12]
    result, x2_out = refs[n_in : n_in + 2]
    saved = dict(zip(SAVED, refs[n_in + 2 : n_in + 2 + len(SAVED)]))
    scratch = refs[n_in + 2 + len(SAVED) :]
    images, top, queries = rows.images, rows.top, rows.queries
    width = w_out.shape[1]
    scale = HEAD_DIM**-0.5

    @pl.when(where_ref[0] == (0 if rows.first else 1))
    def _():
        if rows.first:
            copies = Copies(scratch[-1])
            wi, wo, wu, wd = scratch[:4]
            get_in = copies.start(w_in.at[0], wi)
            get_out = copies.start(w_out.at[0], wo)
            get_up = copies.start(w_up.at[0], wu)
            get_down = copies.start(w_down.at[0], wd)
        else:
            wi, wo, wu, wd = (ref.at[0] for ref in (w_in, w_out, w_up, w_down))
        flag, place, count = sort_rows(mask_ref, rows)

        def states_of(b, start, length):
            chosen = pick(place, b, start, length)
            if rows.first:
                return dot(chosen.astype(bf16), tok_ref[b])
            from_tokens = dot((chosen * flag[b : b + 1, :]).astype(bf16), tok_ref[b])
            shift = iota((length, lat_ref.shape[0] // images), 0) - iota(
                (length, lat_ref.shape[0] // images), 1
            )
            behind = shift.astype(f32) + float(start) == count[b : b + 1, :]
            seen = iota(behind.shape, 1).astype(f32) < rows.patches - count[b : b + 1, :]
            mover = jnp.where(behind & seen, 1.0, 0.0).astype(bf16)
            height = lat_ref.shape[0] // images
            return from_tokens + dot(mover, lat_ref[b * height : (b + 1) * height])

        pieces = [states_of(b, 0, top) for b in range(images)]
        if rows.rest:
            pieces += [states_of(b, top, rows.rest) for b in range(images)]
        states = jnp.concatenate(pieces, axis=0)
        saved["xs"][...] = states.astype(bf16)
        unit, _ = normed(states)
        h1 = (unit * gains_ref[0, 0:1, :] + biases_ref[0, 0:1, :]).astype(bf16)
        saved["h1"][...] = h1
        qkv = saved["qkv"]
        if rows.first:
            get_in.wait()
        qkv[0:queries, 0:width] = (dot(h1[:queries], wi[:, :width]) + biases_ref[0, 1:2, :]).astype(
            bf16
        )
        if rows.rest:
            qkv[queries:, 0:width] = jnp.zeros((rows.total - queries, width), bf16)
        qkv[:, width : 2 * width] = dot(h1, wi[:, width : 2 * width]).astype(bf16)
        qkv[:, 2 * width :] = (dot(h1, wi[:, 2 * width :]) + biases_ref[0, 2:3, :]).astype(bf16)
        lane = iota((1, LANES), 1)
        sides = [(lane < HEAD_DIM), (lane >= HEAD_DIM)]
        masks = [jnp.where(side, 1.0, 0.0).astype(bf16) for side in sides]

        @pl.loop(0, PAIRS)
        def _(pair):
            lo = pl.multiple_of(pair * LANES, LANES)
            for b in range(images):
                q = qkv[b * top : (b + 1) * top, pl.ds(lo, LANES)]
                k = key_rows(qkv, b, pl.ds(width + lo, LANES), rows)
                v = key_rows(qkv, b, pl.ds(2 * width + lo, LANES), rows)
                at = iota((1, rows.keys), 1).astype(f32)
                if rows.first:
                    usable = at < count[b : b + 1, :]
                else:
                    usable = at < float(rows.patches)
                mixed = []
                for side in range(2):
                    raw = dot_nt(q * masks[side], k)
                    logits = jnp.where(usable, raw * scale, -1e30)
                    grown = jnp.exp(logits - jnp.max(logits, axis=-1, keepdims=True))
                    p = (grown * (1.0 / jnp.sum(grown, axis=-1, keepdims=True))).astype(bf16)
                    saved["p"][(b * 2 + side) * PAIRS + pair] = p
                    mixed.append(dot(p, v))
                saved["o"][b * top : (b + 1) * top, pl.ds(lo, LANES)] = jnp.where(
                    sides[0], mixed[0], mixed[1]
                ).astype(bf16)

        if rows.first:
            get_out.wait()
        a = dot(saved["o"][...], wo[...]) + biases_ref[0, 3:4, :]
        saved["a"][...] = a.astype(bf16)
        usable_rows = valid_rows(count, rows)
        x1 = states[:queries] + gains_ref[0, 1:2, :] * a * usable_rows
        saved["x1"][...] = x1
        unit, _ = normed(x1)
        h2 = (unit * gains_ref[0, 2:3, :] + biases_ref[0, 4:5, :]).astype(bf16)
        saved["h2"][...] = h2
        if rows.first:
            get_up.wait()
            get_down.wait()
        y = jnp.zeros((queries, width), f32)
        for start in range(0, wu.shape[1], TILE):
            cols = slice(start, start + TILE)
            u = dot(h2, wu[:, cols]) + upb_ref[:, cols]
            below, density = gelu_parts(u)
            gl = (u * below).astype(bf16)
            saved["gl"][:, cols] = gl
            saved["gp"][:, cols] = (below + u * density).astype(bf16)
            y = y + dot(gl, wd[cols, :])
        y = y + downb_ref[...]
        saved["y"][...] = y.astype(bf16)
        x2 = (x1 + gains_ref[0, 3:4, :] * y * usable_rows).astype(bf16)
        x2_out[...] = x2
        for b in range(images):
            chosen = (pick(place, b, 0, top) * flag[b : b + 1, :]).astype(bf16)
            result[0, b] = dot_tn(chosen, x2[b * top : (b + 1) * top]).astype(bf16)


def forward(rows, where, mask, tokens, latent, weights, before):
    w_in, w_out, w_up, w_down, gains, biases, up_bias, down_bias = weights
    width, hidden = w_up.shape[1:]
    shapes = saved_shapes(rows, width, hidden)
    operands = [where, mask, tokens, latent, gains, biases, up_bias, down_bias]
    operands += [w_in, w_out, w_up, w_down]
    in_specs = [SMEM] + [VMEM] * 7 + [ANY if rows.first else VMEM] * 4
    aliases = {}
    if before is not None:
        aliases[len(operands)] = 0
        operands.append(before)
        in_specs.append(VMEM)
    outs = [
        jax.ShapeDtypeStruct((1,) + tokens.shape, bf16),
        jax.ShapeDtypeStruct((rows.queries, width), bf16),
    ]
    outs += [jax.ShapeDtypeStruct(*shapes[name]) for name in SAVED]
    scratch = []
    if rows.first:
        scratch = [pltpu.VMEM(w.shape[1:], bf16) for w in (w_in, w_out, w_up, w_down)]
        scratch.append(pltpu.SemaphoreType.DMA((4,)))
    results = pl.pallas_call(
        functools.partial(forward_kernel, rows, len(operands)),
        out_shape=outs,
        in_specs=in_specs,
        out_specs=[VMEM] * len(outs),
        scratch_shapes=scratch,
        input_output_aliases=aliases,
        compiler_params=pltpu.CompilerParams(vmem_limit_bytes=(28 if rows.first else 14) * MIB),
        cost_estimate=COST,
        name="forward_first" if rows.first else "forward_second",
    )(*operands)
    return results[0], results[1], dict(zip(SAVED, results[2:]))


def bit_of(where_ref, order):
    return (where_ref[1] >> order) & 1


def active(where_ref, rows):
    return where_ref[0] == (0 if rows.first else 1)


def plain_call(kernel, operands, in_specs, outs, name, scratch=(), aliases=None, limit=14):
    return pl.pallas_call(
        kernel,
        out_shape=outs,
        in_specs=in_specs,
        out_specs=[VMEM] * len(outs),
        scratch_shapes=list(scratch),
        input_output_aliases=aliases or {},
        compiler_params=pltpu.CompilerParams(vmem_limit_bytes=limit * MIB),
        cost_estimate=COST,
        name=name,
    )(*operands)


def start_kernel(rows, where_ref, mask_ref, cot_ref, ret_ref, gains_ref, y_ref, gl_ref, *outs):
    g_out, dy_out, vec, send = outs
    top = rows.top
    half = gl_ref.shape[1] // 2

    @pl.when(active(where_ref, rows))
    def _():
        flag, place, count = sort_rows(mask_ref, rows)
        pieces = []
        for b in range(rows.images):
            chosen = (pick(place, b, 0, top) * flag[b : b + 1, :]).astype(bf16)
            piece = dot(chosen, cot_ref[0, b])
            if rows.first:
                piece = piece + ret_ref[b * top : (b + 1) * top].astype(f32)
            pieces.append(piece)
        grad = jnp.concatenate(pieces, axis=0)
        g_out[...] = grad
        dy = (grad * gains_ref[0, 3:4, :] * valid_rows(count, rows)).astype(bf16)
        dy_out[...] = dy
        vec[...] = jnp.zeros(vec.shape, f32)
        vec[0:1, :] = total(grad * y_ref[...].astype(f32))
        vec[1:2, :] = total(dy.astype(f32))
        other = pl.multiple_of((1 - bit_of(where_ref, 0)) * half, half)
        send[:, :half] = gl_ref[:, pl.ds(other, half)]
        send[:, half:] = dy


def start_back(rows, where, mask, cot, returned, gains, saved):
    queries, width = saved["y"].shape
    hidden = saved["gl"].shape[1]
    outs = [
        jax.ShapeDtypeStruct((queries, width), f32),
        jax.ShapeDtypeStruct((queries, width), bf16),
        jax.ShapeDtypeStruct((8, width), f32),
        jax.ShapeDtypeStruct((queries, hidden // 2 + width), bf16),
    ]
    operands = [where, mask, cot, returned, gains, saved["y"], saved["gl"]]
    return plain_call(
        functools.partial(start_kernel, rows), operands, [SMEM] + [VMEM] * 6, outs, "start_back"
    )


def up_kernel(rows, where_ref, dy_ref, gp_ref, h2_ref, down_ref, up_ref, *outs):
    keep, send, upb_out, dh2_out = outs
    hidden = gp_ref.shape[1]
    half = TILE // 2

    @pl.when(active(where_ref, rows))
    def _():
        dy = dy_ref[...]
        low_first = bit_of(where_ref, 1) == 0
        dh2 = jnp.zeros(dh2_out.shape, f32)
        for step in range(hidden // TILE):
            cols = slice(step * TILE, (step + 1) * TILE)
            part = slice(step * half, (step + 1) * half)
            dgl = dot_nt(dy, down_ref[0, cols, :])
            du = (dgl * gp_ref[:, cols].astype(f32)).astype(bf16)
            upb_out[:, cols] = total(du.astype(f32))
            low, high = du[:, :half], du[:, half:]
            keep[:, part] = jnp.where(low_first, low, high)
            send[:, part] = jnp.where(low_first, high, low)
            dh2 = dh2 + dot_nt(du, up_ref[0, :, cols])
        dh2_out[...] = dh2
        send[:, hidden // 2 :] = h2_ref[...]


def up_back(rows, where, dy, saved, w_down, w_up):
    queries, width = dy.shape
    hidden = w_up.shape[2]
    outs = [
        jax.ShapeDtypeStruct((queries, hidden // 2), bf16),
        jax.ShapeDtypeStruct((queries, hidden // 2 + width), bf16),
        jax.ShapeDtypeStruct((1, hidden), f32),
        jax.ShapeDtypeStruct((queries, width), f32),
    ]
    operands = [where, dy, saved["gp"], saved["h2"], w_down, w_up]
    return plain_call(
        functools.partial(up_kernel, rows), operands, [SMEM] + [VMEM] * 5, outs, "up_back"
    )


ATTEND = ("dh2", "x1", "g", "a", "w_out", "qkv", "p", "w_in", "xs")


def attend_kernel(rows, n_in, *refs):
    where_ref, mask_ref, gains_ref, vec_ref, upb_ref = refs[:5]
    held = dict(zip(ATTEND, refs[5 : 5 + len(ATTEND)]))
    da_out, dqkv, token_out, ret_out, vec_out, do_ref = refs[n_in:]
    images, top, queries = rows.images, rows.top, rows.queries
    width = upb_ref.shape[1] // 4
    scale = HEAD_DIM**-0.5

    @pl.when(active(where_ref, rows))
    def _():
        flag, place, count = sort_rows(mask_ref, rows)
        usable_rows = valid_rows(count, rows)
        unit, spread = normed(held["x1"][...])
        dh2 = held["dh2"][...]
        vec_out[...] = jnp.zeros(vec_out.shape, f32)
        vec_out[2:3, :] = total(dh2 * unit)
        vec_out[8:9, :] = total(dh2)
        dx1 = held["g"][...] + norm_back(dh2, unit, spread, gains_ref[0, 2:3, :])
        da = (dx1 * gains_ref[0, 1:2, :] * usable_rows).astype(bf16)
        vec_out[1:2, :] = total(dx1 * held["a"][...].astype(f32) * usable_rows)
        vec_out[7:8, :] = total(da.astype(f32))
        da_out[...] = da
        do_ref[...] = dot_nt(da, held["w_out"][0]).astype(bf16)
        qkv = held["qkv"]
        lane = iota((1, LANES), 1)
        sides = [(lane < HEAD_DIM), (lane >= HEAD_DIM)]
        masks = [jnp.where(side, 1.0, 0.0).astype(bf16) for side in sides]
        if rows.rest:
            dqkv[queries:, 0:width] = jnp.zeros((rows.total - queries, width), bf16)

        @pl.loop(0, PAIRS)
        def _(pair):
            lo = pl.multiple_of(pair * LANES, LANES)
            for b in range(images):
                q = qkv[b * top : (b + 1) * top, pl.ds(lo, LANES)]
                k = key_rows(qkv, b, pl.ds(width + lo, LANES), rows)
                v = key_rows(qkv, b, pl.ds(2 * width + lo, LANES), rows)
                do = do_ref[b * top : (b + 1) * top, pl.ds(lo, LANES)]
                parts = []
                for side in range(2):
                    p = held["p"][(b * 2 + side) * PAIRS + pair]
                    wide = p.astype(f32)
                    dp = dot_nt(do * masks[side], v)
                    inner = jnp.sum(wide * dp, axis=-1, keepdims=True)
                    draw = (wide * (dp - inner) * scale).astype(bf16)
                    parts.append((dot(draw, k), dot_tn(draw, q), dot_tn(p, do)))
                for at in range(3):
                    merged = jnp.where(sides[0], parts[0][at], parts[1][at]).astype(bf16)
                    lanes = pl.ds(at * width + lo, LANES)
                    dqkv[b * top : (b + 1) * top, lanes] = merged[:top]
                    if rows.rest and at > 0:
                        start = queries + b * rows.rest
                        dqkv[start : start + rows.rest, lanes] = merged[top:]

        dh1 = jnp.zeros((rows.total, width), f32)
        for at in range(3):
            cols = slice(at * width, (at + 1) * width)
            dh1 = dh1 + dot_nt(dqkv[:, cols], held["w_in"][0, :, cols])
        unit, spread = normed(held["xs"][...].astype(f32))
        dx = norm_back(dh1, unit, spread, gains_ref[0, 0:1, :])
        if rows.rest:
            rest = dx[queries:].astype(bf16)
        dx = dx[:queries] + dx1
        high = dx.astype(bf16)
        low = (dx - high.astype(f32)).astype(bf16)
        for b in range(images):
            chosen = pick(place, b, 0, top)
            mine = (chosen * flag[b : b + 1, :]).astype(bf16)
            part = slice(b * top, (b + 1) * top)
            token_out[0, b] = dot_tn(mine, high[part]) + dot_tn(mine, low[part])
            if not rows.first:
                height = ret_out.shape[0] // images
                place_in = iota((rows.keys, height), 0) - iota((rows.keys, height), 1)
                behind = place_in.astype(f32) == count[b : b + 1, :]
                seen = iota(behind.shape, 1).astype(f32) < rows.patches - count[b : b + 1, :]
                mover = jnp.where(behind & seen, 1.0, 0.0).astype(bf16)
                tail = slice(b * rows.rest, (b + 1) * rows.rest)
                back = dot_tn(mover[:top], high[part]) + dot_tn(mover[top:], rest[tail])
                ret_out[b * height : (b + 1) * height] = back.astype(bf16)
        vec_out[0:1, :] = total(dh1 * unit)
        vec_out[3:4, :] = vec_ref[0:1, :]
        vec_out[4:5, :] = total(dh1)
        vec_out[5:6, :] = total(dqkv[:, 0:width].astype(f32))
        vec_out[6:7, :] = total(dqkv[:, 2 * width :].astype(f32))
        vec_out[9:10, :] = vec_ref[1:2, :]
        for at in range(4):
            vec_out[10 + at : 11 + at, :] = upb_ref[:, at * width : (at + 1) * width]


def attend_back(rows, back_rows, where, mask, weights, vec, upb, dh2, grad, saved, token_before):
    w_in, w_out, _, _, gains, _, _, _ = weights
    queries, width = dh2.shape
    shape = (1, rows.images, rows.patches, width)
    values = dict(saved, dh2=dh2, g=grad, w_in=w_in, w_out=w_out)
    operands = [where, mask, gains, vec, upb] + [values[name] for name in ATTEND]
    outs = [
        jax.ShapeDtypeStruct((queries, width), bf16),
        jax.ShapeDtypeStruct((rows.total, 3 * width), bf16),
        jax.ShapeDtypeStruct(shape, f32),
        jax.ShapeDtypeStruct((8 if rows.first else back_rows, width), bf16),
        jax.ShapeDtypeStruct((16, width), f32),
    ]
    aliases = {}
    if token_before is not None:
        aliases[len(operands)] = 2
        operands.append(token_before)
    return plain_call(
        functools.partial(attend_kernel, rows, len(operands)),
        operands,
        [SMEM] + [VMEM] * (len(operands) - 1),
        outs,
        "attend_back",
        [pltpu.VMEM((queries, width), bf16)],
        aliases,
    )


def in_kernel(rows, order, where_ref, dqkv_ref, h1_ref, da_ref, o_ref, keep, send, out_buf, in_buf):
    @pl.when(active(where_ref, rows))
    def _():
        lean, tall = out_buf.shape[1], in_buf.shape[1]
        tile = dot_tn(da_ref[...], o_ref[...]).astype(bf16)
        for d in range(16):
            out_buf[d] = tile[d * lean : (d + 1) * lean]
        half = dqkv_ref.shape[1] // 2
        for step in range(2):
            tile = dot_tn(dqkv_ref[:, step * half : (step + 1) * half], h1_ref[...]).astype(bf16)
            for d in range(8):
                in_buf[8 * step + d] = tile[d * tall : (d + 1) * tall]
        bit = bit_of(where_ref, order)
        for slot in range(8):
            z, other = slot >> 1, slot & 1
            base = 4 * z + (2 * other if order == 0 else other)
            for target, own in ((keep, bit), (send, 1 - bit)):
                d = base + (own if order == 0 else 2 * own)
                target[slot, :lean] = out_buf[d]
                target[slot, lean:] = in_buf[d]


def in_back(rows, order, where, dqkv, h1, da, o):
    width = h1.shape[1]
    lean, tall = width // 16, dqkv.shape[1] // 16
    outs = [jax.ShapeDtypeStruct((8, lean + tall, width), bf16)] * 2
    scratch = [pltpu.VMEM((16, lean, width), bf16), pltpu.VMEM((16, tall, width), bf16)]
    return plain_call(
        functools.partial(in_kernel, rows, order),
        [where, dqkv, h1, da, o],
        [SMEM] + [VMEM] * 4,
        outs,
        "in_grad",
        scratch,
    )


def down_grad_kernel(where_ref, *refs):
    keep, send, buf = refs[6:]
    height = buf.shape[1]
    half = buf.shape[2]
    bit = bit_of(where_ref, 1)
    for section in range(2):

        @pl.when(where_ref[0] == section)
        def _():
            gl, dy, got = refs[3 * section : 3 * section + 3]
            mine = pl.multiple_of(bit_of(where_ref, 0) * half, half)
            tile = dot_tn(dy[...], gl[:, pl.ds(mine, half)])
            tile = (tile + dot_tn(got[:, half:], got[:, :half])).astype(bf16)
            for d in range(16):
                buf[d] = tile[d * height : (d + 1) * height]

    for slot in range(8):
        z, x = slot >> 1, slot & 1
        keep[slot] = buf[4 * z + x + 2 * bit]
        send[slot] = buf[4 * z + x + 2 * (1 - bit)]


def down_grad(where, first, second):
    hidden = first[0].shape[1]
    width = first[1].shape[1]
    shape = (width // 16, hidden // 2)
    outs = [jax.ShapeDtypeStruct((8,) + shape, bf16)] * 2
    return plain_call(
        down_grad_kernel,
        [where, *first, *second],
        [SMEM] + [VMEM] * 6,
        outs,
        "down_grad",
        [pltpu.VMEM((16,) + shape, bf16)],
    )


def up_grad_kernel(where_ref, *refs):
    keep, send, buf = refs[6:]
    height = buf.shape[1]
    half = 8 * height
    bit = bit_of(where_ref, 0)
    for section in range(2):

        @pl.when(where_ref[0] == section)
        def _():
            du, h2, got = refs[3 * section : 3 * section + 3]
            tile = dot_tn(du[...], h2[...])
            tile = (tile + dot_tn(got[:, :half], got[:, half:])).astype(bf16)
            for d in range(8):
                buf[d] = tile[d * height : (d + 1) * height]

    for z in range(4):
        keep[z] = buf[2 * z + bit]
        send[z] = buf[2 * z + 1 - bit]


def up_grad(where, first, second):
    half = first[0].shape[1]
    width = first[1].shape[1]
    shape = (half // 8, width)
    outs = [jax.ShapeDtypeStruct((4,) + shape, bf16)] * 2
    return plain_call(
        up_grad_kernel,
        [where, *first, *second],
        [SMEM] + [VMEM] * 6,
        outs,
        "up_grad",
        [pltpu.VMEM((8,) + shape, bf16)],
    )


def wide_sum(*terms):
    result = terms[0].astype(f32)
    for term in terms[1:]:
        result = result + term.astype(f32)
    return result


def swap(value, by, count):
    return lax.ppermute(value, "dp", [(i, i ^ by) for i in range(count)])


def one(parts, at, axis=0):
    return lax.dynamic_index_in_dim(parts, at, axis, keepdims=False)


def line_sum(terms, z, count):
    others = [
        swap(wide_sum(*(one(term, z ^ k) for term in terms)).astype(bf16), 4 * k, count)
        for k in (3, 2, 1)
    ]
    return wide_sum(*(one(term, z) for term in terms), *others)


def on_device(
    tokens,
    patch_mask,
    cotangent,
    in_weight,
    out_weight,
    up_weight,
    down_weight,
    gains,
    biases,
    up_bias,
    down_bias,
):
    weights = (in_weight, out_weight, up_weight, down_weight, gains, biases, up_bias, down_bias)
    images, patches, width = tokens.shape
    hidden = up_weight.shape[2]
    count = lax.axis_size("dp")
    section = lax.axis_index("section")
    place = lax.axis_index("dp")
    is_first = section == 0
    where = jnp.stack([section, place]).astype(jnp.int32)
    x, y, z = place & 1, (place >> 1) & 1, place >> 2
    small = count == 16
    rows = [Rows(True, images, patches), Rows(False, images, patches)]

    def exchange(value, phase, by):
        pairs = [(phase * count + i, phase * count + (i ^ by)) for i in range(count)]
        return lax.ppermute(value, ("section", "dp"), pairs) if small else value

    result, sent, kept_first = forward(rows[0], where, patch_mask, tokens, tokens, weights, None)
    latent = lax.ppermute(sent, "section", [(0, 1)])
    result, _, kept_second = forward(rows[1], where, patch_mask, tokens, latent, weights, result)
    kept = [kept_first, kept_second]

    down_parts, up_parts, in_parts, products = [{}, {}, {}, {}]
    vectors = {}
    returned = latent
    token_grads = None
    for phase in (1, 0):
        layout, saved = rows[phase], kept[phase]
        grad, dy, vec, send = start_back(
            layout, where, patch_mask, cotangent, returned, gains, saved
        )
        down_parts[phase] = (saved["gl"], dy, exchange(send, phase, 1))
        keep, send, upb, dh2 = up_back(layout, where, dy, saved, down_weight, up_weight)
        up_parts[phase] = (keep, saved["h2"], exchange(send, phase, 2))
        da, dqkv, token_grads, back, vectors[phase] = attend_back(
            layout,
            rows[0].queries,
            where,
            patch_mask,
            weights,
            vec,
            upb,
            dh2,
            grad,
            saved,
            token_grads,
        )
        if phase == 1:
            returned = lax.ppermute(back, "section", [(1, 0)])
        order = phase ^ 1
        if small:
            keep, send = in_back(layout, order, where, dqkv, saved["h1"], da, saved["o"])
            in_parts[phase] = (keep, exchange(send, phase, 1 << order))
        else:
            half = TILE // 2
            halves = [keep.reshape(-1, 4, half), send[:, : hidden // 2].reshape(-1, 4, half)]
            du = jnp.where(
                y == 0, jnp.stack(halves, axis=2), jnp.stack(halves[::-1], axis=2)
            ).reshape(-1, hidden)
            products[phase] = [
                dot_tn(left, right)
                for left, right in (
                    (dqkv, saved["h1"]),
                    (da, saved["o"]),
                    (du, saved["h2"]),
                    (dy, saved["gl"]),
                )
            ]

    vec = jnp.where(is_first, vectors[0], vectors[1])
    if small:
        keep, send = down_grad(where, down_parts[0], down_parts[1])
        terms = [keep, swap(send, 2, count)]
        part = line_sum(
            [term.reshape(4, 2, *term.shape[1:]) for term in terms], z, count
        )
        mine = one(part, x)
        other = swap(one(part, 1 - x).astype(bf16), 1, count).astype(f32)
        down = jnp.where(
            x == 0,
            jnp.concatenate([mine, other], axis=1),
            jnp.concatenate([other, mine], axis=1),
        )
        keep, send = up_grad(where, up_parts[0], up_parts[1])
        up = line_sum([keep, swap(send, 1, count)], z, count)
        merged = jnp.where(is_first, wide_sum(*in_parts[0]), wide_sum(*in_parts[1])).astype(bf16)
        merged = merged.reshape((4, 2) + merged.shape[1:])
        bit = jnp.where(is_first, x, y)
        pairs = [(i, i ^ 1) for i in range(count)]
        pairs += [(count + i, count + (i ^ 2)) for i in range(count)]
        got = lax.ppermute(one(merged, 1 - bit, 1), ("section", "dp"), pairs)
        both = line_sum([one(merged, bit, 1), got], z, count)
        finals = [both[width // 16 :], both[: width // 16], up, down]
        for by in (1, 2, 4, 8):
            vec = vec + swap(vec, by, count)
    else:
        finals = [
            lax.psum_scatter(
                jnp.where(is_first, left, right), "dp", scatter_dimension=0, tiled=True
            )
            for left, right in zip(products[0], products[1])
        ]
        vec = lax.psum(vec, "dp")

    def columns(values):
        size = values.shape[-1] // count
        return lax.dynamic_slice_in_dim(values, place * size, size, values.ndim - 1)

    return (
        result,
        token_grads,
        *(final.T[None] for final in finals),
        columns(vec[0:4])[None],
        columns(vec[4:9])[None],
        columns(vec[10:14].reshape(1, hidden)),
        columns(vec[9:10]),
    )


def solution(mesh):
    return jax.shard_map(
        on_device,
        mesh=mesh,
        in_specs=(
            P("dp", None, None),
            P("dp", None),
            P("section", "dp", None, None),
            P("section", None, None),
            P("section", None, None),
            P("section", None, None),
            P("section", None, None),
            P("section", None, None),
            P("section", None, None),
            P("section", None),
            P("section", None),
        ),
        out_specs=(
            P("section", "dp", None, None),
            P("section", "dp", None, None),
            P("section", None, "dp"),
            P("section", None, "dp"),
            P("section", None, "dp"),
            P("section", None, "dp"),
            P("section", None, "dp"),
            P("section", None, "dp"),
            P("section", "dp"),
            P("section", "dp"),
        ),
        check_vma=False,
    )
```

```python
import functools

import jax
import jax.numpy as jnp
from jax import lax
from jax.experimental import pallas as pl
from jax.experimental.pallas import tpu as pltpu
from jax.sharding import PartitionSpec

HEADS = 12
HEAD_DIM = 64
PAIRS = HEADS // 2
LANES = 2 * HEAD_DIM
MASK_LO = 59
MASK_HI = 117
TILE = 768

(
    W_IN,
    W_OUT,
    W_UP,
    W_DOWN,
    XS,
    H1,
    QKV,
    P,
    O,
    A,
    X1,
    H2,
    GP,
    GL,
    Y,
    SEND_DOWN,
    KEEP_UP,
    SEND_UP,
    GL_SEND,
    HO,
    KEEP_IO,
    SEND_IO,
    DA,
    DQKV,
    DY,
    DU,
    DO,
    VEC,
    MASK,
    TOKENS,
    LATENT,
    GAINS,
    BIASES,
    UP_BIAS,
    DOWN_BIAS,
    COT,
    RETURNED,
) = range(37)

UNROLL = 6
UNROLL_BACK = 6
MIB = 2**20

epsilon = 1e-06
f32 = jnp.float32
bf16 = jnp.bfloat16
ANY = pl.BlockSpec(memory_space=pl.ANY)
SMEM = pl.BlockSpec(memory_space=pltpu.SMEM)
VMEM = pl.BlockSpec(memory_space=pltpu.VMEM)


def cost(micros, memory=None):
    size = int((memory or micros) * 3.69e6)
    return pl.CostEstimate(flops=int(micros * 1.15e9), bytes_accessed=size, transcendentals=0)


def up16(count):
    return -(-count // 16) * 16


class Rows:
    def __init__(self, first, images, patches):
        most = patches - MASK_LO if first else MASK_HI
        self.first = first
        self.images = images
        self.patches = patches
        self.top = up16(most)
        self.rest = 0 if first else up16(patches - self.top)
        self.keys = self.top + self.rest
        self.queries = images * self.top
        self.total = images * self.keys


def dot(left, right):
    return jnp.dot(left, right, preferred_element_type=f32)


def dot_nt(left, right):
    return lax.dot_general(left, right, (((1,), (1,)), ((), ())), preferred_element_type=f32)


def dot_tn(left, right):
    return lax.dot_general(left, right, (((0,), (0,)), ((), ())), preferred_element_type=f32)


def iota(shape, dim):
    return lax.broadcasted_iota(jnp.int32, shape, dim)


def sort_rows(mask_ref, rows):
    masked = mask_ref[...].astype(f32)
    flag = 1.0 - masked if rows.first else masked
    n = rows.patches
    tri = jnp.where(iota((n, n), 0) <= iota((n, n), 1), 1.0, 0.0).astype(bf16)
    upto = dot(flag.astype(bf16), tri)
    count = jnp.sum(flag, axis=1, keepdims=True)
    at = iota(flag.shape, 1).astype(f32)
    place = jnp.where(flag > 0, upto - 1.0, count + at - upto)
    return flag, place, count


def pick(place, image, start, length):
    slots = iota((length, place.shape[1]), 0).astype(f32) + float(start)
    return jnp.where(slots == place[image : image + 1, :], 1.0, 0.0)


def valid_rows(count, rows):
    parts = [
        jnp.where(iota((rows.top, 1), 0).astype(f32) < count[b : b + 1, :], 1.0, 0.0)
        for b in range(rows.images)
    ]
    return jnp.concatenate(parts, axis=0)


def normed(states):
    centre = states - jnp.mean(states, axis=-1, keepdims=True)
    spread = jnp.mean(centre * centre, axis=-1, keepdims=True)
    scale = lax.rsqrt(spread + epsilon)
    return centre * scale, scale


def norm_back(grad, unit, scale, gain):
    inner = grad * gain
    along = jnp.mean(inner * unit, axis=-1, keepdims=True)
    return scale * (inner - jnp.mean(inner, axis=-1, keepdims=True) - unit * along)


def gelu_parts(values):
    size = jnp.abs(values) * (0.5**0.5)
    t = 1.0 / (1.0 + 0.3275911 * size)
    series = t * (
        0.254829592
        + t * (-0.284496736 + t * (1.421413741 + t * (-1.453152027 + t * 1.061405429)))
    )
    decay = jnp.exp(-0.5 * values * values)
    upper = 0.5 * series * decay
    below = jnp.where(values < 0, upper, 1.0 - upper)
    return below, decay * 0.3989422804014327


def total(values):
    return jnp.sum(values, axis=0, keepdims=True)


def key_rows(ref, image, lanes, rows):
    block = ref[image * rows.top : (image + 1) * rows.top, lanes]
    if rows.rest == 0:
        return block
    start = rows.queries + image * rows.rest
    return jnp.concatenate([block, ref[start : start + rows.rest, lanes]], axis=0)


class Copies:
    def __init__(self, sems):
        self.sems = sems
        self.used = 0

    def start(self, source, target):
        copy = pltpu.make_async_copy(source, target, self.sems.at[self.used])
        self.used += 1
        copy.start()
        return copy


SAVED = (XS, H1, QKV, P, O, A, X1, H2, GP, GL, Y)
WEIGHTS = (W_IN, W_OUT, W_UP, W_DOWN)


def kept_shapes(rows, width, hidden):
    queries = rows.queries
    return {
        W_IN: ((width, 3 * width), bf16),
        W_OUT: ((width, width), bf16),
        W_UP: ((width, hidden), bf16),
        W_DOWN: ((hidden, width), bf16),
        XS: ((rows.total, width), bf16),
        H1: ((rows.total, width), bf16),
        QKV: ((rows.total, 3 * width), bf16),
        P: ((rows.images * PAIRS, 2 * rows.top, rows.keys), bf16),
        O: ((queries, width), bf16),
        A: ((queries, width), bf16),
        X1: ((queries, width), f32),
        H2: ((queries, width), bf16),
        GP: ((queries, hidden), bf16),
        GL: ((queries, hidden), bf16),
        Y: ((queries, width), bf16),
        SEND_DOWN: ((queries, hidden // 2 + width), bf16),
        KEEP_UP: ((queries, hidden // 2), bf16),
        SEND_UP: ((queries, hidden // 2 + width), bf16),
        GL_SEND: ((queries, hidden // 2), bf16),
        HO: ((queries, 2 * width), bf16),
        KEEP_IO: ((queries, 2 * width), bf16),
        SEND_IO: ((queries + 16, 2 * width), bf16),
        DA: ((queries, width), bf16),
        DQKV: ((rows.total, 3 * width), bf16),
        DY: ((queries, width), bf16),
        DU: ((queries, hidden // 2), bf16),
        DO: ((queries, width), bf16),
        VEC: ((16, width), f32),
    }


def bit_of(where_ref, order):
    return (where_ref[1] >> order) & 1


def active(where_ref, rows):
    return where_ref[0] == (0 if rows.first else 1)


def lane_sides():
    lane = iota((1, LANES), 1)
    sides = [(lane < HEAD_DIM), (lane >= HEAD_DIM)]
    return sides, [jnp.where(side, 1.0, 0.0).astype(bf16) for side in sides]


def two_heads(values, masks):
    return jnp.concatenate([values * masks[0], values * masks[1]], axis=0)


def mover(count, rows, image, start, length, height):
    behind = iota((length, height), 0) - iota((length, height), 1)
    behind = behind.astype(f32) + float(start) == count[image : image + 1, :]
    seen = iota((length, height), 1).astype(f32) < rows.patches - count[image : image + 1, :]
    return jnp.where(behind & seen, 1.0, 0.0).astype(bf16)


def forward_part(rows, order, small, held, wait, done):
    tok_ref, lat_ref = small[TOKENS], small[LATENT]
    gains_ref, biases_ref = small[GAINS], small[BIASES]
    flag, place, count = order
    images, top, queries = rows.images, rows.top, rows.queries
    width = held[W_OUT].shape[0]
    scale = HEAD_DIM**-0.5

    def states_of(b, start, length):
        chosen = pick(place, b, start, length)
        if rows.first:
            return dot(chosen.astype(bf16), tok_ref[:, b, :])
        from_tokens = dot((chosen * flag[b : b + 1, :]).astype(bf16), tok_ref[:, b, :])
        height = lat_ref.shape[0] // images
        move = mover(count, rows, b, start, length, height)
        return from_tokens + dot(move, lat_ref[b * height : (b + 1) * height])

    pieces = [states_of(b, 0, top) for b in range(images)]
    if rows.rest:
        pieces += [states_of(b, top, rows.rest) for b in range(images)]
    states = jnp.concatenate(pieces, axis=0)
    held[XS][...] = states.astype(bf16)
    done(XS)
    unit, _ = normed(states)
    h1 = (unit * gains_ref[0, 0:1, :] + biases_ref[0]).astype(bf16)
    held[H1][...] = h1
    done(H1)
    qkv = held[QKV]
    wi = held[W_IN]
    wait(W_IN)
    qkv[0:queries, 0:width] = (dot(h1[:queries], wi[:, :width]) + biases_ref[1]).astype(bf16)
    if rows.rest:
        qkv[queries:, 0:width] = jnp.zeros((rows.total - queries, width), bf16)
    qkv[:, width : 2 * width] = dot(h1, wi[:, width : 2 * width]).astype(bf16)
    qkv[:, 2 * width :] = (dot(h1, wi[:, 2 * width :]) + biases_ref[2]).astype(bf16)
    done(QKV)
    sides, masks = lane_sides()

    @pl.loop(0, PAIRS, unroll=UNROLL)
    def _(pair):
        lo = pl.multiple_of(pair * LANES, LANES)
        for b in range(images):
            q = qkv[b * top : (b + 1) * top, pl.ds(lo, LANES)]
            k = key_rows(qkv, b, pl.ds(width + lo, LANES), rows)
            v = key_rows(qkv, b, pl.ds(2 * width + lo, LANES), rows)
            at = iota((1, rows.keys), 1).astype(f32)
            if rows.first:
                usable = at < count[b : b + 1, :]
            else:
                usable = at < float(rows.patches)
            raw = dot_nt(two_heads(q, masks), k)
            logits = jnp.where(usable, raw * scale, -1e30)
            grown = jnp.exp(logits - jnp.max(logits, axis=-1, keepdims=True))
            p = (grown * (1.0 / jnp.sum(grown, axis=-1, keepdims=True))).astype(bf16)
            held[P][b * PAIRS + pair] = p
            mixed = dot(p, v)
            held[O][b * top : (b + 1) * top, pl.ds(lo, LANES)] = jnp.where(
                sides[0], mixed[:top], mixed[top:]
            ).astype(bf16)

    done(P)
    done(O)
    wait(W_OUT)
    a = dot(held[O][...], held[W_OUT][...]) + biases_ref[3]
    held[A][...] = a.astype(bf16)
    done(A)
    usable_rows = valid_rows(count, rows)
    x1 = states[:queries] + gains_ref[0, 1:2, :] * a * usable_rows
    held[X1][...] = x1
    done(X1)
    unit, _ = normed(x1)
    h2 = (unit * gains_ref[0, 2:3, :] + biases_ref[4]).astype(bf16)
    held[H2][...] = h2
    done(H2)
    wait(W_UP)
    y = jnp.zeros((queries, width), f32)
    for start in range(0, held[W_UP].shape[1], TILE):
        cols = slice(start, start + TILE)
        u = dot(h2, held[W_UP][:, cols]) + small[UP_BIAS][:, cols]
        below, density = gelu_parts(u)
        gl = (u * below).astype(bf16)
        held[GL][:, cols] = gl
        held[GP][:, cols] = (below + u * density).astype(bf16)
        done(GL, cols)
        done(GP, cols)
        wait(W_DOWN)
        y = y + dot(gl, held[W_DOWN][cols, :])
    done(GL_SEND)
    y = y + small[DOWN_BIAS][...]
    held[Y][...] = y.astype(bf16)
    done(Y)
    return (x1 + gains_ref[0, 3:4, :] * y * usable_rows).astype(bf16)


def unsort(rows, order, values, result):
    flag, place, _ = order
    for b in range(rows.images):
        chosen = (pick(place, b, 0, rows.top) * flag[b : b + 1, :]).astype(bf16)
        result[:, b, :] = dot_tn(chosen, values[b * rows.top : (b + 1) * rows.top]).astype(bf16)


def backward_part(rows, order, where_ref, small, held, wait, done, token_buf, ret_buf):
    cot_ref, gains_ref = small[COT], small[GAINS]
    flag, place, count = order
    images, top, queries = rows.images, rows.top, rows.queries
    hidden, width = held[W_DOWN].shape
    scale = HEAD_DIM**-0.5
    usable_rows = valid_rows(count, rows)
    vec = held[VEC]
    vec[...] = jnp.zeros(vec.shape, f32)
    pieces = []
    for b in range(images):
        chosen = (pick(place, b, 0, top) * flag[b : b + 1, :]).astype(bf16)
        piece = dot(chosen, cot_ref[0, :, b, :])
        if rows.first:
            piece = piece + small[RETURNED][b * top : (b + 1) * top].astype(f32)
        pieces.append(piece)
    grad = jnp.concatenate(pieces, axis=0)
    dy = (grad * gains_ref[0, 3:4, :] * usable_rows).astype(bf16)
    held[DY][...] = dy
    done(DY)
    wait(Y)
    vec[3:4, :] = total(grad * held[Y][...].astype(f32))
    vec[9:10, :] = total(dy.astype(f32))

    low_first = bit_of(where_ref, 1) == 0
    half = TILE // 2
    dh2 = jnp.zeros((queries, width), f32)
    wait(W_DOWN)
    wait(GP)
    wait(W_UP)
    for step in range(hidden // TILE):
        cols = slice(step * TILE, (step + 1) * TILE)
        part = slice(step * half, (step + 1) * half)
        dgl = dot_nt(dy, held[W_DOWN][cols, :])
        du = (dgl * held[GP][:, cols].astype(f32)).astype(bf16)
        vec[10 + step : 11 + step, :] = total(du.astype(f32))
        low, high = du[:, :half], du[:, half:]
        held[KEEP_UP][:, part] = jnp.where(low_first, low, high)
        held[DU][:, part] = jnp.where(low_first, high, low)
        dh2 = dh2 + dot_nt(du, held[W_UP][:, cols])
    done(KEEP_UP)
    done(DU)

    wait(X1)
    unit, spread = normed(held[X1][...])
    vec[2:3, :] = total(dh2 * unit)
    vec[8:9, :] = total(dh2)
    dx1 = grad + norm_back(dh2, unit, spread, gains_ref[0, 2:3, :])
    da = (dx1 * gains_ref[0, 1:2, :] * usable_rows).astype(bf16)
    wait(A)
    vec[1:2, :] = total(dx1 * held[A][...].astype(f32) * usable_rows)
    vec[7:8, :] = total(da.astype(f32))
    held[DA][...] = da
    done(DA)
    do_ref = held[DO]
    wait(W_OUT)
    do_ref[...] = dot_nt(da, held[W_OUT][...]).astype(bf16)
    qkv, dqkv = held[QKV], held[DQKV]
    sides, masks = lane_sides()
    if rows.rest:
        dqkv[queries:, 0:width] = jnp.zeros((rows.total - queries, width), bf16)
    wait(QKV)
    wait(P)

    @pl.loop(0, PAIRS, unroll=UNROLL_BACK)
    def _(pair):
        lo = pl.multiple_of(pair * LANES, LANES)
        for b in range(images):
            q = qkv[b * top : (b + 1) * top, pl.ds(lo, LANES)]
            k = key_rows(qkv, b, pl.ds(width + lo, LANES), rows)
            v = key_rows(qkv, b, pl.ds(2 * width + lo, LANES), rows)
            do = two_heads(do_ref[b * top : (b + 1) * top, pl.ds(lo, LANES)], masks)
            p = held[P][b * PAIRS + pair]
            wide = p.astype(f32)
            dp = dot_nt(do, v)
            inner = jnp.sum(wide * dp, axis=-1, keepdims=True)
            draw = (wide * (dp - inner) * scale).astype(bf16)
            mixed = dot(draw, k)
            dq = jnp.where(sides[0], mixed[:top], mixed[top:])
            dk = dot_tn(draw, two_heads(q, masks))
            dv = dot_tn(p, do)
            for at, part in enumerate((dq, dk, dv)):
                part = part.astype(bf16)
                lanes = pl.ds(at * width + lo, LANES)
                dqkv[b * top : (b + 1) * top, lanes] = part[:top]
                if rows.rest and at > 0:
                    start = queries + b * rows.rest
                    dqkv[start : start + rows.rest, lanes] = part[top:]

    done(DQKV)
    if rows.first:
        at = 0
        for values in (dqkv, held[DA]):
            size = values.shape[1] // 8
            for own in range(2):
                picked = [values[:, j * size : (j + 1) * size] for j in range(own, 8, 2)]
                lanes = slice(at, at + 4 * size)
                picked = jnp.concatenate(picked, axis=1)
                keep = held[KEEP_IO]
                if own == 0:
                    keep[:, lanes] = picked
                else:
                    even = keep[:, lanes]
                    keep[:, lanes] = jnp.where(low_first, even, picked)
                    held[SEND_IO][:queries, lanes] = jnp.where(low_first, picked, even)
            at += 4 * size
        done(KEEP_IO)
    wait(W_IN)
    dh1 = jnp.zeros((rows.total, width), f32)
    for at in range(3):
        cols = slice(at * width, (at + 1) * width)
        dh1 = dh1 + dot_nt(dqkv[:, cols], held[W_IN][:, cols])
    wait(XS)
    unit, spread = normed(held[XS][...].astype(f32))
    dx = norm_back(dh1, unit, spread, gains_ref[0, 0:1, :])
    if rows.rest:
        rest = dx[queries:].astype(bf16)
    dx = dx[:queries] + dx1
    high = dx.astype(bf16)
    low = (dx - high.astype(f32)).astype(bf16)
    for b in range(images):
        chosen = pick(place, b, 0, top)
        mine = (chosen * flag[b : b + 1, :]).astype(bf16)
        part = slice(b * top, (b + 1) * top)
        if not rows.first:
            height = ret_buf.shape[0] // images
            move = mover(count, rows, b, 0, rows.keys, height)
            tail = slice(b * rows.rest, (b + 1) * rows.rest)
            back = dot_tn(move[:top], high[part]) + dot_tn(move[top:], rest[tail])
            ret_buf[b * height : (b + 1) * height] = back.astype(bf16)
        token_buf[:, b, :] = dot_tn(mine, high[part]) + dot_tn(mine, low[part])
    vec[0:1, :] = total(dh1 * unit)
    vec[4:5, :] = total(dh1)
    vec[5:6, :] = total(dqkv[:, 0:width].astype(f32))
    vec[6:7, :] = total(dqkv[:, 2 * width :].astype(f32))
    done(VEC)
    if rows.first:
        held[SEND_IO][queries:, :width] = vec[...].astype(bf16)
        held[SEND_IO][queries:, width:] = jnp.zeros((16, width), bf16)
        done(SEND_IO)


class Flow:
    def __init__(self, held, sems):
        self.held = held
        self.copies = Copies(sems)
        self.gets = {}
        self.puts = []

    def fetch(self, name, ref):
        self.gets[name] = self.copies.start(ref, self.held[name])

    def wait(self, name):
        if name in self.gets:
            self.gets.pop(name).wait()

    def put(self, source, target):
        self.puts.append(self.copies.start(source, target))

    def finish(self):
        for name in list(self.gets):
            self.wait(name)
        for copy in self.puts:
            copy.wait()


FORWARD_SMALL = (MASK, TOKENS, LATENT, GAINS, BIASES, UP_BIAS, DOWN_BIAS)
SECOND_SMALL = FORWARD_SMALL + (COT,)
BACK_SMALL = (MASK, COT, RETURNED, GAINS)
FIRST_HELD = WEIGHTS + SAVED
FIRST_OUTS = (XS, QKV, P, A, X1, H2, GP, GL, Y, GL_SEND, HO)
SECOND_HELD = WEIGHTS + SAVED + (KEEP_UP, DA, DQKV, DY, DU, DO, VEC)
SECOND_OUTS = (H1, O, GL, SEND_DOWN, KEEP_UP, SEND_UP, DA, DQKV, VEC)
BACK_IN = WEIGHTS + (XS, QKV, P, A, X1, GP, Y)
BACK_OUTS = (DY, KEEP_UP, DU, KEEP_IO, SEND_IO, VEC)
BACK_HELD = BACK_IN + (DA, DQKV, DO) + BACK_OUTS


def take_from(refs):
    def take(names):
        taken = dict(zip(names, refs))
        del refs[: len(names)]
        return taken

    return take


def other_half(where_ref, half):
    return pl.ds(pl.multiple_of((1 - bit_of(where_ref, 0)) * half, half), half)


def first_kernel(rows, where_ref, *refs):
    refs = list(refs)
    take = take_from(refs)
    small, weights = take(FORWARD_SMALL), take(WEIGHTS)
    (result, x2_out), outs = (refs.pop(0), refs.pop(0)), take(FIRST_OUTS)
    held = take(FIRST_HELD)
    res, x2_buf, sems = refs

    @pl.when(active(where_ref, rows))
    def _():
        flow = Flow(held, sems)
        for name in WEIGHTS:
            flow.fetch(name, weights[name].at[0])
        order = sort_rows(small[MASK], rows)
        width = held[O].shape[1]

        def done(name, cols=None):
            if cols is not None:
                flow.put(held[name].at[:, cols], outs[name].at[:, cols])
            elif name in (H1, O):
                start = 0 if name == H1 else width
                flow.put(held[name], outs[HO].at[:, pl.ds(start, width)])
            elif name == GL_SEND:
                half = held[GL].shape[1] // 2
                flow.put(held[GL].at[:, other_half(where_ref, half)], outs[GL_SEND])
            else:
                flow.put(held[name], outs[name])

        x2 = forward_part(rows, order, small, held, flow.wait, done)
        x2_buf[...] = x2
        flow.put(x2_buf, x2_out)
        unsort(rows, order, x2, res)
        flow.put(res, result.at[0])
        flow.finish()


def big_call(kernel, operands, in_specs, outs, scratch, name, micros, aliases=None):
    return pl.pallas_call(
        kernel,
        out_shape=outs,
        in_specs=in_specs,
        out_specs=[ANY] * len(outs),
        scratch_shapes=scratch,
        input_output_aliases=aliases or {},
        compiler_params=pltpu.CompilerParams(vmem_limit_bytes=56 * MIB),
        cost_estimate=cost(micros),
        name=name,
    )(*operands)


def shaped(shapes, names, make):
    return [make(*shapes[name]) for name in names]


def first_block(rows, where, small, weights):
    width, hidden = weights[2].shape[1:]
    shapes = kept_shapes(rows, width, hidden)
    tokens = small[TOKENS]
    outs = [
        jax.ShapeDtypeStruct((1,) + tokens.shape, bf16),
        jax.ShapeDtypeStruct((rows.queries, width), bf16),
    ]
    results = big_call(
        functools.partial(first_kernel, rows),
        [where] + [small[name] for name in FORWARD_SMALL] + list(weights),
        [SMEM] + [VMEM] * len(FORWARD_SMALL) + [ANY] * 4,
        outs + shaped(shapes, FIRST_OUTS, jax.ShapeDtypeStruct),
        shaped(shapes, FIRST_HELD, pltpu.VMEM)
        + [pltpu.VMEM(tokens.shape, bf16), pltpu.VMEM((rows.queries, width), bf16)]
        + [pltpu.SemaphoreType.DMA((32,))],
        "first_block",
        1500,
    )
    return results[0], results[1], dict(zip(FIRST_OUTS, results[2:]))


def second_kernel(rows, where_ref, *refs):
    refs = list(refs)
    take = take_from(refs)
    small, weights = take(SECOND_SMALL), take(WEIGHTS)
    refs.pop(0)
    result, token_out, ret_out = (refs.pop(0) for _ in range(3))
    outs = take(SECOND_OUTS)
    held = take(SECOND_HELD)
    res, token_buf, ret_buf, sems = refs

    @pl.when(active(where_ref, rows))
    def _():
        flow = Flow(held, sems)
        for name in WEIGHTS:
            flow.fetch(name, weights[name].at[0])
        order = sort_rows(small[MASK], rows)
        queries, half = held[KEEP_UP].shape
        width = held[DY].shape[1]

        def done(name, cols=None):
            if cols is not None:
                if name in outs:
                    flow.put(held[name].at[:, cols], outs[name].at[:, cols])
            elif name == GL_SEND:
                flow.put(
                    held[GL].at[:, other_half(where_ref, half)],
                    outs[SEND_DOWN].at[:, pl.ds(0, half)],
                )
            elif name == H2:
                flow.put(held[H2], outs[SEND_UP].at[:, pl.ds(half, width)])
            elif name == DY:
                flow.put(held[DY], outs[SEND_DOWN].at[:, pl.ds(half, width)])
            elif name == DU:
                flow.put(held[DU], outs[SEND_UP].at[:, pl.ds(0, half)])
            elif name in outs:
                flow.put(held[name], outs[name])

        x2 = forward_part(rows, order, small, held, flow.wait, done)
        backward_part(
            rows, order, where_ref, small, held, flow.wait, done, token_buf, ret_buf
        )
        flow.put(ret_buf, ret_out)
        flow.put(token_buf, token_out.at[0])
        unsort(rows, order, x2, res)
        flow.put(res, result.at[0])
        flow.finish()


def second_block(rows, where, small, weights, before, back_rows):
    width, hidden = weights[2].shape[1:]
    shapes = kept_shapes(rows, width, hidden)
    shape = small[TOKENS].shape
    operands = [where] + [small[name] for name in SECOND_SMALL] + list(weights) + [before]
    outs = [
        jax.ShapeDtypeStruct((1,) + shape, bf16),
        jax.ShapeDtypeStruct((1,) + shape, f32),
        jax.ShapeDtypeStruct((back_rows, width), bf16),
    ]
    results = big_call(
        functools.partial(second_kernel, rows),
        operands,
        [SMEM] + [VMEM] * len(SECOND_SMALL) + [ANY] * 5,
        outs + shaped(shapes, SECOND_OUTS, jax.ShapeDtypeStruct),
        shaped(shapes, SECOND_HELD, pltpu.VMEM)
        + [
            pltpu.VMEM(shape, bf16),
            pltpu.VMEM(shape, f32),
            pltpu.VMEM((back_rows, width), bf16),
            pltpu.SemaphoreType.DMA((32,)),
        ],
        "second_block",
        3000,
        {len(operands) - 1: 0},
    )
    return results[0], results[1], results[2], dict(zip(SECOND_OUTS, results[3:]))


def back_kernel(rows, where_ref, *refs):
    refs = list(refs)
    take = take_from(refs)
    small, source = take(BACK_SMALL), take(BACK_IN)
    token_out, outs = refs.pop(0), take(BACK_OUTS)
    held = take(BACK_HELD)
    token_buf, sems = refs

    @pl.when(active(where_ref, rows))
    def _():
        flow = Flow(held, sems)
        for name in (Y, W_DOWN, GP, W_UP, X1, A, W_OUT, QKV, P, W_IN, XS):
            flow.fetch(name, source[name].at[0] if name in WEIGHTS else source[name])

        def done(name):
            if name in outs:
                flow.put(held[name], outs[name])

        backward_part(
            rows,
            sort_rows(small[MASK], rows),
            where_ref,
            small,
            held,
            flow.wait,
            done,
            token_buf,
            None,
        )
        flow.put(token_buf, token_out.at[0])
        flow.finish()


def back_block(rows, where, small, weights, saved):
    width, hidden = weights[2].shape[1:]
    shapes = kept_shapes(rows, width, hidden)
    shape = small[COT].shape[1:]
    values = {**saved, **dict(zip(WEIGHTS, weights))}
    operands = [where] + [small[name] for name in BACK_SMALL]
    operands += [values[name] for name in BACK_IN]
    results = big_call(
        functools.partial(back_kernel, rows),
        operands,
        [SMEM] + [VMEM] * len(BACK_SMALL) + [ANY] * len(BACK_IN),
        [jax.ShapeDtypeStruct((1,) + shape, f32)]
        + shaped(shapes, BACK_OUTS, jax.ShapeDtypeStruct),
        shaped(shapes, BACK_HELD, pltpu.VMEM)
        + [pltpu.VMEM(shape, f32), pltpu.SemaphoreType.DMA((32,))],
        "back_block",
        2000,
    )
    return results[0], dict(zip(BACK_OUTS, results[1:]))


class Order:
    def __init__(self, where):
        self.where = where
        self.last = None

    def call(self, kernel, rows, ins, outs, name, scratch=()):
        def body(where_ref, *refs):
            refs = list(refs)
            if extra:
                del refs[len(ins)]

            @pl.when(active(where_ref, rows))
            def _():
                kernel(where_ref, *refs)

        extra = [] if self.last is None else [self.last]
        results = pl.pallas_call(
            body,
            out_shape=outs,
            in_specs=[SMEM] + [VMEM] * len(ins) + [ANY] * len(extra),
            out_specs=[VMEM] * len(outs),
            scratch_shapes=list(scratch),
            compiler_params=pltpu.CompilerParams(vmem_limit_bytes=30 * MIB),
            cost_estimate=cost(30, 3000),
            name=name,
        )(self.where, *ins, *extra)
        self.last = results[-1]
        return results

    def gate(self, value):
        def body(value_ref, last_ref, out_ref):
            pass

        self.last = pl.pallas_call(
            body,
            out_shape=jax.ShapeDtypeStruct(value.shape, value.dtype),
            in_specs=[ANY] * 2,
            out_specs=ANY,
            input_output_aliases={0: 0},
            cost_estimate=cost(30, 3000),
            name="gate",
        )(value, self.last)
        return self.last


def vec_rows(vec_ref, d, lean):
    width = vec_ref.shape[1]
    long = 4 * lean
    at = long * d % width
    row = 10 + long * d // width
    block = jnp.zeros((16, width), f32)
    first = jnp.concatenate(
        [vec_ref[0:10, d * lean : (d + 1) * lean], jnp.zeros((10, width - lean), f32)], axis=1
    )
    second = jnp.concatenate(
        [vec_ref[row : row + 1, at : at + long], jnp.zeros((1, width - long), f32)], axis=1
    )
    return jnp.concatenate([first, second, block[11:]], axis=0)


def in_kernel(where_ref, dqkv_ref, h1_ref, da_ref, o_ref, vec_ref, *refs):
    keep_x, send_x, keep_y, send_y, buf = refs
    width = h1_ref.shape[1]
    lean, tall = width // 16, dqkv_ref.shape[1] // 16
    tile = dot_tn(da_ref[...], o_ref[...]).astype(bf16)
    for d in range(16):
        buf[d, :lean] = tile[d * lean : (d + 1) * lean]
    half = dqkv_ref.shape[1] // 2
    for step in range(2):
        tile = dot_tn(dqkv_ref[:, step * half : (step + 1) * half], h1_ref[...]).astype(bf16)
        for d in range(8):
            buf[8 * step + d, lean : lean + tall] = tile[d * tall : (d + 1) * tall]
    for d in range(16):
        buf[d, lean + tall :] = vec_rows(vec_ref, d, lean).astype(bf16)
    cut = keep_x.shape[1]
    x, y = bit_of(where_ref, 0), bit_of(where_ref, 1)
    for slot in range(8):
        z, other = slot >> 1, slot & 1
        keep_x[slot] = buf[2 * slot + x, :cut]
        send_x[slot] = buf[2 * slot + 1 - x, :cut]
        keep_y[slot] = buf[4 * z + other + 2 * y, cut:]
        send_y[slot] = buf[4 * z + other + 2 * (1 - y), cut:]


def in_back(order, rows, state):
    operands = [state[name] for name in (DQKV, H1, DA, O, VEC)]
    width = operands[1].shape[1]
    height, cut = width // 4 + 16, width // 8
    outs = [jax.ShapeDtypeStruct((8, size, width), bf16) for size in (cut, height - cut)]
    return order.call(
        in_kernel,
        rows,
        operands,
        [outs[0], outs[0], outs[1], outs[1]],
        "in_grad",
        [pltpu.VMEM((16, height, width), bf16)],
    )


def in_first_kernel(where_ref, own_ref, ho_ref, got_ref, got_ho_ref, vec_ref, keep, send, buf, sums):
    queries, width = own_ref.shape[0], vec_ref.shape[1]
    lean, tall = width // 16, 3 * width // 16
    edge = 8 * tall
    for lanes, part, height, at in (
        (slice(0, edge), slice(0, width), tall, lean),
        (slice(edge, 2 * width), slice(width, 2 * width), lean, 0),
    ):
        tile = dot_tn(own_ref[:, lanes], ho_ref[:, part])
        tile = tile + dot_tn(got_ref[:queries, lanes], got_ho_ref[:, part])
        tile = tile.astype(bf16)
        for d in range(8):
            buf[d, at : at + height] = tile[d * height : (d + 1) * height]
    sums[...] = vec_ref[...] + got_ref[queries:, :width].astype(f32)
    low = bit_of(where_ref, 1) == 0
    for d in range(8):
        first = 4 * (d >> 1) + (d & 1)
        mine = jnp.where(low, vec_rows(sums, first, lean), vec_rows(sums, first + 2, lean))
        buf[d, lean + tall :] = mine.astype(bf16)
    bit = bit_of(where_ref, 0)
    for z in range(4):
        keep[z] = buf[2 * z + bit]
        send[z] = buf[2 * z + 1 - bit]


def in_first(order, rows, own, ho, got, got_ho, vec):
    width = vec.shape[1]
    shape = (width // 4 + 16, width)
    return order.call(
        in_first_kernel,
        rows,
        [own, ho, got, got_ho, vec],
        [jax.ShapeDtypeStruct((4,) + shape, bf16)] * 2,
        "in_grad",
        [pltpu.VMEM((8,) + shape, bf16), pltpu.VMEM(vec.shape, f32)],
    )


def down_grad_kernel(where_ref, *refs):
    *ins, keep, send, buf = refs
    height, half = buf.shape[1:]
    bit = bit_of(where_ref, 1)
    mine = pl.multiple_of(bit_of(where_ref, 0) * half, half)
    if len(ins) == 4:
        gl, dy, got_gl, got_dy = ins
        own, got_gl, got_dy = dy[...], got_gl[...], got_dy[...]
    else:
        gl, own, got = ins
        own, got_gl, got_dy = own[:, half:], got[:, :half], got[:, half:]
    tile = dot_tn(own, gl[:, pl.ds(mine, half)])
    tile = (tile + dot_tn(got_dy, got_gl)).astype(bf16)
    for d in range(16):
        buf[d] = tile[d * height : (d + 1) * height]
    for z in range(4):
        for x in range(2):
            part = slice(x * height, (x + 1) * height)
            keep[z, part] = buf[4 * z + x + 2 * bit]
            send[z, part] = buf[4 * z + x + 2 * (1 - bit)]


def down_grad(order, rows, ins, width):
    half = ins[0].shape[1] // 2
    shape = (width // 16, half)
    outs = [jax.ShapeDtypeStruct((4, 2 * shape[0], half), bf16)] * 2
    scratch = [pltpu.VMEM((16,) + shape, bf16)]
    return order.call(down_grad_kernel, rows, ins, outs, "down_grad", scratch)


def up_grad_kernel(where_ref, *refs):
    *ins, keep, send, buf = refs
    height = buf.shape[1]
    half = 8 * height
    bit = bit_of(where_ref, 0)
    if len(ins) == 4:
        du, h2, got_du, got_h2 = (ref[...] for ref in ins)
    else:
        du, own, got = ins
        du, h2, got_du, got_h2 = du[...], own[:, half:], got[:, :half], got[:, half:]
    tile = (dot_tn(du, h2) + dot_tn(got_du, got_h2)).astype(bf16)
    for d in range(8):
        buf[d] = tile[d * height : (d + 1) * height]
    for z in range(4):
        keep[z] = buf[2 * z + bit]
        send[z] = buf[2 * z + 1 - bit]


def up_grad(order, rows, ins, width):
    shape = (ins[0].shape[1] // 8, width)
    outs = [jax.ShapeDtypeStruct((4,) + shape, bf16)] * 2
    scratch = [pltpu.VMEM((8,) + shape, bf16)]
    return order.call(up_grad_kernel, rows, ins, outs, "up_grad", scratch)


def swap(value, phase, bit, count):
    pairs = [(phase * count + i, phase * count + (i ^ (1 << bit))) for i in range(count)]
    return lax.ppermute(value, ("section", "dp"), pairs)


def halve_kernel(position, where_ref, *refs):
    *terms, keep, send = refs
    bit = bit_of(where_ref, position)
    at = 0
    for left, right in zip(terms[::2], terms[1::2]):
        part = slice(at, at + left.shape[1])
        at += left.shape[1]
        for slot in range(keep.shape[0]):
            mine, other = 2 * slot + bit, 2 * slot + 1 - bit
            keep[slot, part] = left[mine].astype(f32) + right[mine].astype(f32)
            sent = left[other].astype(f32) + right[other].astype(f32)
            send[slot, part] = sent.astype(bf16)


def halve(order, rows, phase, position, terms, count):
    height = sum(term.shape[1] for term in terms[::2])
    shape = (terms[0].shape[0] // 2, height, terms[0].shape[2])
    keep, send = order.call(
        functools.partial(halve_kernel, position),
        rows,
        terms,
        [jax.ShapeDtypeStruct(shape, f32), jax.ShapeDtypeStruct(shape, bf16)],
        "halve",
    )
    return [keep, swap(send, phase, position, count)]


def both_terms(refs):
    return refs[0][0].astype(f32) + refs[1][0].astype(f32)


def side_kernel(where_ref, left, right, keep, send):
    height = keep.shape[0]
    low = bit_of(where_ref, 0) == 0
    both = both_terms((left, right))
    keep[...] = jnp.where(low, both[:height], both[height:])
    send[...] = jnp.where(low, both[height:], both[:height]).astype(bf16)


def side(order, rows, terms):
    shape = (terms[0].shape[1] // 2, terms[0].shape[2])
    outs = [jax.ShapeDtypeStruct(shape, f32), jax.ShapeDtypeStruct(shape, bf16)]
    return order.call(side_kernel, rows, terms, outs, "side")


def down_end_kernel(where_ref, keep, got, out):
    half = keep.shape[1]
    x = bit_of(where_ref, 0)
    out[0, :, pl.ds(pl.multiple_of(x * half, half), half)] = keep[...]
    out[0, :, other_half(where_ref, half)] = got[...].astype(f32)


def up_end_kernel(where_ref, left, right, out):
    out[0] = both_terms((left, right))


def in_end_kernel(where_ref, left, right, *outs):
    in_out, out_out, gain_out, bias_out, upb_out, downb_out = outs
    both = both_terms((left, right))
    lean, tall = out_out.shape[1], upb_out.shape[1]
    out_out[0] = both[:lean]
    in_out[0] = both[lean:tall]
    gain_out[0] = both[tall : tall + 4, :lean]
    bias_out[:, 0, :] = both[tall + 4 : tall + 9, :lean]
    downb_out[...] = both[tall + 9 : tall + 10, :lean]
    upb_out[...] = both[tall + 10 : tall + 11, :tall]


def end(order, kernel, rows, terms, shapes, name):
    outs = [jax.ShapeDtypeStruct(shape, f32) for shape in shapes]
    return order.call(kernel, rows, terms, outs, name)


def on_device(
    tokens,
    patch_mask,
    cotangent,
    in_weight,
    out_weight,
    up_weight,
    down_weight,
    gains,
    biases,
    up_bias,
    down_bias,
):
    weights = (in_weight, out_weight, up_weight, down_weight, gains, biases, up_bias, down_bias)
    images, patches, width = tokens.shape
    hidden = up_weight.shape[2]
    count = lax.axis_size("dp")
    section = lax.axis_index("section")
    place = lax.axis_index("dp")
    is_first = section == 0
    where = jnp.stack([section, place]).astype(jnp.int32)
    y = (place >> 1) & 1
    small = count == 16
    rows = [Rows(True, images, patches), Rows(False, images, patches)]

    small_args = {
        MASK: patch_mask,
        TOKENS: jnp.swapaxes(tokens, 0, 1),
        LATENT: gains,
        GAINS: gains,
        BIASES: jnp.swapaxes(biases, 0, 1),
        UP_BIAS: up_bias,
        DOWN_BIAS: down_bias,
        COT: jnp.swapaxes(cotangent, 1, 2),
    }
    matrices = weights[:4]
    result, sent, kept_first = first_block(rows[0], where, small_args, matrices)
    small_args[LATENT] = lax.ppermute(sent, "section", [(0, 1)])
    early = ()
    if small:
        early = tuple(
            swap(kept_first[name], 0, bit, count)
            for name, bit in ((GL_SEND, 0), (H2, 1), (HO, 1))
        )
    result, tokens_second, back, state_second = second_block(
        rows[1], where, small_args, matrices, result, rows[0].queries
    )
    returned = lax.ppermute(back, "section", [(1, 0)])

    def first_back(returned, saved):
        return back_block(rows[0], where, {**small_args, RETURNED: returned}, matrices, saved)

    def sums(order, phase):
        layout = rows[phase]
        lean, tall = width // 16, hidden // 16

        def step(position, terms):
            return halve(order, layout, phase, position, terms, count)

        def cross(terms):
            keep, send = side(order, layout, terms)
            return [keep, swap(send, phase, 0, count)]

        def up_end(terms):
            return end(order, up_end_kernel, layout, terms, [(1, tall, width)], "up_end")

        def down_end(terms):
            return end(order, down_end_kernel, layout, terms, [(1, lean, hidden)], "down_end")

        def in_end(terms):
            shapes = [(1, 3 * lean, width), (1, lean, width), (1, 4, lean), (5, 1, lean)]
            shapes += [(1, tall), (1, lean)]
            return end(order, in_end_kernel, layout, terms, shapes, "in_end")

        return step, cross, up_end, down_end, in_end

    if small:

        def first_rest(returned, early, tokens_second, state, saved):
            token_grads, state = first_back(returned, saved)
            got_gl, got_h2, got_ho = early
            got_dy = swap(state[DY], 0, 0, count)
            got_du = swap(state[DU], 0, 1, count)
            order = Order(where)
            order.last = state[VEC]
            got_io = swap(order.gate(state[SEND_IO]), 0, 1, count)
            keep, send = down_grad(
                order, rows[0], [saved[GL], state[DY], got_gl, got_dy], width
            )
            down = [keep, swap(send, 0, 1, count)]
            keep, send = up_grad(
                order, rows[0], [state[KEEP_UP], saved[H2], got_du, got_h2], width
            )
            up = [keep, swap(send, 0, 0, count)]
            keep, send = in_first(
                order, rows[0], state[KEEP_IO], saved[HO], got_io, got_ho, state[VEC]
            )
            rest = [keep, swap(send, 0, 0, count)]

            step, cross, up_end, down_end, in_end = sums(order, 0)
            down = step(2, down)
            up = step(2, up)
            down = step(3, down)
            rest = step(2, rest)
            up = step(3, up)
            down = cross(down)
            rest = step(3, rest)
            up = up_end(up)
            down = down_end(down)
            rest = in_end(rest)
            return token_grads, *rest[:2], *up, *down, *rest[2:]

        def second_rest(returned, early, tokens_second, state, saved):
            got_up = swap(state[SEND_UP], 1, 1, count)
            got_down = swap(state[SEND_DOWN], 1, 0, count)
            order = Order(where)
            keep, send = up_grad(
                order, rows[1], [state[KEEP_UP], state[SEND_UP], got_up], width
            )
            up = [keep, swap(send, 1, 0, count)]
            keep, send = down_grad(
                order, rows[1], [state[GL], state[SEND_DOWN], got_down], width
            )
            down = [keep, swap(send, 1, 1, count)]
            step, cross, up_end, down_end, in_end = sums(order, 1)
            up = step(2, up)
            down = step(2, down)
            keep_x, send_x, keep_y, send_y = in_back(order, rows[1], state)
            upper = [keep_x, swap(send_x, 1, 0, count)]
            lower = [keep_y, swap(send_y, 1, 1, count)]
            up = step(3, up)
            down = step(3, down)
            upper = step(1, upper)
            lower = step(0, lower)
            down = cross(down)
            up = up_end(up)
            rest = step(2, upper + lower)
            down = down_end(down)
            rest = in_end(step(3, rest))
            return tokens_second, *rest[:2], *up, *down, *rest[2:]

        done = lax.cond(
            is_first,
            first_rest,
            second_rest,
            returned,
            early,
            tokens_second,
            state_second,
            kept_first,
        )
        return (
            jnp.swapaxes(result, 1, 2),
            *(jnp.swapaxes(values, 1, 2) for values in done[:5]),
            done[5],
            jnp.swapaxes(done[6], 0, 1),
            *done[7:],
        )

    tokens_first, state_first = first_back(returned, kept_first)
    half = hidden // 2

    def merged(keep, send):
        parts = [keep.reshape(-1, 4, half // 4), send.reshape(-1, 4, half // 4)]
        both = jnp.where(y == 0, jnp.stack(parts, axis=2), jnp.stack(parts[::-1], axis=2))
        return both.reshape(-1, hidden)

    io = []
    for at, size in ((0, 3 * width), (3 * width // 2, width)):
        keep = state_first[KEEP_IO][:, at : at + size // 2].reshape(-1, 4, size // 8)
        send = state_first[SEND_IO][: keep.shape[0], at : at + size // 2]
        parts = [keep, send.reshape(-1, 4, size // 8)]
        both = jnp.where(y == 0, jnp.stack(parts, axis=2), jnp.stack(parts[::-1], axis=2))
        io.append(both.reshape(-1, size))
    ho = kept_first[HO]
    first = [
        (io[0], ho[:, :width]),
        (io[1], ho[:, width:]),
        (merged(state_first[KEEP_UP], state_first[DU]), kept_first[H2]),
        (state_first[DY], kept_first[GL]),
    ]
    send = state_second[SEND_UP]
    second = [
        (state_second[DQKV], state_second[H1]),
        (state_second[DA], state_second[O]),
        (merged(state_second[KEEP_UP], send[:, :half]), send[:, half:]),
        (state_second[SEND_DOWN][:, half:], state_second[GL]),
    ]
    grads = [
        [tokens_second, state_second[VEC], *(dot_tn(*pair) for pair in second)],
        [tokens_first, state_first[VEC], *(dot_tn(*pair) for pair in first)],
    ]
    token_grads, vec, *finals = [
        jnp.where(is_first, left, right) for left, right in zip(grads[1], grads[0])
    ]
    finals = [lax.psum_scatter(f, "dp", scatter_dimension=0, tiled=True) for f in finals]
    vec = lax.psum(vec, "dp")
    lean, tall = width // count, hidden // count
    up_vec = vec[10:14].reshape(1, hidden)
    vec = lax.dynamic_slice_in_dim(vec, place * lean, lean, 1)
    up_vec = lax.dynamic_slice_in_dim(up_vec, place * tall, tall, 1)
    return (
        jnp.swapaxes(result, 1, 2),
        jnp.swapaxes(token_grads, 1, 2),
        *(final.T[None] for final in finals),
        vec[0:4][None],
        vec[4:9][None],
        up_vec,
        vec[9:10],
    )


def solution(mesh):
    return jax.shard_map(
        on_device,
        mesh=mesh,
        in_specs=(
            PartitionSpec("dp", None, None),
            PartitionSpec("dp", None),
            PartitionSpec("section", "dp", None, None),
            PartitionSpec("section", None, None),
            PartitionSpec("section", None, None),
            PartitionSpec("section", None, None),
            PartitionSpec("section", None, None),
            PartitionSpec("section", None, None),
            PartitionSpec("section", None, None),
            PartitionSpec("section", None),
            PartitionSpec("section", None),
        ),
        out_specs=(
            PartitionSpec("section", "dp", None, None),
            PartitionSpec("section", "dp", None, None),
            PartitionSpec("section", None, "dp"),
            PartitionSpec("section", None, "dp"),
            PartitionSpec("section", None, "dp"),
            PartitionSpec("section", None, "dp"),
            PartitionSpec("section", None, "dp"),
            PartitionSpec("section", None, "dp"),
            PartitionSpec("section", "dp"),
            PartitionSpec("section", "dp"),
        ),
        check_vma=False,
    )
```

```python
import functools

import jax
import jax.numpy as jnp
from jax import lax
from jax.experimental import pallas as pl
from jax.experimental.pallas import tpu as pltpu
from jax.sharding import PartitionSpec

HEADS = 12
HEAD_DIM = 64
PAIRS = HEADS // 2
LANES = 2 * HEAD_DIM
MASK_LO = 59
MASK_HI = 117
TILE = 768

(
    W_IN,
    W_OUT,
    W_UP,
    W_DOWN,
    XS,
    H1,
    QKV,
    P,
    O,
    A,
    X1,
    H2,
    GP,
    GL,
    Y,
    SEND_DOWN,
    KEEP_UP,
    SEND_UP,
    GL_SEND,
    HO,
    KEEP_IO,
    SEND_IO,
    DA,
    DQKV,
    DY,
    DU,
    DO,
    VEC,
    MASK,
    TOKENS,
    LATENT,
    GAINS,
    BIASES,
    UP_BIAS,
    DOWN_BIAS,
    COT,
    RETURNED,
    SEND_DU,
) = range(38)

UNROLL = 6
UNROLL_BACK = 6
MIB = 2**20

epsilon = 1e-06
f32 = jnp.float32
bf16 = jnp.bfloat16
ANY = pl.BlockSpec(memory_space=pl.ANY)
SMEM = pl.BlockSpec(memory_space=pltpu.SMEM)
VMEM = pl.BlockSpec(memory_space=pltpu.VMEM)


def cost(micros, memory=None):
    size = int((memory or micros) * 3.69e6)
    return pl.CostEstimate(flops=int(micros * 1.15e9), bytes_accessed=size, transcendentals=0)


def up16(count):
    return -(-count // 16) * 16


class Rows:
    def __init__(self, first, images, patches):
        most = patches - MASK_LO if first else MASK_HI
        self.first = first
        self.images = images
        self.patches = patches
        self.top = up16(most)
        self.rest = 0 if first else up16(patches - self.top)
        self.keys = self.top + self.rest
        self.queries = images * self.top
        self.total = images * self.keys


def dot(left, right):
    return jnp.dot(left, right, preferred_element_type=f32)


def dot_nt(left, right):
    return lax.dot_general(left, right, (((1,), (1,)), ((), ())), preferred_element_type=f32)


def dot_tn(left, right):
    return lax.dot_general(left, right, (((0,), (0,)), ((), ())), preferred_element_type=f32)


def iota(shape, dim):
    return lax.broadcasted_iota(jnp.int32, shape, dim)


def sort_rows(mask_ref, rows):
    masked = mask_ref[...].astype(f32)
    flag = 1.0 - masked if rows.first else masked
    n = rows.patches
    tri = jnp.where(iota((n, n), 0) <= iota((n, n), 1), 1.0, 0.0).astype(bf16)
    upto = dot(flag.astype(bf16), tri)
    count = jnp.sum(flag, axis=1, keepdims=True)
    at = iota(flag.shape, 1).astype(f32)
    place = jnp.where(flag > 0, upto - 1.0, count + at - upto)
    return flag, place, count


def pick(place, image, start, length):
    slots = iota((length, place.shape[1]), 0).astype(f32) + float(start)
    return jnp.where(slots == place[image : image + 1, :], 1.0, 0.0)


def valid_rows(count, rows):
    parts = [
        jnp.where(iota((rows.top, 1), 0).astype(f32) < count[b : b + 1, :], 1.0, 0.0)
        for b in range(rows.images)
    ]
    return jnp.concatenate(parts, axis=0)


def normed(states):
    centre = states - jnp.mean(states, axis=-1, keepdims=True)
    spread = jnp.mean(centre * centre, axis=-1, keepdims=True)
    scale = lax.rsqrt(spread + epsilon)
    return centre * scale, scale


def norm_back(grad, unit, scale, gain):
    inner = grad * gain
    along = jnp.mean(inner * unit, axis=-1, keepdims=True)
    return scale * (inner - jnp.mean(inner, axis=-1, keepdims=True) - unit * along)


def gelu_parts(values):
    size = jnp.abs(values) * (0.5**0.5)
    t = 1.0 / (1.0 + 0.3275911 * size)
    series = t * (
        0.254829592
        + t * (-0.284496736 + t * (1.421413741 + t * (-1.453152027 + t * 1.061405429)))
    )
    decay = jnp.exp(-0.5 * values * values)
    upper = 0.5 * series * decay
    below = jnp.where(values < 0, upper, 1.0 - upper)
    return below, decay * 0.3989422804014327


def total(values):
    return jnp.sum(values, axis=0, keepdims=True)


def key_rows(ref, image, lanes, rows):
    block = ref[image * rows.top : (image + 1) * rows.top, lanes]
    if rows.rest == 0:
        return block
    start = rows.queries + image * rows.rest
    return jnp.concatenate([block, ref[start : start + rows.rest, lanes]], axis=0)


class Copies:
    def __init__(self, sems):
        self.sems = sems
        self.used = 0

    def start(self, source, target):
        copy = pltpu.make_async_copy(source, target, self.sems.at[self.used])
        self.used += 1
        copy.start()
        return copy


SAVED = (XS, H1, QKV, P, O, A, X1, H2, GP, GL, Y)
WEIGHTS = (W_IN, W_OUT, W_UP, W_DOWN)


def kept_shapes(rows, width, hidden):
    queries = rows.queries
    return {
        W_IN: ((width, 3 * width), bf16),
        W_OUT: ((width, width), bf16),
        W_UP: ((width, hidden), bf16),
        W_DOWN: ((hidden, width), bf16),
        XS: ((rows.total, width), bf16),
        H1: ((rows.total, width), bf16),
        QKV: ((rows.total, 3 * width), bf16),
        P: ((rows.images * PAIRS, 2 * rows.top, rows.keys), bf16),
        O: ((queries, width), bf16),
        A: ((queries, width), bf16),
        X1: ((queries, width), f32),
        H2: ((queries, width), bf16),
        GP: ((queries, hidden), bf16),
        GL: ((queries, hidden), bf16),
        Y: ((queries, width), bf16),
        SEND_DOWN: ((queries, hidden // 2 + width), bf16),
        KEEP_UP: ((queries, hidden // 2), bf16),
        SEND_UP: ((queries, hidden // 2 + width), bf16),
        GL_SEND: ((queries, hidden // 2), bf16),
        HO: ((queries, 2 * width), bf16),
        KEEP_IO: ((queries, 2 * width), bf16),
        SEND_IO: ((queries + 16, 2 * width), bf16),
        DA: ((queries, width), bf16),
        DQKV: ((rows.total, 3 * width), bf16),
        DY: ((queries, width), bf16),
        DU: ((queries, hidden), bf16),
        SEND_DU: ((queries, hidden // 2), bf16),
        DO: ((queries, width), bf16),
        VEC: ((16, width), f32),
    }


def bit_of(where_ref, order):
    return (where_ref[1] >> order) & 1


def active(where_ref, rows):
    return where_ref[0] == (0 if rows.first else 1)


def lane_sides():
    lane = iota((1, LANES), 1)
    sides = [(lane < HEAD_DIM), (lane >= HEAD_DIM)]
    return sides, [jnp.where(side, 1.0, 0.0).astype(bf16) for side in sides]


def two_heads(values, masks):
    return jnp.concatenate([values * masks[0], values * masks[1]], axis=0)


def mover(count, rows, image, start, length, height):
    behind = iota((length, height), 0) - iota((length, height), 1)
    behind = behind.astype(f32) + float(start) == count[image : image + 1, :]
    seen = iota((length, height), 1).astype(f32) < rows.patches - count[image : image + 1, :]
    return jnp.where(behind & seen, 1.0, 0.0).astype(bf16)


def forward_part(rows, order, small, held, wait, done):
    tok_ref, lat_ref = small[TOKENS], small[LATENT]
    gains_ref, biases_ref = small[GAINS], small[BIASES]
    flag, place, count = order
    images, top, queries = rows.images, rows.top, rows.queries
    width = held[W_OUT].shape[0]
    scale = HEAD_DIM**-0.5

    def states_of(b, start, length):
        chosen = pick(place, b, start, length)
        if rows.first:
            return dot(chosen.astype(bf16), tok_ref[:, b, :])
        from_tokens = dot((chosen * flag[b : b + 1, :]).astype(bf16), tok_ref[:, b, :])
        height = lat_ref.shape[0] // images
        move = mover(count, rows, b, start, length, height)
        return from_tokens + dot(move, lat_ref[b * height : (b + 1) * height])

    pieces = [states_of(b, 0, top) for b in range(images)]
    if rows.rest:
        pieces += [states_of(b, top, rows.rest) for b in range(images)]
    states = jnp.concatenate(pieces, axis=0)
    held[XS][...] = states.astype(bf16)
    done(XS)
    unit, _ = normed(states)
    h1 = (unit * gains_ref[0, 0:1, :] + biases_ref[0]).astype(bf16)
    held[H1][...] = h1
    done(H1)
    qkv = held[QKV]
    wi = held[W_IN]
    wait(W_IN)
    qkv[0:queries, 0:width] = (dot(h1[:queries], wi[:, :width]) + biases_ref[1]).astype(bf16)
    if rows.rest:
        qkv[queries:, 0:width] = jnp.zeros((rows.total - queries, width), bf16)
    qkv[:, width : 2 * width] = dot(h1, wi[:, width : 2 * width]).astype(bf16)
    qkv[:, 2 * width :] = (dot(h1, wi[:, 2 * width :]) + biases_ref[2]).astype(bf16)
    done(QKV)
    sides, masks = lane_sides()

    @pl.loop(0, PAIRS, unroll=UNROLL)
    def _(pair):
        lo = pl.multiple_of(pair * LANES, LANES)
        for b in range(images):
            q = qkv[b * top : (b + 1) * top, pl.ds(lo, LANES)]
            k = key_rows(qkv, b, pl.ds(width + lo, LANES), rows)
            v = key_rows(qkv, b, pl.ds(2 * width + lo, LANES), rows)
            at = iota((1, rows.keys), 1).astype(f32)
            if rows.first:
                usable = at < count[b : b + 1, :]
            else:
                usable = at < float(rows.patches)
            raw = dot_nt(two_heads(q, masks), k)
            logits = jnp.where(usable, raw * scale, -1e30)
            grown = jnp.exp(logits - jnp.max(logits, axis=-1, keepdims=True))
            p = (grown * (1.0 / jnp.sum(grown, axis=-1, keepdims=True))).astype(bf16)
            held[P][b * PAIRS + pair] = p
            mixed = dot(p, v)
            held[O][b * top : (b + 1) * top, pl.ds(lo, LANES)] = jnp.where(
                sides[0], mixed[:top], mixed[top:]
            ).astype(bf16)

    done(P)
    done(O)
    wait(W_OUT)
    a = dot(held[O][...], held[W_OUT][...]) + biases_ref[3]
    held[A][...] = a.astype(bf16)
    done(A)
    usable_rows = valid_rows(count, rows)
    x1 = states[:queries] + gains_ref[0, 1:2, :] * a * usable_rows
    held[X1][...] = x1
    done(X1)
    unit, _ = normed(x1)
    h2 = (unit * gains_ref[0, 2:3, :] + biases_ref[4]).astype(bf16)
    held[H2][...] = h2
    done(H2)
    wait(W_UP)
    y = jnp.zeros((queries, width), f32)
    for start in range(0, held[W_UP].shape[1], TILE):
        cols = slice(start, start + TILE)
        u = dot(h2, held[W_UP][:, cols]) + small[UP_BIAS][:, cols]
        below, density = gelu_parts(u)
        gl = (u * below).astype(bf16)
        held[GL][:, cols] = gl
        held[GP][:, cols] = (below + u * density).astype(bf16)
        done(GL, cols)
        done(GP, cols)
        wait(W_DOWN)
        y = y + dot(gl, held[W_DOWN][cols, :])
    done(GL_SEND)
    y = y + small[DOWN_BIAS][...]
    held[Y][...] = y.astype(bf16)
    done(Y)
    return (x1 + gains_ref[0, 3:4, :] * y * usable_rows).astype(bf16)


def backward_part(rows, order, where_ref, small, held, wait, done, dx_ref, ret_buf):
    cot_ref, gains_ref = small[COT], small[GAINS]
    flag, place, count = order
    images, top, queries = rows.images, rows.top, rows.queries
    hidden, width = held[W_DOWN].shape
    scale = HEAD_DIM**-0.5
    usable_rows = valid_rows(count, rows)
    vec = held[VEC]
    vec[...] = jnp.zeros(vec.shape, f32)
    pieces = []
    for b in range(images):
        chosen = (pick(place, b, 0, top) * flag[b : b + 1, :]).astype(bf16)
        piece = dot(chosen, cot_ref[0, :, b, :])
        if rows.first:
            piece = piece + small[RETURNED][b * top : (b + 1) * top].astype(f32)
        pieces.append(piece)
    grad = jnp.concatenate(pieces, axis=0)
    dy = (grad * gains_ref[0, 3:4, :] * usable_rows).astype(bf16)
    held[DY][...] = dy
    done(DY)
    wait(Y)
    vec[3:4, :] = total(grad * held[Y][...].astype(f32))
    vec[9:10, :] = total(dy.astype(f32))

    low_first = bit_of(where_ref, 0) == 0
    wait(W_DOWN)
    wait(GP)
    for step in range(hidden // TILE):
        cols = slice(step * TILE, (step + 1) * TILE)
        dgl = dot_nt(dy, held[W_DOWN][cols, :])
        du = (dgl * held[GP][:, cols].astype(f32)).astype(bf16)
        vec[10 + step : 11 + step, :] = total(du.astype(f32))
        held[DU][:, cols] = du
    done(DU)
    wait(W_UP)
    dh2 = dot_nt(held[DU][...], held[W_UP][...])

    wait(X1)
    unit, spread = normed(held[X1][...])
    vec[2:3, :] = total(dh2 * unit)
    vec[8:9, :] = total(dh2)
    dx1 = grad + norm_back(dh2, unit, spread, gains_ref[0, 2:3, :])
    da = (dx1 * gains_ref[0, 1:2, :] * usable_rows).astype(bf16)
    wait(A)
    vec[1:2, :] = total(dx1 * held[A][...].astype(f32) * usable_rows)
    vec[7:8, :] = total(da.astype(f32))
    held[DA][...] = da
    done(DA)
    do_ref = held[DO]
    wait(W_OUT)
    do_ref[...] = dot_nt(da, held[W_OUT][...]).astype(bf16)
    qkv, dqkv = held[QKV], held[DQKV]
    sides, masks = lane_sides()
    if rows.rest:
        dqkv[queries:, 0:width] = jnp.zeros((rows.total - queries, width), bf16)
    wait(QKV)
    wait(P)

    @pl.loop(0, PAIRS, unroll=UNROLL_BACK)
    def _(pair):
        lo = pl.multiple_of(pair * LANES, LANES)
        for b in range(images):
            q = qkv[b * top : (b + 1) * top, pl.ds(lo, LANES)]
            k = key_rows(qkv, b, pl.ds(width + lo, LANES), rows)
            v = key_rows(qkv, b, pl.ds(2 * width + lo, LANES), rows)
            do = two_heads(do_ref[b * top : (b + 1) * top, pl.ds(lo, LANES)], masks)
            p = held[P][b * PAIRS + pair]
            wide = p.astype(f32)
            dp = dot_nt(do, v)
            inner = jnp.sum(wide * dp, axis=-1, keepdims=True)
            draw = (wide * (dp - inner) * scale).astype(bf16)
            mixed = dot(draw, k)
            dq = jnp.where(sides[0], mixed[:top], mixed[top:])
            dk = dot_tn(draw, two_heads(q, masks))
            dv = dot_tn(p, do)
            for at, part in enumerate((dq, dk, dv)):
                part = part.astype(bf16)
                lanes = pl.ds(at * width + lo, LANES)
                dqkv[b * top : (b + 1) * top, lanes] = part[:top]
                if rows.rest and at > 0:
                    start = queries + b * rows.rest
                    dqkv[start : start + rows.rest, lanes] = part[top:]

    done(DQKV)
    if rows.first:
        at = 0
        for values in (dqkv, held[DA]):
            size = values.shape[1] // 16
            for own in range(2):
                picked = [values[:, j * size : (j + 1) * size] for j in range(own, 16, 2)]
                lanes = slice(at, at + 8 * size)
                picked = jnp.concatenate(picked, axis=1)
                keep = held[KEEP_IO]
                if own == 0:
                    keep[:, lanes] = picked
                else:
                    even = keep[:, lanes]
                    keep[:, lanes] = jnp.where(low_first, even, picked)
                    held[SEND_IO][:queries, lanes] = jnp.where(low_first, picked, even)
            at += 8 * size
        done(KEEP_IO)
    wait(W_IN)
    dh1 = jnp.zeros((rows.total, width), f32)
    for at in range(3):
        cols = slice(at * width, (at + 1) * width)
        dh1 = dh1 + dot_nt(dqkv[:, cols], held[W_IN][:, cols])
    wait(XS)
    unit, spread = normed(held[XS][...].astype(f32))
    dx = norm_back(dh1, unit, spread, gains_ref[0, 0:1, :])
    if rows.rest:
        rest = dx[queries:].astype(bf16)
    dx = dx[:queries] + dx1
    dx_ref[...] = dx
    if not rows.first:
        high = dx.astype(bf16)
        for b in range(images):
            height = ret_buf.shape[0] // images
            move = mover(count, rows, b, 0, rows.keys, height)
            part = slice(b * top, (b + 1) * top)
            tail = slice(b * rows.rest, (b + 1) * rows.rest)
            back = dot_tn(move[:top], high[part]) + dot_tn(move[top:], rest[tail])
            ret_buf[b * height : (b + 1) * height] = back.astype(bf16)
    vec[0:1, :] = total(dh1 * unit)
    vec[4:5, :] = total(dh1)
    vec[5:6, :] = total(dqkv[:, 0:width].astype(f32))
    vec[6:7, :] = total(dqkv[:, 2 * width :].astype(f32))
    done(VEC)
    if rows.first:
        held[SEND_IO][queries:, :width] = vec[...].astype(bf16)
        held[SEND_IO][queries:, width:] = jnp.zeros((16, width), bf16)
        done(SEND_IO)


class Flow:
    def __init__(self, held, sems, source):
        self.held = held
        self.source = source
        self.copies = Copies(sems)
        self.gets = {}
        self.later = {}
        self.puts = []

    def fetch(self, *names, after=None):
        if after is not None:
            self.later[after] = names
            return
        for name in names:
            ref = self.source[name]
            ref = ref.at[0] if name in WEIGHTS else ref
            self.gets[name] = self.copies.start(ref, self.held[name])

    def wait(self, name):
        if name in self.gets:
            self.gets.pop(name).wait()
            self.fetch(*self.later.pop(name, ()))

    def put(self, source, target):
        self.puts.append(self.copies.start(source, target))

    def finish(self):
        while self.gets:
            self.wait(next(iter(self.gets)))
        for copy in self.puts:
            copy.wait()


FORWARD_SMALL = (MASK, TOKENS, LATENT, GAINS, BIASES, UP_BIAS, DOWN_BIAS)
SECOND_SMALL = FORWARD_SMALL + (COT,)
BACK_SMALL = (MASK, COT, RETURNED, GAINS)
FIRST_HELD = WEIGHTS + SAVED
FIRST_OUTS = (XS, QKV, P, A, X1, H2, GP, GL, Y, GL_SEND, HO)
SECOND_HELD = WEIGHTS + SAVED + (DA, DQKV, DY, DU, DO)
SECOND_OUTS = (H1, O, GL, SEND_DOWN, KEEP_UP, SEND_UP, DA, DQKV)
BACK_IN = WEIGHTS + (XS, QKV, P, A, X1, GP, Y)
BACK_OUTS = (DY, KEEP_UP, SEND_DU, KEEP_IO)
BACK_HELD = BACK_IN + (DA, DQKV, DO, DY, DU, KEEP_IO)


def take_from(refs):
    def take(names):
        taken = dict(zip(names, refs))
        del refs[: len(names)]
        return taken

    return take


def part_du(flow, where_ref, keep, send):
    du = flow.held[DU]
    size = du.shape[1] // 8
    bit = bit_of(where_ref, 1)
    for target, own in ((keep, bit), (send, 1 - bit)):
        for z in range(4):
            start = pl.multiple_of((2 * z + own) * size, size)
            flow.put(du.at[:, pl.ds(start, size)], target.at[:, pl.ds(z * size, size)])


def other_half(where_ref, half):
    return pl.ds(pl.multiple_of((1 - bit_of(where_ref, 0)) * half, half), half)


def first_kernel(rows, where_ref, *refs):
    refs = list(refs)
    take = take_from(refs)
    small, weights = take(FORWARD_SMALL), take(WEIGHTS)
    x2_out, outs = refs.pop(0), take(FIRST_OUTS)
    held = take(FIRST_HELD)
    (sems,) = refs

    @pl.when(active(where_ref, rows))
    def _():
        flow = Flow(held, sems, weights)
        flow.fetch(W_IN, W_OUT)
        flow.fetch(W_UP, W_DOWN, after=W_IN)
        order = sort_rows(small[MASK], rows)
        width = held[O].shape[1]

        def done(name, cols=None):
            if cols is not None:
                flow.put(held[name].at[:, cols], outs[name].at[:, cols])
            elif name in (H1, O):
                start = 0 if name == H1 else width
                flow.put(held[name], outs[HO].at[:, pl.ds(start, width)])
            elif name == GL_SEND:
                half = held[GL].shape[1] // 2
                flow.put(held[GL].at[:, other_half(where_ref, half)], outs[GL_SEND])
            else:
                flow.put(held[name], outs[name])

        x2_out[...] = forward_part(rows, order, small, held, flow.wait, done)
        flow.finish()


def big_call(kernel, operands, in_specs, direct, outs, scratch, name, micros):
    return pl.pallas_call(
        kernel,
        out_shape=direct + outs,
        in_specs=in_specs,
        out_specs=[VMEM] * len(direct) + [ANY] * len(outs),
        scratch_shapes=scratch,
        compiler_params=pltpu.CompilerParams(vmem_limit_bytes=56 * MIB),
        cost_estimate=cost(micros),
        name=name,
    )(*operands)


def shaped(shapes, names, make):
    return [make(*shapes[name]) for name in names]


def first_block(rows, where, small, weights):
    width, hidden = weights[2].shape[1:]
    shapes = kept_shapes(rows, width, hidden)
    results = big_call(
        functools.partial(first_kernel, rows),
        [where] + [small[name] for name in FORWARD_SMALL] + list(weights),
        [SMEM] + [VMEM] * len(FORWARD_SMALL) + [ANY] * 4,
        [jax.ShapeDtypeStruct((rows.queries, width), bf16)],
        shaped(shapes, FIRST_OUTS, jax.ShapeDtypeStruct),
        shaped(shapes, FIRST_HELD, pltpu.VMEM) + [pltpu.SemaphoreType.DMA((48,))],
        "first_block",
        1500,
    )
    return results[0], dict(zip(FIRST_OUTS, results[1:]))


def second_kernel(rows, where_ref, *refs):
    refs = list(refs)
    take = take_from(refs)
    small, weights = take(SECOND_SMALL), take(WEIGHTS)
    ret_out, dx_out, x2_out, vec_out = (refs.pop(0) for _ in range(4))
    outs = take(SECOND_OUTS)
    held = take(SECOND_HELD)
    held[VEC] = vec_out
    (sems,) = refs

    @pl.when(active(where_ref, rows))
    def _():
        flow = Flow(held, sems, weights)
        flow.fetch(W_IN, W_OUT)
        flow.fetch(W_UP, W_DOWN, after=W_IN)
        order = sort_rows(small[MASK], rows)
        half = held[DU].shape[1] // 2
        width = held[DY].shape[1]

        def done(name, cols=None):
            if cols is not None:
                if name in outs:
                    flow.put(held[name].at[:, cols], outs[name].at[:, cols])
            elif name == GL_SEND:
                flow.put(
                    held[GL].at[:, other_half(where_ref, half)],
                    outs[SEND_DOWN].at[:, pl.ds(0, half)],
                )
            elif name == H2:
                flow.put(held[H2], outs[SEND_UP].at[:, pl.ds(half, width)])
            elif name == DY:
                flow.put(held[DY], outs[SEND_DOWN].at[:, pl.ds(half, width)])
            elif name == DU:
                part_du(flow, where_ref, outs[KEEP_UP], outs[SEND_UP])
            elif name in outs:
                flow.put(held[name], outs[name])

        x2_out[...] = forward_part(rows, order, small, held, flow.wait, done)
        backward_part(rows, order, where_ref, small, held, flow.wait, done, dx_out, ret_out)
        flow.finish()


def second_block(rows, where, small, weights, back_rows):
    width, hidden = weights[2].shape[1:]
    shapes = kept_shapes(rows, width, hidden)
    results = big_call(
        functools.partial(second_kernel, rows),
        [where] + [small[name] for name in SECOND_SMALL] + list(weights),
        [SMEM] + [VMEM] * len(SECOND_SMALL) + [ANY] * 4,
        [
            jax.ShapeDtypeStruct((back_rows, width), bf16),
            jax.ShapeDtypeStruct((rows.queries, width), f32),
            jax.ShapeDtypeStruct((rows.queries, width), bf16),
            jax.ShapeDtypeStruct((16, width), f32),
        ],
        shaped(shapes, SECOND_OUTS, jax.ShapeDtypeStruct),
        shaped(shapes, SECOND_HELD, pltpu.VMEM) + [pltpu.SemaphoreType.DMA((48,))],
        "second_block",
        3000,
    )
    ret, dx, x2, vec = results[:4]
    return ret, dx, x2, {**dict(zip(SECOND_OUTS, results[4:])), VEC: vec}


def back_kernel(rows, where_ref, *refs):
    refs = list(refs)
    take = take_from(refs)
    small, source = take(BACK_SMALL), take(BACK_IN)
    dx_out, vec_out, send_out = (refs.pop(0) for _ in range(3))
    outs = take(BACK_OUTS)
    held = take(BACK_HELD)
    held[VEC], held[SEND_IO] = vec_out, send_out
    (sems,) = refs

    @pl.when(active(where_ref, rows))
    def _():
        flow = Flow(held, sems, source)
        flow.fetch(Y, W_DOWN, GP)
        flow.fetch(W_UP, X1, after=W_DOWN)
        flow.fetch(A, W_OUT, QKV, P, W_IN, XS, after=W_UP)

        def done(name):
            if name == DU:
                part_du(flow, where_ref, outs[KEEP_UP], outs[SEND_DU])
            elif name in outs:
                flow.put(held[name], outs[name])

        backward_part(
            rows,
            sort_rows(small[MASK], rows),
            where_ref,
            small,
            held,
            flow.wait,
            done,
            dx_out,
            None,
        )
        flow.finish()


def back_block(rows, where, small, weights, saved):
    width, hidden = weights[2].shape[1:]
    shapes = kept_shapes(rows, width, hidden)
    values = {**saved, **dict(zip(WEIGHTS, weights))}
    operands = [where] + [small[name] for name in BACK_SMALL]
    operands += [values[name] for name in BACK_IN]
    results = big_call(
        functools.partial(back_kernel, rows),
        operands,
        [SMEM] + [VMEM] * len(BACK_SMALL) + [ANY] * len(BACK_IN),
        [jax.ShapeDtypeStruct((rows.queries, width), f32)]
        + shaped(shapes, (VEC, SEND_IO), jax.ShapeDtypeStruct),
        shaped(shapes, BACK_OUTS, jax.ShapeDtypeStruct),
        shaped(shapes, BACK_HELD, pltpu.VMEM) + [pltpu.SemaphoreType.DMA((48,))],
        "back_block",
        2000,
    )
    return results[0], {**dict(zip((VEC, SEND_IO) + BACK_OUTS, results[1:]))}


class Order:
    def __init__(self, where):
        self.where = where
        self.last = None

    def call(self, kernel, rows, ins, outs, name, scratch=()):
        def body(where_ref, *refs):
            refs = list(refs)
            if extra:
                del refs[len(ins)]

            @pl.when(active(where_ref, rows))
            def _():
                kernel(where_ref, *refs)

        extra = [] if self.last is None else [self.last]
        results = pl.pallas_call(
            body,
            out_shape=outs,
            in_specs=[SMEM] + [VMEM] * len(ins) + [ANY] * len(extra),
            out_specs=[VMEM] * len(outs),
            scratch_shapes=list(scratch),
            compiler_params=pltpu.CompilerParams(vmem_limit_bytes=30 * MIB),
            cost_estimate=cost(30, 3000),
            name=name,
        )(self.where, *ins, *extra)
        self.last = results[-1]
        return results

    def gate(self, value):
        def body(value_ref, last_ref, out_ref):
            pass

        self.last = pl.pallas_call(
            body,
            out_shape=jax.ShapeDtypeStruct(value.shape, value.dtype),
            in_specs=[ANY] * 2,
            out_specs=ANY,
            input_output_aliases={0: 0},
            cost_estimate=cost(30, 3000),
            name="gate",
        )(value, self.last)
        return self.last


def vec_rows(vec_ref, d, lean):
    width = vec_ref.shape[1]
    long = 4 * lean
    at = long * d % width
    row = 10 + long * d // width
    block = jnp.zeros((16, width), f32)
    first = jnp.concatenate(
        [vec_ref[0:10, d * lean : (d + 1) * lean], jnp.zeros((10, width - lean), f32)], axis=1
    )
    second = jnp.concatenate(
        [vec_ref[row : row + 1, at : at + long], jnp.zeros((1, width - long), f32)], axis=1
    )
    return jnp.concatenate([first, second, block[11:]], axis=0)


def in_kernel(where_ref, dqkv_ref, h1_ref, da_ref, o_ref, vec_ref, *refs):
    keep_z, send_z, keep_y, send_y, buf = refs
    width = h1_ref.shape[1]
    lean, tall = width // 16, dqkv_ref.shape[1] // 16
    tile = dot_tn(da_ref[...], o_ref[...]).astype(bf16)
    for d in range(16):
        buf[d, :lean] = tile[d * lean : (d + 1) * lean]
    half = dqkv_ref.shape[1] // 2
    for step in range(2):
        tile = dot_tn(dqkv_ref[:, step * half : (step + 1) * half], h1_ref[...]).astype(bf16)
        for d in range(8):
            buf[8 * step + d, lean : lean + tall] = tile[d * tall : (d + 1) * tall]
    for d in range(16):
        buf[d, lean + tall :] = vec_rows(vec_ref, d, lean).astype(bf16)
    cut = keep_z.shape[1]
    y, z = bit_of(where_ref, 1), bit_of(where_ref, 2)
    for slot in range(8):
        high, other = slot >> 1, slot & 1
        keep_y[slot] = buf[4 * high + other + 2 * y, cut:]
        send_y[slot] = buf[4 * high + other + 2 * (1 - y), cut:]
        keep_z[slot] = buf[8 * other + high + 4 * z, :cut]
        send_z[slot] = buf[8 * other + high + 4 * (1 - z), :cut]


def in_back(order, rows, state):
    operands = [state[name] for name in (DQKV, H1, DA, O, VEC)]
    width = operands[1].shape[1]
    height, cut = width // 4 + 16, 3 * width // 16
    outs = [jax.ShapeDtypeStruct((8, size, width), bf16) for size in (cut, height - cut)]
    return order.call(
        in_kernel,
        rows,
        operands,
        [outs[0], outs[0], outs[1], outs[1]],
        "in_grad",
        [pltpu.VMEM((16, height, width), bf16)],
    )


def in_first_kernel(where_ref, own_ref, ho_ref, got_ref, got_ho_ref, vec_ref, keep, send, buf, sums):
    queries, width = own_ref.shape[0], vec_ref.shape[1]
    lean, tall = width // 16, 3 * width // 16
    edge = 8 * tall
    for lanes, part, height, at in (
        (slice(0, edge), slice(0, width), tall, lean),
        (slice(edge, 2 * width), slice(width, 2 * width), lean, 0),
    ):
        tile = dot_tn(own_ref[:, lanes], ho_ref[:, part])
        tile = tile + dot_tn(got_ref[:queries, lanes], got_ho_ref[:, part])
        tile = tile.astype(bf16)
        for d in range(8):
            buf[d, at : at + height] = tile[d * height : (d + 1) * height]
    sums[...] = vec_ref[...] + got_ref[queries:, :width].astype(f32)
    low = bit_of(where_ref, 0) == 0
    for d in range(8):
        mine = jnp.where(low, vec_rows(sums, 2 * d, lean), vec_rows(sums, 2 * d + 1, lean))
        buf[d, lean + tall :] = mine.astype(bf16)
    bit = bit_of(where_ref, 1)
    for z in range(4):
        keep[z] = buf[2 * z + bit]
        send[z] = buf[2 * z + 1 - bit]


def in_first(order, rows, own, ho, got, got_ho, vec):
    width = vec.shape[1]
    shape = (width // 4 + 16, width)
    return order.call(
        in_first_kernel,
        rows,
        [own, ho, got, got_ho, vec],
        [jax.ShapeDtypeStruct((4,) + shape, bf16)] * 2,
        "in_grad",
        [pltpu.VMEM((8,) + shape, bf16), pltpu.VMEM(vec.shape, f32)],
    )


def down_grad_kernel(where_ref, *refs):
    *ins, keep, send, buf = refs
    height, half = buf.shape[1:]
    mine = pl.multiple_of(bit_of(where_ref, 0) * half, half)
    if len(ins) == 4:
        gl, dy, got_gl, got_dy = ins
        own, got_gl, got_dy = dy[...], got_gl[...], got_dy[...]
    else:
        gl, own, got = ins
        own, got_gl, got_dy = own[:, half:], got[:, :half], got[:, half:]
    tile = dot_tn(own, gl[:, pl.ds(mine, half)])
    tile = (tile + dot_tn(got_dy, got_gl)).astype(bf16)
    for d in range(16):
        buf[d] = tile[d * height : (d + 1) * height]
    first = len(ins) == 4
    bit = bit_of(where_ref, 1 if first else 2)
    for slot in range(4):
        for x in range(2):
            part = slice(x * height, (x + 1) * height)
            base = 4 * slot if first else 8 * (slot & 1) + (slot & 2)
            step = 2 if first else 4
            keep[slot, part] = buf[base + x + step * bit]
            send[slot, part] = buf[base + x + step * (1 - bit)]


def down_grad(order, rows, ins, width):
    half = ins[0].shape[1] // 2
    shape = (width // 16, half)
    outs = [jax.ShapeDtypeStruct((4, 2 * shape[0], half), bf16)] * 2
    scratch = [pltpu.VMEM((16,) + shape, bf16)]
    return order.call(down_grad_kernel, rows, ins, outs, "down_grad", scratch)


def up_grad_kernel(where_ref, *refs):
    *ins, keep, send, buf = refs
    height = buf.shape[1]
    half = 8 * height
    bit = bit_of(where_ref, 0)
    if len(ins) == 4:
        du, h2, got_du, got_h2 = (ref[...] for ref in ins)
    else:
        du, own, got = ins
        du, h2, got_du, got_h2 = du[...], own[:, half:], got[:, :half], got[:, half:]
    tile = (dot_tn(du, h2) + dot_tn(got_du, got_h2)).astype(bf16)
    for d in range(8):
        buf[d] = tile[d * height : (d + 1) * height]
    for z in range(4):
        keep[z] = buf[2 * z + bit]
        send[z] = buf[2 * z + 1 - bit]


def up_grad(order, rows, ins, width):
    shape = (ins[0].shape[1] // 8, width)
    outs = [jax.ShapeDtypeStruct((4,) + shape, bf16)] * 2
    scratch = [pltpu.VMEM((8,) + shape, bf16)]
    return order.call(up_grad_kernel, rows, ins, outs, "up_grad", scratch)


def swap(value, phase, bit, count):
    pairs = [(phase * count + i, phase * count + (i ^ (1 << bit))) for i in range(count)]
    return lax.ppermute(value, ("section", "dp"), pairs)


def halve_kernel(position, where_ref, *refs):
    *terms, keep, send = refs
    bit = bit_of(where_ref, position)
    at = 0
    for left, right in zip(terms[::2], terms[1::2]):
        part = slice(at, at + left.shape[1])
        at += left.shape[1]
        for slot in range(keep.shape[0]):
            mine, other = 2 * slot + bit, 2 * slot + 1 - bit
            keep[slot, part] = left[mine].astype(f32) + right[mine].astype(f32)
            sent = left[other].astype(f32) + right[other].astype(f32)
            send[slot, part] = sent.astype(bf16)


def halve(order, rows, phase, position, terms, count):
    height = sum(term.shape[1] for term in terms[::2])
    shape = (terms[0].shape[0] // 2, height, terms[0].shape[2])
    keep, send = order.call(
        functools.partial(halve_kernel, position),
        rows,
        terms,
        [jax.ShapeDtypeStruct(shape, f32), jax.ShapeDtypeStruct(shape, bf16)],
        "halve",
    )
    return [keep, swap(send, phase, position, count)]


def unsort_kernel(rows, where_ref, mask_ref, x2_ref, dx_ref, result, grads):
    flag, place, _ = sort_rows(mask_ref, rows)
    for b in range(rows.images):
        part = slice(b * rows.top, (b + 1) * rows.top)
        chosen = (pick(place, b, 0, rows.top) * flag[b : b + 1, :]).astype(bf16)
        dx = dx_ref[part]
        high = dx.astype(bf16)
        low = (dx - high.astype(f32)).astype(bf16)
        result[0, :, b, :] = dot_tn(chosen, x2_ref[part]).astype(bf16)
        grads[0, :, b, :] = dot_tn(chosen, high) + dot_tn(chosen, low)


def unsort(order, rows, mask, x2, dx):
    shape = (1, rows.patches, rows.images, x2.shape[1])
    outs = [jax.ShapeDtypeStruct(shape, kind) for kind in (bf16, f32)]
    return order.call(
        functools.partial(unsort_kernel, rows), rows, [mask, x2, dx], outs, "unsort"
    )


def both_terms(refs):
    return refs[0][0].astype(f32) + refs[1][0].astype(f32)


def side_kernel(where_ref, left, right, keep, send):
    height = keep.shape[0]
    low = bit_of(where_ref, 0) == 0
    both = both_terms((left, right))
    keep[...] = jnp.where(low, both[:height], both[height:])
    send[...] = jnp.where(low, both[height:], both[:height]).astype(bf16)


def side(order, rows, terms):
    shape = (terms[0].shape[1] // 2, terms[0].shape[2])
    outs = [jax.ShapeDtypeStruct(shape, f32), jax.ShapeDtypeStruct(shape, bf16)]
    return order.call(side_kernel, rows, terms, outs, "side")


def down_end_kernel(where_ref, keep, got, out):
    half = keep.shape[1]
    x = bit_of(where_ref, 0)
    out[0, :, pl.ds(pl.multiple_of(x * half, half), half)] = keep[...]
    out[0, :, other_half(where_ref, half)] = got[...].astype(f32)


def up_end_kernel(where_ref, left, right, out):
    out[0] = both_terms((left, right))


def in_end_kernel(where_ref, *refs):
    *terms, in_out, out_out, gain_out, bias_out, upb_out, downb_out = refs
    both = jnp.concatenate(
        [both_terms(pair) for pair in zip(terms[::2], terms[1::2])], axis=0
    )
    lean, tall = out_out.shape[1], upb_out.shape[1]
    out_out[0] = both[:lean]
    in_out[0] = both[lean:tall]
    gain_out[0] = both[tall : tall + 4, :lean]
    bias_out[:, 0, :] = both[tall + 4 : tall + 9, :lean]
    downb_out[...] = both[tall + 9 : tall + 10, :lean]
    upb_out[...] = both[tall + 10 : tall + 11, :tall]


def end(order, kernel, rows, terms, shapes, name):
    outs = [jax.ShapeDtypeStruct(shape, f32) for shape in shapes]
    return order.call(kernel, rows, terms, outs, name)


def on_device(
    tokens,
    patch_mask,
    cotangent,
    in_weight,
    out_weight,
    up_weight,
    down_weight,
    gains,
    biases,
    up_bias,
    down_bias,
):
    weights = (in_weight, out_weight, up_weight, down_weight, gains, biases, up_bias, down_bias)
    images, patches, width = tokens.shape
    hidden = up_weight.shape[2]
    count = lax.axis_size("dp")
    section = lax.axis_index("section")
    place = lax.axis_index("dp")
    is_first = section == 0
    where = jnp.stack([section, place]).astype(jnp.int32)
    x, y = place & 1, (place >> 1) & 1
    small = count == 16
    rows = [Rows(True, images, patches), Rows(False, images, patches)]

    small_args = {
        MASK: patch_mask,
        TOKENS: jnp.swapaxes(tokens, 0, 1),
        LATENT: gains,
        GAINS: gains,
        BIASES: jnp.swapaxes(biases, 0, 1),
        UP_BIAS: up_bias,
        DOWN_BIAS: down_bias,
        COT: jnp.swapaxes(cotangent, 1, 2),
    }
    matrices = weights[:4]
    sent, kept_first = first_block(rows[0], where, small_args, matrices)
    small_args[LATENT] = lax.ppermute(sent, "section", [(0, 1)])
    early = ()
    if small:
        early = tuple(
            swap(kept_first[name], 0, bit, count)
            for name, bit in ((GL_SEND, 0), (H2, 1), (HO, 0))
        )
    back, dx_second, x2_second, state_second = second_block(
        rows[1], where, small_args, matrices, rows[0].queries
    )
    returned = lax.ppermute(back, "section", [(1, 0)])

    def first_back(returned, saved):
        return back_block(rows[0], where, {**small_args, RETURNED: returned}, matrices, saved)

    def sums(order, phase):
        layout = rows[phase]
        lean, tall = width // 16, hidden // 16

        def step(position, terms):
            return halve(order, layout, phase, position, terms, count)

        def cross(terms):
            keep, send = side(order, layout, terms)
            return [keep, swap(send, phase, 0, count)]

        def up_end(terms):
            return end(order, up_end_kernel, layout, terms, [(1, tall, width)], "up_end")

        def down_end(terms):
            return end(order, down_end_kernel, layout, terms, [(1, lean, hidden)], "down_end")

        def in_end(terms):
            shapes = [(1, 3 * lean, width), (1, lean, width), (1, 4, lean), (5, 1, lean)]
            shapes += [(1, tall), (1, lean)]
            return end(order, in_end_kernel, layout, terms, shapes, "in_end")

        return step, cross, up_end, down_end, in_end

    if small:

        def first_rest(returned, early, sent, saved, x2, dx, state):
            dx, state = first_back(returned, saved)
            got_gl, got_h2, got_ho = early
            got_dy = swap(state[DY], 0, 0, count)
            got_du = swap(state[SEND_DU], 0, 1, count)
            order = Order(where)
            order.last = state[VEC]
            got_io = swap(order.gate(state[SEND_IO]), 0, 0, count)
            keep, send = down_grad(
                order, rows[0], [saved[GL], state[DY], got_gl, got_dy], width
            )
            down = [keep, swap(send, 0, 1, count)]
            keep, send = up_grad(
                order, rows[0], [state[KEEP_UP], saved[H2], got_du, got_h2], width
            )
            up = [keep, swap(send, 0, 0, count)]
            keep, send = in_first(
                order, rows[0], state[KEEP_IO], saved[HO], got_io, got_ho, state[VEC]
            )
            rest = [keep, swap(send, 0, 1, count)]

            step, cross, up_end, down_end, in_end = sums(order, 0)
            outputs = unsort(order, rows[0], patch_mask, sent, dx)
            down = step(2, down)
            up = step(2, up)
            rest = step(2, rest)
            down = step(3, down)
            up = step(3, up)
            rest = step(3, rest)
            down = cross(down)
            up = up_end(up)
            down = down_end(down)
            rest = in_end(rest)
            return *outputs, *rest[:2], *up, *down, *rest[2:]

        def second_rest(returned, early, sent, saved, x2, dx, state):
            got_up = swap(state[SEND_UP], 1, 1, count)
            got_down = swap(state[SEND_DOWN], 1, 0, count)
            order = Order(where)
            keep_z, send_z, keep_y, send_y = in_back(order, rows[1], state)
            upper = [keep_z, swap(send_z, 1, 2, count)]
            lower = [keep_y, swap(send_y, 1, 1, count)]
            keep, send = up_grad(
                order, rows[1], [state[KEEP_UP], state[SEND_UP], got_up], width
            )
            up = [keep, swap(send, 1, 0, count)]
            keep, send = down_grad(
                order, rows[1], [state[GL], state[SEND_DOWN], got_down], width
            )
            down = [keep, swap(send, 1, 2, count)]
            step, cross, up_end, down_end, in_end = sums(order, 1)
            lower = step(0, lower)
            upper = step(3, upper)
            up = step(2, up)
            down = step(3, down)
            lower = step(2, lower)
            upper = step(0, upper)
            up = step(3, up)
            outputs = unsort(order, rows[1], patch_mask, x2, dx)
            down = step(1, down)
            lower = step(3, lower)
            upper = step(1, upper)
            down = cross(down)
            up = up_end(up)
            down = down_end(down)
            rest = in_end(upper + lower)
            return *outputs, *rest[:2], *up, *down, *rest[2:]

        done = lax.cond(
            is_first,
            first_rest,
            second_rest,
            returned,
            early,
            sent,
            kept_first,
            x2_second,
            dx_second,
            state_second,
        )
        return (
            *(jnp.swapaxes(values, 1, 2) for values in done[:6]),
            done[6],
            jnp.swapaxes(done[7], 0, 1),
            *done[8:],
        )

    dx_first, state_first = first_back(returned, kept_first)
    order = Order(where)
    outputs_second = unsort(order, rows[1], patch_mask, x2_second, dx_second)
    outputs_first = unsort(order, rows[0], patch_mask, sent, dx_first)
    half = hidden // 2

    def merged(keep, send):
        parts = [keep.reshape(-1, 4, half // 4), send.reshape(-1, 4, half // 4)]
        both = jnp.where(y == 0, jnp.stack(parts, axis=2), jnp.stack(parts[::-1], axis=2))
        return both.reshape(-1, hidden)

    io = []
    for at, size in ((0, 3 * width), (3 * width // 2, width)):
        keep = state_first[KEEP_IO][:, at : at + size // 2].reshape(-1, 8, size // 16)
        send = state_first[SEND_IO][: keep.shape[0], at : at + size // 2]
        parts = [keep, send.reshape(-1, 8, size // 16)]
        both = jnp.where(x == 0, jnp.stack(parts, axis=2), jnp.stack(parts[::-1], axis=2))
        io.append(both.reshape(-1, size))
    ho = kept_first[HO]
    first = [
        (io[0], ho[:, :width]),
        (io[1], ho[:, width:]),
        (merged(state_first[KEEP_UP], state_first[SEND_DU]), kept_first[H2]),
        (state_first[DY], kept_first[GL]),
    ]
    send = state_second[SEND_UP]
    second = [
        (state_second[DQKV], state_second[H1]),
        (state_second[DA], state_second[O]),
        (merged(state_second[KEEP_UP], send[:, :half]), send[:, half:]),
        (state_second[SEND_DOWN][:, half:], state_second[GL]),
    ]
    grads = [
        [*outputs_second, state_second[VEC], *(dot_tn(*pair) for pair in second)],
        [*outputs_first, state_first[VEC], *(dot_tn(*pair) for pair in first)],
    ]
    result, token_grads, vec, *finals = [
        jnp.where(is_first, left, right) for left, right in zip(grads[1], grads[0])
    ]
    finals = [lax.psum_scatter(f, "dp", scatter_dimension=0, tiled=True) for f in finals]
    vec = lax.psum(vec, "dp")
    lean, tall = width // count, hidden // count
    up_vec = vec[10:14].reshape(1, hidden)
    vec = lax.dynamic_slice_in_dim(vec, place * lean, lean, 1)
    up_vec = lax.dynamic_slice_in_dim(up_vec, place * tall, tall, 1)
    return (
        jnp.swapaxes(result, 1, 2),
        jnp.swapaxes(token_grads, 1, 2),
        *(final.T[None] for final in finals),
        vec[0:4][None],
        vec[4:9][None],
        up_vec,
        vec[9:10],
    )


def solution(mesh):
    return jax.shard_map(
        on_device,
        mesh=mesh,
        in_specs=(
            PartitionSpec("dp", None, None),
            PartitionSpec("dp", None),
            PartitionSpec("section", "dp", None, None),
            PartitionSpec("section", None, None),
            PartitionSpec("section", None, None),
            PartitionSpec("section", None, None),
            PartitionSpec("section", None, None),
            PartitionSpec("section", None, None),
            PartitionSpec("section", None, None),
            PartitionSpec("section", None),
            PartitionSpec("section", None),
        ),
        out_specs=(
            PartitionSpec("section", "dp", None, None),
            PartitionSpec("section", "dp", None, None),
            PartitionSpec("section", None, "dp"),
            PartitionSpec("section", None, "dp"),
            PartitionSpec("section", None, "dp"),
            PartitionSpec("section", None, "dp"),
            PartitionSpec("section", None, "dp"),
            PartitionSpec("section", None, "dp"),
            PartitionSpec("section", "dp"),
            PartitionSpec("section", "dp"),
        ),
        check_vma=False,
    )
```

```python
import functools

import jax
import jax.numpy as jnp
from jax import lax
from jax.experimental import pallas as pl
from jax.experimental.pallas import tpu as pltpu
from jax.sharding import PartitionSpec

HEADS = 12
HEAD_DIM = 64
PAIRS = HEADS // 2
LANES = 2 * HEAD_DIM
MASK_LO = 59
MASK_HI = 117
TILE = 768

(
    W_IN,
    W_OUT,
    W_UP,
    W_DOWN,
    XS,
    H1,
    QKV,
    P,
    O,
    A,
    X1,
    H2,
    GP,
    GL,
    Y,
    SEND_DOWN,
    KEEP_UP,
    SEND_UP,
    GL_SEND,
    HO,
    KEEP_IO,
    SEND_IO,
    DA,
    DQKV,
    DY,
    DU,
    DO,
    VEC,
    MASK,
    TOKENS,
    LATENT,
    GAINS,
    BIASES,
    UP_BIAS,
    DOWN_BIAS,
    COT,
    RETURNED,
    SEND_DU,
    KEEP_DY,
    SEND_DY,
) = range(40)

UNROLL = 6
UNROLL_BACK = 3
MIB = 2**20

epsilon = 1e-06
f32 = jnp.float32
bf16 = jnp.bfloat16
ANY = pl.BlockSpec(memory_space=pl.ANY)
SMEM = pl.BlockSpec(memory_space=pltpu.SMEM)
VMEM = pl.BlockSpec(memory_space=pltpu.VMEM)


def cost(micros, memory=None):
    size = int((memory or micros) * 3.69e6)
    return pl.CostEstimate(flops=int(micros * 1.15e9), bytes_accessed=size, transcendentals=0)


def up16(count):
    return -(-count // 16) * 16


class Rows:
    def __init__(self, first, images, patches):
        most = patches - MASK_LO if first else MASK_HI
        self.first = first
        self.images = images
        self.patches = patches
        self.top = up16(most)
        self.rest = 0 if first else up16(patches - self.top)
        self.keys = self.top + self.rest
        self.queries = images * self.top
        self.total = images * self.keys


def dot(left, right):
    return jnp.dot(left, right, preferred_element_type=f32)


def dot_nt(left, right):
    return lax.dot_general(left, right, (((1,), (1,)), ((), ())), preferred_element_type=f32)


def dot_tn(left, right):
    return lax.dot_general(left, right, (((0,), (0,)), ((), ())), preferred_element_type=f32)


def iota(shape, dim):
    return lax.broadcasted_iota(jnp.int32, shape, dim)


def sort_rows(mask_ref, rows):
    masked = mask_ref[...].astype(f32)
    flag = 1.0 - masked if rows.first else masked
    n = rows.patches
    tri = jnp.where(iota((n, n), 0) <= iota((n, n), 1), 1.0, 0.0).astype(bf16)
    upto = dot(flag.astype(bf16), tri)
    count = jnp.sum(flag, axis=1, keepdims=True)
    at = iota(flag.shape, 1).astype(f32)
    place = jnp.where(flag > 0, upto - 1.0, count + at - upto)
    return flag, place, count


def pick(place, image, start, length):
    slots = iota((length, place.shape[1]), 0).astype(f32) + float(start)
    return jnp.where(slots == place[image : image + 1, :], 1.0, 0.0)


def valid_rows(count, rows):
    parts = [
        jnp.where(iota((rows.top, 1), 0).astype(f32) < count[b : b + 1, :], 1.0, 0.0)
        for b in range(rows.images)
    ]
    return jnp.concatenate(parts, axis=0)


def normed(states):
    centre = states - jnp.mean(states, axis=-1, keepdims=True)
    spread = jnp.mean(centre * centre, axis=-1, keepdims=True)
    scale = lax.rsqrt(spread + epsilon)
    return centre * scale, scale


def norm_back(grad, unit, scale, gain):
    inner = grad * gain
    along = jnp.mean(inner * unit, axis=-1, keepdims=True)
    return scale * (inner - jnp.mean(inner, axis=-1, keepdims=True) - unit * along)


def gelu_parts(values):
    size = jnp.abs(values) * (0.5**0.5)
    t = 1.0 / (1.0 + 0.3275911 * size)
    series = t * (
        0.254829592
        + t * (-0.284496736 + t * (1.421413741 + t * (-1.453152027 + t * 1.061405429)))
    )
    decay = jnp.exp(-0.5 * values * values)
    upper = 0.5 * series * decay
    below = jnp.where(values < 0, upper, 1.0 - upper)
    return below, decay * 0.3989422804014327


def total(values):
    return jnp.sum(values, axis=0, keepdims=True)


def key_rows(ref, image, lanes, rows):
    block = ref[image * rows.top : (image + 1) * rows.top, lanes]
    if rows.rest == 0:
        return block
    start = rows.queries + image * rows.rest
    return jnp.concatenate([block, ref[start : start + rows.rest, lanes]], axis=0)


class Copies:
    def __init__(self, sems):
        self.sems = sems
        self.used = 0

    def start(self, source, target):
        copy = pltpu.make_async_copy(source, target, self.sems.at[self.used])
        self.used += 1
        copy.start()
        return copy


SAVED = (XS, H1, QKV, P, O, A, X1, H2, GP, GL, Y)
WEIGHTS = (W_IN, W_OUT, W_UP, W_DOWN)


def kept_shapes(rows, width, hidden):
    queries = rows.queries
    return {
        W_IN: ((width, 3 * width), bf16),
        W_OUT: ((width, width), bf16),
        W_UP: ((width, hidden), bf16),
        W_DOWN: ((hidden, width), bf16),
        XS: ((rows.total, width), bf16),
        H1: ((rows.total, width), bf16),
        QKV: ((rows.total, 3 * width), bf16),
        P: ((rows.images * PAIRS, 2 * rows.top, rows.keys), bf16),
        O: ((queries, width), bf16),
        A: ((queries, width), bf16),
        X1: ((queries, width), f32),
        H2: ((queries, width), bf16),
        GP: ((queries, hidden), bf16),
        GL: ((queries, hidden), bf16),
        Y: ((queries, width), bf16),
        SEND_DOWN: ((queries, hidden // 2 + width), bf16),
        KEEP_UP: ((queries, hidden // 2), bf16),
        SEND_UP: ((queries, hidden // 2 + width), bf16),
        GL_SEND: ((queries, hidden // 2), bf16),
        HO: ((queries, 2 * width), bf16),
        KEEP_IO: ((queries, 2 * width), bf16),
        SEND_IO: ((queries + 16, 2 * width), bf16),
        DA: ((queries, width), bf16),
        DQKV: ((rows.total, 3 * width), bf16),
        DY: ((queries, width), bf16),
        DU: ((queries, hidden), bf16),
        SEND_DU: ((queries, hidden // 2), bf16),
        KEEP_DY: ((queries, width // 2), bf16),
        SEND_DY: ((queries, width // 2), bf16),
        DO: ((queries, width), bf16),
        VEC: ((16, width), f32),
    }


def bit_of(where_ref, order):
    return (where_ref[1] >> order) & 1


def active(where_ref, rows):
    return where_ref[0] == (0 if rows.first else 1)


def lane_sides():
    lane = iota((1, LANES), 1)
    sides = [(lane < HEAD_DIM), (lane >= HEAD_DIM)]
    return sides, [jnp.where(side, 1.0, 0.0).astype(bf16) for side in sides]


def two_heads(values, masks):
    return jnp.concatenate([values * masks[0], values * masks[1]], axis=0)


def mover(count, rows, image, start, length, height):
    behind = iota((length, height), 0) - iota((length, height), 1)
    behind = behind.astype(f32) + float(start) == count[image : image + 1, :]
    seen = iota((length, height), 1).astype(f32) < rows.patches - count[image : image + 1, :]
    return jnp.where(behind & seen, 1.0, 0.0).astype(bf16)


def forward_part(rows, order, small, held, wait, done):
    tok_ref, lat_ref = small[TOKENS], small[LATENT]
    gains_ref, biases_ref = small[GAINS], small[BIASES]
    flag, place, count = order
    images, top, queries = rows.images, rows.top, rows.queries
    width = held[W_OUT].shape[0]
    scale = HEAD_DIM**-0.5

    def states_of(b, start, length):
        chosen = pick(place, b, start, length)
        if rows.first:
            return dot(chosen.astype(bf16), tok_ref[:, b, :])
        from_tokens = dot((chosen * flag[b : b + 1, :]).astype(bf16), tok_ref[:, b, :])
        height = lat_ref.shape[0] // images
        move = mover(count, rows, b, start, length, height)
        return from_tokens + dot(move, lat_ref[b * height : (b + 1) * height])

    pieces = [states_of(b, 0, top) for b in range(images)]
    if rows.rest:
        pieces += [states_of(b, top, rows.rest) for b in range(images)]
    states = jnp.concatenate(pieces, axis=0)
    held[XS][...] = states.astype(bf16)
    done(XS)
    unit, _ = normed(states)
    h1 = (unit * gains_ref[0, 0:1, :] + biases_ref[0]).astype(bf16)
    held[H1][...] = h1
    done(H1)
    qkv = held[QKV]
    wi = held[W_IN]
    wait(W_IN)
    qkv[0:queries, 0:width] = (dot(h1[:queries], wi[:, :width]) + biases_ref[1]).astype(bf16)
    if rows.rest:
        qkv[queries:, 0:width] = jnp.zeros((rows.total - queries, width), bf16)
    qkv[:, width : 2 * width] = dot(h1, wi[:, width : 2 * width]).astype(bf16)
    qkv[:, 2 * width :] = (dot(h1, wi[:, 2 * width :]) + biases_ref[2]).astype(bf16)
    done(QKV)
    sides, masks = lane_sides()

    @pl.loop(0, PAIRS, unroll=UNROLL)
    def _(pair):
        lo = pl.multiple_of(pair * LANES, LANES)
        for b in range(images):
            q = qkv[b * top : (b + 1) * top, pl.ds(lo, LANES)]
            k = key_rows(qkv, b, pl.ds(width + lo, LANES), rows)
            v = key_rows(qkv, b, pl.ds(2 * width + lo, LANES), rows)
            at = iota((1, rows.keys), 1).astype(f32)
            if rows.first:
                usable = at < count[b : b + 1, :]
            else:
                usable = at < float(rows.patches)
            raw = dot_nt(two_heads(q, masks), k)
            logits = jnp.where(usable, raw * scale, -1e30)
            grown = jnp.exp(logits - jnp.max(logits, axis=-1, keepdims=True))
            p = (grown * (1.0 / jnp.sum(grown, axis=-1, keepdims=True))).astype(bf16)
            held[P][b * PAIRS + pair] = p
            mixed = dot(p, v)
            held[O][b * top : (b + 1) * top, pl.ds(lo, LANES)] = jnp.where(
                sides[0], mixed[:top], mixed[top:]
            ).astype(bf16)

    done(P)
    done(O)
    wait(W_OUT)
    a = dot(held[O][...], held[W_OUT][...]) + biases_ref[3]
    held[A][...] = a.astype(bf16)
    done(A)
    usable_rows = valid_rows(count, rows)
    x1 = states[:queries] + gains_ref[0, 1:2, :] * a * usable_rows
    held[X1][...] = x1
    done(X1)
    unit, _ = normed(x1)
    h2 = (unit * gains_ref[0, 2:3, :] + biases_ref[4]).astype(bf16)
    held[H2][...] = h2
    done(H2)
    wait(W_UP)
    y = jnp.zeros((queries, width), f32)
    for start in range(0, held[W_UP].shape[1], TILE):
        cols = slice(start, start + TILE)
        u = dot(h2, held[W_UP][:, cols]) + small[UP_BIAS][:, cols]
        below, density = gelu_parts(u)
        gl = (u * below).astype(bf16)
        held[GL][:, cols] = gl
        held[GP][:, cols] = (below + u * density).astype(bf16)
        done(GL, cols)
        done(GP, cols)
        wait(W_DOWN)
        y = y + dot(gl, held[W_DOWN][cols, :])
    done(GL_SEND)
    y = y + small[DOWN_BIAS][...]
    held[Y][...] = y.astype(bf16)
    done(Y)
    return (x1 + gains_ref[0, 3:4, :] * y * usable_rows).astype(bf16)


def part_shards(where_ref, values, keep, send, at):
    low_first = bit_of(where_ref, 0) == 0
    size = values.shape[1] // 16
    lanes = slice(at, at + 8 * size)
    height = values.shape[0]
    for own in range(2):
        picked = [values[:, j * size : (j + 1) * size] for j in range(own, 16, 2)]
        picked = jnp.concatenate(picked, axis=1)
        if own == 0:
            keep[:, lanes] = picked
        else:
            even = keep[:, lanes]
            keep[:, lanes] = jnp.where(low_first, even, picked)
            send[:height, lanes] = jnp.where(low_first, picked, even)


def backward_part(rows, order, where_ref, small, held, wait, done, dx_ref, ret_buf):
    cot_ref, gains_ref = small[COT], small[GAINS]
    flag, place, count = order
    images, top, queries = rows.images, rows.top, rows.queries
    hidden, width = held[W_DOWN].shape
    scale = HEAD_DIM**-0.5
    usable_rows = valid_rows(count, rows)
    vec = held[VEC]
    vec[...] = jnp.zeros(vec.shape, f32)
    pieces = []
    for b in range(images):
        chosen = (pick(place, b, 0, top) * flag[b : b + 1, :]).astype(bf16)
        piece = dot(chosen, cot_ref[0, :, b, :])
        if rows.first:
            piece = piece + small[RETURNED][b * top : (b + 1) * top].astype(f32)
        pieces.append(piece)
    grad = jnp.concatenate(pieces, axis=0)
    dy = (grad * gains_ref[0, 3:4, :] * usable_rows).astype(bf16)
    held[DY][...] = dy
    done(DY)
    if rows.first:
        part_shards(where_ref, held[DY], held[KEEP_DY], held[SEND_DY], 0)
        done(KEEP_DY)
        done(SEND_DY)
    wait(Y)
    vec[3:4, :] = total(grad * held[Y][...].astype(f32))
    vec[9:10, :] = total(dy.astype(f32))

    wait(W_DOWN)
    wait(GP)
    for step in range(hidden // TILE):
        cols = slice(step * TILE, (step + 1) * TILE)
        dgl = dot_nt(dy, held[W_DOWN][cols, :])
        du = (dgl * held[GP][:, cols].astype(f32)).astype(bf16)
        vec[10 + step : 11 + step, :] = total(du.astype(f32))
        held[DU][:, cols] = du
    done(DU)
    wait(W_UP)
    dh2 = dot_nt(held[DU][...], held[W_UP][...])

    wait(X1)
    unit, spread = normed(held[X1][...])
    vec[2:3, :] = total(dh2 * unit)
    vec[8:9, :] = total(dh2)
    dx1 = grad + norm_back(dh2, unit, spread, gains_ref[0, 2:3, :])
    da = (dx1 * gains_ref[0, 1:2, :] * usable_rows).astype(bf16)
    wait(A)
    vec[1:2, :] = total(dx1 * held[A][...].astype(f32) * usable_rows)
    vec[7:8, :] = total(da.astype(f32))
    held[DA][...] = da
    done(DA)
    do_ref = held[DO]
    wait(W_OUT)
    do_ref[...] = dot_nt(da, held[W_OUT][...]).astype(bf16)
    qkv, dqkv = held[QKV], held[DQKV]
    sides, masks = lane_sides()
    if rows.rest:
        dqkv[queries:, 0:width] = jnp.zeros((rows.total - queries, width), bf16)
    wait(QKV)
    wait(P)

    @pl.loop(0, PAIRS, unroll=UNROLL_BACK)
    def _(pair):
        lo = pl.multiple_of(pair * LANES, LANES)
        for b in range(images):
            q = qkv[b * top : (b + 1) * top, pl.ds(lo, LANES)]
            k = key_rows(qkv, b, pl.ds(width + lo, LANES), rows)
            v = key_rows(qkv, b, pl.ds(2 * width + lo, LANES), rows)
            do = two_heads(do_ref[b * top : (b + 1) * top, pl.ds(lo, LANES)], masks)
            p = held[P][b * PAIRS + pair]
            wide = p.astype(f32)
            dp = dot_nt(do, v)
            inner = jnp.sum(wide * dp, axis=-1, keepdims=True)
            draw = (wide * (dp - inner) * scale).astype(bf16)
            mixed = dot(draw, k)
            dq = jnp.where(sides[0], mixed[:top], mixed[top:])
            dk = dot_tn(draw, two_heads(q, masks))
            dv = dot_tn(p, do)
            for at, part in enumerate((dq, dk, dv)):
                part = part.astype(bf16)
                lanes = pl.ds(at * width + lo, LANES)
                dqkv[b * top : (b + 1) * top, lanes] = part[:top]
                if rows.rest and at > 0:
                    start = queries + b * rows.rest
                    dqkv[start : start + rows.rest, lanes] = part[top:]

    done(DQKV)
    if rows.first:
        part_shards(where_ref, dqkv, held[KEEP_IO], held[SEND_IO], 0)
        part_shards(where_ref, held[DA], held[KEEP_IO], held[SEND_IO], dqkv.shape[1] // 2)
        done(KEEP_IO)
    wait(W_IN)
    dh1 = jnp.zeros((rows.total, width), f32)
    for at in range(3):
        cols = slice(at * width, (at + 1) * width)
        dh1 = dh1 + dot_nt(dqkv[:, cols], held[W_IN][:, cols])
    wait(XS)
    unit, spread = normed(held[XS][...].astype(f32))
    dx = norm_back(dh1, unit, spread, gains_ref[0, 0:1, :])
    if rows.rest:
        rest = dx[queries:].astype(bf16)
    dx = dx[:queries] + dx1
    dx_ref[...] = dx
    if not rows.first:
        high = dx.astype(bf16)
        for b in range(images):
            height = ret_buf.shape[0] // images
            move = mover(count, rows, b, 0, rows.keys, height)
            part = slice(b * top, (b + 1) * top)
            tail = slice(b * rows.rest, (b + 1) * rows.rest)
            back = dot_tn(move[:top], high[part]) + dot_tn(move[top:], rest[tail])
            ret_buf[b * height : (b + 1) * height] = back.astype(bf16)
    vec[0:1, :] = total(dh1 * unit)
    vec[4:5, :] = total(dh1)
    vec[5:6, :] = total(dqkv[:, 0:width].astype(f32))
    vec[6:7, :] = total(dqkv[:, 2 * width :].astype(f32))
    done(VEC)
    if rows.first:
        held[SEND_IO][queries:, :width] = vec[...].astype(bf16)
        held[SEND_IO][queries:, width:] = jnp.zeros((16, width), bf16)
        done(SEND_IO)


class Flow:
    def __init__(self, held, sems, source):
        self.held = held
        self.source = source
        self.copies = Copies(sems)
        self.gets = {}
        self.later = {}
        self.puts = []

    def fetch(self, *names, after=None):
        if after is not None:
            self.later[after] = names
            return
        for name in names:
            ref = self.source[name]
            ref = ref.at[0] if name in WEIGHTS else ref
            self.gets[name] = self.copies.start(ref, self.held[name])

    def wait(self, name):
        if name in self.gets:
            self.gets.pop(name).wait()
            self.fetch(*self.later.pop(name, ()))

    def put(self, source, target):
        self.puts.append(self.copies.start(source, target))

    def finish(self):
        while self.gets:
            self.wait(next(iter(self.gets)))
        for copy in self.puts:
            copy.wait()


FORWARD_SMALL = (MASK, TOKENS, LATENT, GAINS, BIASES, UP_BIAS, DOWN_BIAS)
SECOND_SMALL = FORWARD_SMALL + (COT,)
BACK_SMALL = (MASK, COT, RETURNED, GAINS)
FIRST_HELD = WEIGHTS + SAVED
FIRST_OUTS = (XS, QKV, P, A, X1, H2, GP, GL, Y, HO)
SECOND_HELD = (W_IN, W_OUT) + SAVED + (DA, DQKV, DY, DU, DO)
SECOND_OUTS = (H1, O, GL, SEND_DOWN, KEEP_UP, SEND_UP, DA, DQKV)
BACK_IN = WEIGHTS + (XS, QKV, P, A, X1, GP, Y)
BACK_OUTS = (KEEP_DY, SEND_DY, KEEP_UP, SEND_DU, KEEP_IO)
BACK_HELD = BACK_IN + (DA, DQKV, DO, DY, DU, KEEP_DY, SEND_DY, KEEP_IO)


def take_from(refs):
    def take(names):
        taken = dict(zip(names, refs))
        del refs[: len(names)]
        return taken

    return take


def part_du(flow, where_ref, keep, send):
    du = flow.held[DU]
    size = du.shape[1] // 8
    bit = bit_of(where_ref, 1)
    for target, own in ((keep, bit), (send, 1 - bit)):
        for z in range(4):
            start = pl.multiple_of((2 * z + own) * size, size)
            flow.put(du.at[:, pl.ds(start, size)], target.at[:, pl.ds(z * size, size)])


def other_half(where_ref, half):
    return pl.ds(pl.multiple_of((1 - bit_of(where_ref, 0)) * half, half), half)


def first_kernel(rows, where_ref, *refs):
    refs = list(refs)
    take = take_from(refs)
    small, weights = take(FORWARD_SMALL), take(WEIGHTS)
    x2_out, outs = refs.pop(0), take(FIRST_OUTS)
    held = take(FIRST_HELD)
    x2_buf, sems = refs

    @pl.when(active(where_ref, rows))
    def _():
        flow = Flow(held, sems, weights)
        flow.fetch(W_IN, W_OUT)
        flow.fetch(W_UP, W_DOWN, after=W_IN)
        order = sort_rows(small[MASK], rows)
        width = held[O].shape[1]

        def done(name, cols=None):
            if cols is not None:
                flow.put(held[name].at[:, cols], outs[name].at[:, cols])
            elif name in (H1, O):
                start = 0 if name == H1 else width
                flow.put(held[name], outs[HO].at[:, pl.ds(start, width)])
            elif name in outs:
                flow.put(held[name], outs[name])

        x2_buf[...] = forward_part(rows, order, small, held, flow.wait, done)
        flow.put(x2_buf, x2_out)
        flow.finish()


def hold_kernel(rows, where_ref, *refs):
    *refs, sems = refs
    half = len(refs) // 2

    @pl.when(active(where_ref, rows))
    def _():
        copies = Copies(sems)
        started = []
        for source, target in zip(refs[:half], refs[half:]):
            source = source.at[0] if len(source.shape) > len(target.shape) else source
            started.append(copies.start(source, target))
        for copy in started:
            copy.wait()


def hold(rows, where, arrays):
    return pl.pallas_call(
        functools.partial(hold_kernel, rows),
        out_shape=[jax.ShapeDtypeStruct(a.shape[-2:], a.dtype) for a in arrays],
        in_specs=[SMEM] + [ANY] * len(arrays),
        out_specs=[VMEM] * len(arrays),
        scratch_shapes=[pltpu.SemaphoreType.DMA((len(arrays),))],
        compiler_params=pltpu.CompilerParams(vmem_limit_bytes=16 * MIB),
        cost_estimate=cost(30, 3000),
        name="hold",
    )(where, *arrays)


def big_call(kernel, operands, in_specs, direct, outs, scratch, name, micros):
    return pl.pallas_call(
        kernel,
        out_shape=direct + outs,
        in_specs=in_specs,
        out_specs=[VMEM] * len(direct) + [ANY] * len(outs),
        scratch_shapes=scratch,
        compiler_params=pltpu.CompilerParams(vmem_limit_bytes=(36 if micros == 3000 else 56) * MIB),
        cost_estimate=cost(micros),
        name=name,
    )(*operands)


def shaped(shapes, names, make):
    return [make(*shapes[name]) for name in names]


def first_block(rows, where, small, weights):
    width, hidden = weights[2].shape[1:]
    shapes = kept_shapes(rows, width, hidden)
    results = big_call(
        functools.partial(first_kernel, rows),
        [where] + [small[name] for name in FORWARD_SMALL] + list(weights),
        [SMEM] + [VMEM] * len(FORWARD_SMALL) + [ANY] * 4,
        [],
        [jax.ShapeDtypeStruct((rows.queries, width), bf16)]
        + shaped(shapes, FIRST_OUTS, jax.ShapeDtypeStruct),
        shaped(shapes, FIRST_HELD, pltpu.VMEM)
        + [pltpu.VMEM((rows.queries, width), bf16), pltpu.SemaphoreType.DMA((48,))],
        "first_block",
        1500,
    )
    return results[0], dict(zip(FIRST_OUTS, results[1:]))


def second_kernel(rows, where_ref, *refs):
    refs = list(refs)
    take = take_from(refs)
    small, weights = take(SECOND_SMALL), take((W_IN, W_OUT))
    resident = take((W_UP, W_DOWN))
    ret_out, dx_out, x2_out, vec_out = (refs.pop(0) for _ in range(4))
    outs = take(SECOND_OUTS)
    held = take(SECOND_HELD)
    held.update(resident)
    held[VEC] = vec_out
    (sems,) = refs

    @pl.when(active(where_ref, rows))
    def _():
        flow = Flow(held, sems, weights)
        flow.fetch(W_IN, W_OUT)
        order = sort_rows(small[MASK], rows)
        half = held[DU].shape[1] // 2
        width = held[DY].shape[1]

        def done(name, cols=None):
            if cols is not None:
                if name in outs:
                    flow.put(held[name].at[:, cols], outs[name].at[:, cols])
            elif name == GL_SEND:
                flow.put(
                    held[GL].at[:, other_half(where_ref, half)],
                    outs[SEND_DOWN].at[:, pl.ds(0, half)],
                )
            elif name == H2:
                flow.put(held[H2], outs[SEND_UP].at[:, pl.ds(half, width)])
            elif name == DY:
                flow.put(held[DY], outs[SEND_DOWN].at[:, pl.ds(half, width)])
            elif name == DU:
                part_du(flow, where_ref, outs[KEEP_UP], outs[SEND_UP])
            elif name in outs:
                flow.put(held[name], outs[name])

        x2_out[...] = forward_part(rows, order, small, held, flow.wait, done)
        backward_part(rows, order, where_ref, small, held, flow.wait, done, dx_out, ret_out)
        flow.finish()


def second_block(rows, where, small, weights, resident, back_rows):
    width, hidden = weights[2].shape[1:]
    shapes = kept_shapes(rows, width, hidden)
    results = big_call(
        functools.partial(second_kernel, rows),
        [where] + [small[name] for name in SECOND_SMALL] + list(weights[:2]) + list(resident),
        [SMEM] + [VMEM] * len(SECOND_SMALL) + [ANY] * 2 + [VMEM] * 2,
        [
            jax.ShapeDtypeStruct((back_rows, width), bf16),
            jax.ShapeDtypeStruct((rows.queries, width), f32),
            jax.ShapeDtypeStruct((rows.queries, width), bf16),
            jax.ShapeDtypeStruct((16, width), f32),
        ],
        shaped(shapes, SECOND_OUTS, jax.ShapeDtypeStruct),
        shaped(shapes, SECOND_HELD, pltpu.VMEM) + [pltpu.SemaphoreType.DMA((48,))],
        "second_block",
        3000,
    )
    ret, dx, x2, vec = results[:4]
    return ret, dx, x2, {**dict(zip(SECOND_OUTS, results[4:])), VEC: vec}


def back_kernel(rows, where_ref, *refs):
    refs = list(refs)
    take = take_from(refs)
    small, source = take(BACK_SMALL), take(BACK_IN)
    dx_out, vec_out, send_out = (refs.pop(0) for _ in range(3))
    outs = take(BACK_OUTS)
    held = take(BACK_HELD)
    held[VEC], held[SEND_IO] = vec_out, send_out
    (sems,) = refs

    @pl.when(active(where_ref, rows))
    def _():
        flow = Flow(held, sems, source)
        flow.fetch(Y, W_DOWN, GP)
        flow.fetch(W_UP, X1, after=W_DOWN)
        flow.fetch(A, W_OUT, QKV, P, W_IN, XS, after=W_UP)

        def done(name):
            if name == DU:
                part_du(flow, where_ref, outs[KEEP_UP], outs[SEND_DU])
            elif name in outs:
                flow.put(held[name], outs[name])

        backward_part(
            rows,
            sort_rows(small[MASK], rows),
            where_ref,
            small,
            held,
            flow.wait,
            done,
            dx_out,
            None,
        )
        flow.finish()


def back_block(rows, where, small, weights, saved):
    width, hidden = weights[2].shape[1:]
    shapes = kept_shapes(rows, width, hidden)
    values = {**saved, **dict(zip(WEIGHTS, weights))}
    operands = [where] + [small[name] for name in BACK_SMALL]
    operands += [values[name] for name in BACK_IN]
    results = big_call(
        functools.partial(back_kernel, rows),
        operands,
        [SMEM] + [VMEM] * len(BACK_SMALL) + [ANY] * len(BACK_IN),
        [jax.ShapeDtypeStruct((rows.queries, width), f32)]
        + shaped(shapes, (VEC, SEND_IO), jax.ShapeDtypeStruct),
        shaped(shapes, BACK_OUTS, jax.ShapeDtypeStruct),
        shaped(shapes, BACK_HELD, pltpu.VMEM) + [pltpu.SemaphoreType.DMA((48,))],
        "back_block",
        2000,
    )
    return results[0], {**dict(zip((VEC, SEND_IO) + BACK_OUTS, results[1:]))}


class Order:
    def __init__(self, where):
        self.where = where
        self.last = None

    def call(self, kernel, rows, ins, outs, name, scratch=()):
        def body(where_ref, *refs):
            refs = list(refs)
            if extra:
                del refs[len(ins)]

            @pl.when(active(where_ref, rows))
            def _():
                kernel(where_ref, *refs)

        extra = [] if self.last is None else [self.last]
        results = pl.pallas_call(
            body,
            out_shape=outs,
            in_specs=[SMEM] + [VMEM] * len(ins) + [ANY] * len(extra),
            out_specs=[VMEM] * len(outs),
            scratch_shapes=list(scratch),
            compiler_params=pltpu.CompilerParams(vmem_limit_bytes=30 * MIB),
            cost_estimate=cost(30, 3000),
            name=name,
        )(self.where, *ins, *extra)
        self.last = results[-1]
        return results

    def gate(self, value):
        def body(value_ref, last_ref, out_ref):
            pass

        self.last = pl.pallas_call(
            body,
            out_shape=jax.ShapeDtypeStruct(value.shape, value.dtype),
            in_specs=[ANY] * 2,
            out_specs=ANY,
            input_output_aliases={0: 0},
            cost_estimate=cost(30, 3000),
            name="gate",
        )(value, self.last)
        return self.last


def vec_rows(vec_ref, d, lean):
    width = vec_ref.shape[1]
    long = 4 * lean
    at = long * d % width
    row = 10 + long * d // width
    block = jnp.zeros((16, width), f32)
    first = jnp.concatenate(
        [vec_ref[0:10, d * lean : (d + 1) * lean], jnp.zeros((10, width - lean), f32)], axis=1
    )
    second = jnp.concatenate(
        [vec_ref[row : row + 1, at : at + long], jnp.zeros((1, width - long), f32)], axis=1
    )
    return jnp.concatenate([first, second, block[11:]], axis=0)


def in_kernel(where_ref, dqkv_ref, h1_ref, da_ref, o_ref, vec_ref, *refs):
    keep_z, send_z, keep_y, send_y, buf = refs
    width = h1_ref.shape[1]
    lean, tall = width // 16, dqkv_ref.shape[1] // 16
    tile = dot_tn(da_ref[...], o_ref[...]).astype(bf16)
    for d in range(16):
        buf[d, :lean] = tile[d * lean : (d + 1) * lean]
    half = dqkv_ref.shape[1] // 2
    for step in range(2):
        tile = dot_tn(dqkv_ref[:, step * half : (step + 1) * half], h1_ref[...]).astype(bf16)
        for d in range(8):
            buf[8 * step + d, lean : lean + tall] = tile[d * tall : (d + 1) * tall]
    for d in range(16):
        buf[d, lean + tall :] = vec_rows(vec_ref, d, lean).astype(bf16)
    cut = keep_z.shape[1]
    y, z = bit_of(where_ref, 1), bit_of(where_ref, 2)
    for slot in range(8):
        high, other = slot >> 1, slot & 1
        keep_y[slot] = buf[4 * high + other + 2 * y, cut:]
        send_y[slot] = buf[4 * high + other + 2 * (1 - y), cut:]
        keep_z[slot] = buf[8 * other + high + 4 * z, :cut]
        send_z[slot] = buf[8 * other + high + 4 * (1 - z), :cut]


def in_back(order, rows, state):
    operands = [state[name] for name in (DQKV, H1, DA, O, VEC)]
    width = operands[1].shape[1]
    height, cut = width // 4 + 16, width // 8 + 16
    outs = [jax.ShapeDtypeStruct((8, size, width), bf16) for size in (cut, height - cut)]
    return order.call(
        in_kernel,
        rows,
        operands,
        [outs[0], outs[0], outs[1], outs[1]],
        "in_grad",
        [pltpu.VMEM((16, height, width), bf16)],
    )


def in_first_kernel(where_ref, own_ref, ho_ref, got_ref, got_ho_ref, vec_ref, keep, send, buf, sums):
    queries, width = own_ref.shape[0], vec_ref.shape[1]
    lean, tall = width // 16, 3 * width // 16
    edge = 8 * tall
    for lanes, part, height, at in (
        (slice(0, edge), slice(0, width), tall, lean),
        (slice(edge, 2 * width), slice(width, 2 * width), lean, 0),
    ):
        tile = joined(
            own_ref[:, lanes], got_ref[:queries, lanes], ho_ref[:, part], got_ho_ref[:, part]
        )
        for d in range(8):
            buf[d, at : at + height] = tile[d * height : (d + 1) * height]
    sums[...] = vec_ref[...] + got_ref[queries:, :width].astype(f32)
    low = bit_of(where_ref, 0) == 0
    for d in range(8):
        mine = jnp.where(low, vec_rows(sums, 2 * d, lean), vec_rows(sums, 2 * d + 1, lean))
        buf[d, lean + tall :] = mine.astype(bf16)
    bit = bit_of(where_ref, 1)
    for z in range(4):
        keep[z] = buf[2 * z + bit]
        send[z] = buf[2 * z + 1 - bit]


def in_first(order, rows, own, ho, got, got_ho, vec):
    width = vec.shape[1]
    shape = (width // 4 + 16, width)
    return order.call(
        in_first_kernel,
        rows,
        [own, ho, got, got_ho, vec],
        [jax.ShapeDtypeStruct((4,) + shape, bf16)] * 2,
        "in_grad",
        [pltpu.VMEM((8,) + shape, bf16), pltpu.VMEM(vec.shape, f32)],
    )


def joined(left, left_got, right, right_got):
    left = jnp.concatenate([left, left_got], axis=0)
    right = jnp.concatenate([right, right_got], axis=0)
    return dot_tn(left, right).astype(bf16)


def down_first_kernel(where_ref, dy, got_dy, gl, got_gl, keep, send, buf):
    height = buf.shape[1]
    width = keep.shape[2]
    tile = joined(dy[...], got_dy[...], gl[...], got_gl[...])
    for d in range(8):
        buf[d] = tile[d * height : (d + 1) * height]
    y = bit_of(where_ref, 1)
    for z in range(4):
        for part in range(4):
            rows = slice(part * height, (part + 1) * height)
            cols = slice(part * width, (part + 1) * width)
            keep[z, rows] = buf[2 * z + y, :, cols]
            send[z, rows] = buf[2 * z + 1 - y, :, cols]


def down_first(order, rows, ins, width):
    shape = (width // 16, ins[2].shape[1])
    outs = [jax.ShapeDtypeStruct((4, 4 * shape[0], width), bf16)] * 2
    scratch = [pltpu.VMEM((8,) + shape, bf16)]
    return order.call(down_first_kernel, rows, ins, outs, "down_grad", scratch)


def down_grad_kernel(where_ref, gl, own, got, keep, send, buf):
    height, half = buf.shape[1:]
    width = keep.shape[2]
    mine = pl.multiple_of(bit_of(where_ref, 0) * half, half)
    tile = joined(own[:, half:], got[:, half:], gl[:, pl.ds(mine, half)], got[:, :half])
    for d in range(16):
        buf[d] = tile[d * height : (d + 1) * height]
    bit = bit_of(where_ref, 2)
    for slot in range(4):
        base = 8 * (slot & 1) + (slot & 2)
        for x in range(2):
            for side in range(2):
                start = (2 * x + side) * height
                part = slice(start, start + height)
                cols = slice(side * width, (side + 1) * width)
                keep[slot, part] = buf[base + x + 4 * bit, :, cols]
                send[slot, part] = buf[base + x + 4 * (1 - bit), :, cols]


def down_grad(order, rows, ins, width):
    half = ins[0].shape[1] // 2
    shape = (width // 16, half)
    outs = [jax.ShapeDtypeStruct((4, 4 * shape[0], width), bf16)] * 2
    scratch = [pltpu.VMEM((16,) + shape, bf16)]
    return order.call(down_grad_kernel, rows, ins, outs, "down_grad", scratch)


def up_grad_kernel(where_ref, *refs):
    *ins, keep, send, buf = refs
    height = buf.shape[1]
    half = 8 * height
    bit = bit_of(where_ref, 0)
    if len(ins) == 4:
        du, h2, got_du, got_h2 = (ref[...] for ref in ins)
    else:
        du, own, got = ins
        du, h2, got_du, got_h2 = du[...], own[:, half:], got[:, :half], got[:, half:]
    tile = joined(du, got_du, h2, got_h2)
    for d in range(8):
        buf[d] = tile[d * height : (d + 1) * height]
    for z in range(4):
        keep[z] = buf[2 * z + bit]
        send[z] = buf[2 * z + 1 - bit]


def up_grad(order, rows, ins, width):
    shape = (ins[0].shape[1] // 8, width)
    outs = [jax.ShapeDtypeStruct((4,) + shape, bf16)] * 2
    scratch = [pltpu.VMEM((8,) + shape, bf16)]
    return order.call(up_grad_kernel, rows, ins, outs, "up_grad", scratch)


def swap(value, phase, bit, count):
    pairs = [(phase * count + i, phase * count + (i ^ (1 << bit))) for i in range(count)]
    return lax.ppermute(value, ("section", "dp"), pairs)


def halve_kernel(position, where_ref, *refs):
    *terms, keep, send = refs
    bit = bit_of(where_ref, position)
    at = 0
    for left, right in zip(terms[::2], terms[1::2]):
        part = slice(at, at + left.shape[1])
        at += left.shape[1]
        for slot in range(keep.shape[0]):
            mine, other = 2 * slot + bit, 2 * slot + 1 - bit
            keep[slot, part] = left[mine].astype(f32) + right[mine].astype(f32)
            sent = left[other].astype(f32) + right[other].astype(f32)
            send[slot, part] = sent.astype(bf16)


def halve(order, rows, phase, position, terms, count):
    height = sum(term.shape[1] for term in terms[::2])
    shape = (terms[0].shape[0] // 2, height, terms[0].shape[2])
    keep, send = order.call(
        functools.partial(halve_kernel, position),
        rows,
        terms,
        [jax.ShapeDtypeStruct(shape, f32), jax.ShapeDtypeStruct(shape, bf16)],
        "halve",
    )
    return [keep, swap(send, phase, position, count)]


def unsort_kernel(rows, where_ref, mask_ref, x2_ref, dx_ref, result, grads):
    flag, place, _ = sort_rows(mask_ref, rows)
    for b in range(rows.images):
        part = slice(b * rows.top, (b + 1) * rows.top)
        chosen = (pick(place, b, 0, rows.top) * flag[b : b + 1, :]).astype(bf16)
        dx = dx_ref[part]
        high = dx.astype(bf16)
        low = (dx - high.astype(f32)).astype(bf16)
        result[0, :, b, :] = dot_tn(chosen, x2_ref[part]).astype(bf16)
        grads[0, :, b, :] = dot_tn(chosen, high) + dot_tn(chosen, low)


def unsort(order, rows, mask, x2, dx):
    shape = (1, rows.patches, rows.images, x2.shape[1])
    outs = [jax.ShapeDtypeStruct(shape, kind) for kind in (bf16, f32)]
    return order.call(
        functools.partial(unsort_kernel, rows), rows, [mask, x2, dx], outs, "unsort"
    )


def both_terms(refs):
    return refs[0][0].astype(f32) + refs[1][0].astype(f32)


def side_kernel(where_ref, left, right, keep, send):
    height = keep.shape[0]
    low = bit_of(where_ref, 0) == 0
    both = left[0, : 2 * height].astype(f32) + right[0, : 2 * height].astype(f32)
    keep[...] = jnp.where(low, both[:height], both[height:])
    send[...] = jnp.where(low, both[height:], both[:height]).astype(bf16)


def side(order, rows, terms, lean):
    shape = (2 * lean, terms[0].shape[2])
    outs = [jax.ShapeDtypeStruct(shape, f32), jax.ShapeDtypeStruct(shape, bf16)]
    return order.call(side_kernel, rows, terms, outs, "side")


def down_end_kernel(where_ref, keep, got, out):
    lean, width = keep.shape[0] // 2, keep.shape[1]
    x = bit_of(where_ref, 0)
    for part in range(2):
        source = slice(part * lean, (part + 1) * lean)
        for ref, own in ((keep, x), (got, 1 - x)):
            start = pl.multiple_of((2 * own + part) * width, width)
            out[0, :, pl.ds(start, width)] = ref[source].astype(f32)


def down_first_end_kernel(where_ref, left, right, out):
    lean, width = out.shape[1], left.shape[2]
    for part in range(4):
        source = slice(part * lean, (part + 1) * lean)
        both = left[0, source].astype(f32) + right[0, source].astype(f32)
        out[0, :, part * width : (part + 1) * width] = both


def up_end_kernel(where_ref, left, right, out):
    tall = out.shape[1]
    start = left.shape[1] - tall
    out[0] = left[0, start:].astype(f32) + right[0, start:].astype(f32)


def in_end_kernel(where_ref, *refs):
    *terms, in_out, out_out, gain_out, bias_out, upb_out, downb_out = refs
    both = jnp.concatenate(
        [both_terms(pair) for pair in zip(terms[::2], terms[1::2])], axis=0
    )
    lean, tall = out_out.shape[1], upb_out.shape[1]
    out_out[0] = both[:lean]
    in_out[0] = both[lean:tall]
    gain_out[0] = both[tall : tall + 4, :lean]
    bias_out[:, 0, :] = both[tall + 4 : tall + 9, :lean]
    downb_out[...] = both[tall + 9 : tall + 10, :lean]
    upb_out[...] = both[tall + 10 : tall + 11, :tall]


def end(order, kernel, rows, terms, shapes, name):
    outs = [jax.ShapeDtypeStruct(shape, f32) for shape in shapes]
    return order.call(kernel, rows, terms, outs, name)


def on_device(
    tokens,
    patch_mask,
    cotangent,
    in_weight,
    out_weight,
    up_weight,
    down_weight,
    gains,
    biases,
    up_bias,
    down_bias,
):
    weights = (in_weight, out_weight, up_weight, down_weight, gains, biases, up_bias, down_bias)
    images, patches, width = tokens.shape
    hidden = up_weight.shape[2]
    count = lax.axis_size("dp")
    section = lax.axis_index("section")
    place = lax.axis_index("dp")
    is_first = section == 0
    where = jnp.stack([section, place]).astype(jnp.int32)
    x, y = place & 1, (place >> 1) & 1
    small = count == 16
    rows = [Rows(True, images, patches), Rows(False, images, patches)]

    small_args = {
        MASK: patch_mask,
        TOKENS: jnp.swapaxes(tokens, 0, 1),
        LATENT: gains,
        GAINS: gains,
        BIASES: jnp.swapaxes(biases, 0, 1),
        UP_BIAS: up_bias,
        DOWN_BIAS: down_bias,
        COT: jnp.swapaxes(cotangent, 1, 2),
    }
    matrices = weights[:4]
    sent, kept_first = first_block(rows[0], where, small_args, matrices)
    small_args[LATENT] = lax.ppermute(sent, "section", [(0, 1)])
    early = ()
    if small:
        early = tuple(
            swap(kept_first[name], 0, bit, count)
            for name, bit in ((HO, 0), (H2, 1), (GL, 0))
        )
    resident = hold(rows[1], where, matrices[2:])
    back, dx_second, x2_second, state_second = second_block(
        rows[1], where, small_args, matrices, resident, rows[0].queries
    )
    returned = lax.ppermute(back, "section", [(1, 0)])

    def first_back(returned, saved):
        return back_block(rows[0], where, {**small_args, RETURNED: returned}, matrices, saved)

    def sums(order, phase):
        layout = rows[phase]
        lean, tall = width // 16, hidden // 16

        def step(position, terms):
            return halve(order, layout, phase, position, terms, count)

        def cross(terms):
            keep, send = side(order, layout, terms, lean)
            return [keep, swap(send, phase, 0, count)]

        def up_end(terms):
            return end(order, up_end_kernel, layout, terms, [(1, tall, width)], "up_end")

        def down_end(terms):
            kernel = down_end_kernel if phase else down_first_end_kernel
            return end(order, kernel, layout, terms, [(1, lean, hidden)], "down_end")

        def in_end(terms):
            shapes = [(1, 3 * lean, width), (1, lean, width), (1, 4, lean), (5, 1, lean)]
            shapes += [(1, tall), (1, lean)]
            return end(order, in_end_kernel, layout, terms, shapes, "in_end")

        return step, cross, up_end, down_end, in_end

    if small:

        def first_rest(returned, early, sent, saved, x2, dx, state):
            dx, state = first_back(returned, saved)
            got_ho, got_h2, got_gl = early
            got_dy = swap(state[SEND_DY], 0, 0, count)
            got_du = swap(state[SEND_DU], 0, 1, count)
            order = Order(where)
            order.last = state[VEC]
            got_io = swap(order.gate(state[SEND_IO]), 0, 0, count)
            keep, send = down_first(
                order, rows[0], [state[KEEP_DY], got_dy, saved[GL], got_gl], width
            )
            down = [keep, swap(send, 0, 1, count)]
            keep, send = up_grad(
                order, rows[0], [state[KEEP_UP], saved[H2], got_du, got_h2], width
            )
            up = [keep, swap(send, 0, 0, count)]
            keep, send = in_first(
                order, rows[0], state[KEEP_IO], saved[HO], got_io, got_ho, state[VEC]
            )
            rest = [keep, swap(send, 0, 1, count)]

            step, cross, up_end, down_end, in_end = sums(order, 0)
            down = step(2, down)
            up = step(2, up)
            outputs = unsort(order, rows[0], patch_mask, sent, dx)
            rest = step(2, rest)
            down = step(3, down)
            up = step(3, up)
            rest = step(3, rest)
            up = up_end(up)
            down = down_end(down)
            rest = in_end(rest)
            return *outputs, *rest[:2], *up, *down, *rest[2:]

        def second_rest(returned, early, sent, saved, x2, dx, state):
            got_up = swap(state[SEND_UP], 1, 1, count)
            got_down = swap(state[SEND_DOWN], 1, 0, count)
            order = Order(where)
            keep_z, send_z, keep_y, send_y = in_back(order, rows[1], state)
            upper = [keep_z, swap(send_z, 1, 2, count)]
            lower = [keep_y, swap(send_y, 1, 1, count)]
            keep, send = up_grad(
                order, rows[1], [state[KEEP_UP], state[SEND_UP], got_up], width
            )
            up = [keep, swap(send, 1, 0, count)]
            keep, send = down_grad(
                order, rows[1], [state[GL], state[SEND_DOWN], got_down], width
            )
            down = [keep, swap(send, 1, 2, count)]
            step, cross, up_end, down_end, in_end = sums(order, 1)
            lower = step(0, lower)
            upper = step(3, upper)
            up = step(2, up)
            down = step(3, down)
            lower = step(2, lower)
            upper = step(0, upper)
            up = step(3, up)
            outputs = unsort(order, rows[1], patch_mask, x2, dx)
            down = step(1, down)
            lower = step(3, lower)
            upper = step(1, upper)
            down = cross(down)
            up = up_end(up)
            down = down_end(down)
            rest = in_end(upper + lower)
            return *outputs, *rest[:2], *up, *down, *rest[2:]

        done = lax.cond(
            is_first,
            first_rest,
            second_rest,
            returned,
            early,
            sent,
            kept_first,
            x2_second,
            dx_second,
            state_second,
        )
        return (
            *(jnp.swapaxes(values, 1, 2) for values in done[:6]),
            done[6],
            jnp.swapaxes(done[7], 0, 1),
            *done[8:],
        )

    dx_first, state_first = first_back(returned, kept_first)
    order = Order(where)
    outputs_second = unsort(order, rows[1], patch_mask, x2_second, dx_second)
    outputs_first = unsort(order, rows[0], patch_mask, sent, dx_first)
    half = hidden // 2

    def merged(keep, send):
        parts = [keep.reshape(-1, 4, half // 4), send.reshape(-1, 4, half // 4)]
        both = jnp.where(y == 0, jnp.stack(parts, axis=2), jnp.stack(parts[::-1], axis=2))
        return both.reshape(-1, hidden)

    io = []
    for at, size in ((0, 3 * width), (3 * width // 2, width)):
        keep = state_first[KEEP_IO][:, at : at + size // 2].reshape(-1, 8, size // 16)
        send = state_first[SEND_IO][: keep.shape[0], at : at + size // 2]
        parts = [keep, send.reshape(-1, 8, size // 16)]
        both = jnp.where(x == 0, jnp.stack(parts, axis=2), jnp.stack(parts[::-1], axis=2))
        io.append(both.reshape(-1, size))
    keep = state_first[KEEP_DY].reshape(-1, 8, width // 16)
    parts = [keep, state_first[SEND_DY].reshape(-1, 8, width // 16)]
    dy_first = jnp.where(x == 0, jnp.stack(parts, axis=2), jnp.stack(parts[::-1], axis=2))
    dy_first = dy_first.reshape(-1, width)
    ho = kept_first[HO]
    first = [
        (io[0], ho[:, :width]),
        (io[1], ho[:, width:]),
        (merged(state_first[KEEP_UP], state_first[SEND_DU]), kept_first[H2]),
        (dy_first, kept_first[GL]),
    ]
    send = state_second[SEND_UP]
    second = [
        (state_second[DQKV], state_second[H1]),
        (state_second[DA], state_second[O]),
        (merged(state_second[KEEP_UP], send[:, :half]), send[:, half:]),
        (state_second[SEND_DOWN][:, half:], state_second[GL]),
    ]
    grads = [
        [*outputs_second, state_second[VEC], *(dot_tn(*pair) for pair in second)],
        [*outputs_first, state_first[VEC], *(dot_tn(*pair) for pair in first)],
    ]
    result, token_grads, vec, *finals = [
        jnp.where(is_first, left, right) for left, right in zip(grads[1], grads[0])
    ]
    finals = [lax.psum_scatter(f, "dp", scatter_dimension=0, tiled=True) for f in finals]
    vec = lax.psum(vec, "dp")
    lean, tall = width // count, hidden // count
    up_vec = vec[10:14].reshape(1, hidden)
    vec = lax.dynamic_slice_in_dim(vec, place * lean, lean, 1)
    up_vec = lax.dynamic_slice_in_dim(up_vec, place * tall, tall, 1)
    return (
        jnp.swapaxes(result, 1, 2),
        jnp.swapaxes(token_grads, 1, 2),
        *(final.T[None] for final in finals),
        vec[0:4][None],
        vec[4:9][None],
        up_vec,
        vec[9:10],
    )


def solution(mesh):
    return jax.shard_map(
        on_device,
        mesh=mesh,
        in_specs=(
            PartitionSpec("dp", None, None),
            PartitionSpec("dp", None),
            PartitionSpec("section", "dp", None, None),
            PartitionSpec("section", None, None),
            PartitionSpec("section", None, None),
            PartitionSpec("section", None, None),
            PartitionSpec("section", None, None),
            PartitionSpec("section", None, None),
            PartitionSpec("section", None, None),
            PartitionSpec("section", None),
            PartitionSpec("section", None),
        ),
        out_specs=(
            PartitionSpec("section", "dp", None, None),
            PartitionSpec("section", "dp", None, None),
            PartitionSpec("section", None, "dp"),
            PartitionSpec("section", None, "dp"),
            PartitionSpec("section", None, "dp"),
            PartitionSpec("section", None, "dp"),
            PartitionSpec("section", None, "dp"),
            PartitionSpec("section", None, "dp"),
            PartitionSpec("section", "dp"),
            PartitionSpec("section", "dp"),
        ),
        check_vma=False,
    )
```

```python
import functools

import jax
import jax.numpy as jnp
from jax import lax
from jax.experimental import pallas as pl
from jax.experimental.pallas import tpu as pltpu
from jax.sharding import PartitionSpec

HEADS = 12
HEAD_DIM = 64
PAIRS = HEADS // 2
LANES = 2 * HEAD_DIM
MASK_LO = 59
MASK_HI = 117
TILE = 768

(
    W_IN,
    W_OUT,
    W_UP,
    W_DOWN,
    XS,
    H1,
    QKV,
    P,
    O,
    A,
    X1,
    H2,
    GP,
    GL,
    Y,
    SEND_DOWN,
    KEEP_UP,
    SEND_UP,
    GL_SEND,
    HO,
    KEEP_IO,
    SEND_IO,
    DA,
    DQKV,
    DY,
    DU,
    DO,
    VEC,
    MASK,
    TOKENS,
    LATENT,
    GAINS,
    BIASES,
    UP_BIAS,
    DOWN_BIAS,
    COT,
    RETURNED,
    SEND_DU,
    KEEP_DY,
    SEND_DY,
) = range(40)

UNROLL = 6
UNROLL_BACK = 3
MIB = 2**20

epsilon = 1e-06
f32 = jnp.float32
bf16 = jnp.bfloat16
ANY = pl.BlockSpec(memory_space=pl.ANY)
SMEM = pl.BlockSpec(memory_space=pltpu.SMEM)
VMEM = pl.BlockSpec(memory_space=pltpu.VMEM)


def cost(micros, memory=None):
    size = int((memory or micros) * 3.69e6)
    return pl.CostEstimate(flops=int(micros * 1.15e9), bytes_accessed=size, transcendentals=0)


def up16(count):
    return -(-count // 16) * 16


class Rows:
    def __init__(self, first, images, patches):
        most = patches - MASK_LO if first else MASK_HI
        self.first = first
        self.images = images
        self.patches = patches
        self.top = up16(most)
        self.rest = 0 if first else up16(patches - self.top)
        self.keys = self.top + self.rest
        self.queries = images * self.top
        self.total = images * self.keys


def dot(left, right):
    return jnp.dot(left, right, preferred_element_type=f32)


def dot_nt(left, right):
    return lax.dot_general(left, right, (((1,), (1,)), ((), ())), preferred_element_type=f32)


def dot_tn(left, right):
    return lax.dot_general(left, right, (((0,), (0,)), ((), ())), preferred_element_type=f32)


def iota(shape, dim):
    return lax.broadcasted_iota(jnp.int32, shape, dim)


def sort_rows(mask_ref, rows):
    masked = mask_ref[...].astype(f32)
    flag = 1.0 - masked if rows.first else masked
    n = rows.patches
    tri = jnp.where(iota((n, n), 0) <= iota((n, n), 1), 1.0, 0.0).astype(bf16)
    upto = dot(flag.astype(bf16), tri)
    count = jnp.sum(flag, axis=1, keepdims=True)
    at = iota(flag.shape, 1).astype(f32)
    place = jnp.where(flag > 0, upto - 1.0, count + at - upto)
    return flag, place, count


def pick(place, image, start, length):
    slots = iota((length, place.shape[1]), 0).astype(f32) + float(start)
    return jnp.where(slots == place[image : image + 1, :], 1.0, 0.0)


def valid_rows(count, rows):
    parts = [
        jnp.where(iota((rows.top, 1), 0).astype(f32) < count[b : b + 1, :], 1.0, 0.0)
        for b in range(rows.images)
    ]
    return jnp.concatenate(parts, axis=0)


def normed(states):
    centre = states - jnp.mean(states, axis=-1, keepdims=True)
    spread = jnp.mean(centre * centre, axis=-1, keepdims=True)
    scale = lax.rsqrt(spread + epsilon)
    return centre * scale, scale


def norm_back(grad, unit, scale, gain):
    inner = grad * gain
    along = jnp.mean(inner * unit, axis=-1, keepdims=True)
    return scale * (inner - jnp.mean(inner, axis=-1, keepdims=True) - unit * along)


def gelu_parts(values):
    size = jnp.abs(values) * (0.5**0.5)
    t = 1.0 / (1.0 + 0.3275911 * size)
    series = t * (
        0.254829592
        + t * (-0.284496736 + t * (1.421413741 + t * (-1.453152027 + t * 1.061405429)))
    )
    decay = jnp.exp(-0.5 * values * values)
    upper = 0.5 * series * decay
    below = jnp.where(values < 0, upper, 1.0 - upper)
    return below, decay * 0.3989422804014327


def total(values):
    return jnp.sum(values, axis=0, keepdims=True)


def key_rows(ref, image, lanes, rows):
    block = ref[image * rows.top : (image + 1) * rows.top, lanes]
    if rows.rest == 0:
        return block
    start = rows.queries + image * rows.rest
    return jnp.concatenate([block, ref[start : start + rows.rest, lanes]], axis=0)


class Copies:
    def __init__(self, sems):
        self.sems = sems
        self.used = 0

    def start(self, source, target):
        copy = pltpu.make_async_copy(source, target, self.sems.at[self.used])
        self.used += 1
        copy.start()
        return copy


SAVED = (XS, H1, QKV, P, O, A, X1, H2, GP, GL, Y)
WEIGHTS = (W_IN, W_OUT, W_UP, W_DOWN)


def kept_shapes(rows, width, hidden):
    queries = rows.queries
    return {
        W_IN: ((width, 3 * width), bf16),
        W_OUT: ((width, width), bf16),
        W_UP: ((width, hidden), bf16),
        W_DOWN: ((hidden, width), bf16),
        XS: ((rows.total, width), bf16),
        H1: ((rows.total, width), bf16),
        QKV: ((rows.total, 3 * width), bf16),
        P: ((rows.images * PAIRS, 2 * rows.top, rows.keys), bf16),
        O: ((queries, width), bf16),
        A: ((queries, width), bf16),
        X1: ((queries, width), f32),
        H2: ((queries, width), bf16),
        GP: ((queries, hidden), bf16),
        GL: ((queries, hidden), bf16),
        Y: ((queries, width), bf16),
        SEND_DOWN: ((queries, hidden // 2 + width), bf16),
        KEEP_UP: ((queries, hidden // 2), bf16),
        SEND_UP: ((queries, hidden // 2 + width), bf16),
        GL_SEND: ((queries, hidden // 2), bf16),
        HO: ((queries, 2 * width), bf16),
        KEEP_IO: ((queries, 2 * width), bf16),
        SEND_IO: ((queries + 16, 2 * width), bf16),
        DA: ((queries, width), bf16),
        DQKV: ((rows.total, 3 * width), bf16),
        DY: ((queries, width), bf16),
        DU: ((queries, hidden), bf16),
        SEND_DU: ((queries, hidden // 2), bf16),
        KEEP_DY: ((queries, width // 2), bf16),
        SEND_DY: ((queries, width // 2), bf16),
        DO: ((queries, width), bf16),
        VEC: ((16, width), f32),
    }


def bit_of(where_ref, order):
    return (where_ref[1] >> order) & 1


def active(where_ref, rows):
    return where_ref[0] == (0 if rows.first else 1)


def lane_sides():
    lane = iota((1, LANES), 1)
    sides = [(lane < HEAD_DIM), (lane >= HEAD_DIM)]
    return sides, [jnp.where(side, 1.0, 0.0).astype(bf16) for side in sides]


def two_heads(values, masks):
    return jnp.concatenate([values * masks[0], values * masks[1]], axis=0)


def mover(count, rows, image, start, length, height):
    behind = iota((length, height), 0) - iota((length, height), 1)
    behind = behind.astype(f32) + float(start) == count[image : image + 1, :]
    seen = iota((length, height), 1).astype(f32) < rows.patches - count[image : image + 1, :]
    return jnp.where(behind & seen, 1.0, 0.0).astype(bf16)


def forward_part(rows, order, small, held, wait, done):
    tok_ref, lat_ref = small[TOKENS], small[LATENT]
    gains_ref, biases_ref = small[GAINS], small[BIASES]
    flag, place, count = order
    images, top, queries = rows.images, rows.top, rows.queries
    width = held[W_OUT].shape[0]
    scale = HEAD_DIM**-0.5

    def states_of(b, start, length):
        chosen = pick(place, b, start, length)
        if rows.first:
            return dot(chosen.astype(bf16), tok_ref[:, b, :])
        from_tokens = dot((chosen * flag[b : b + 1, :]).astype(bf16), tok_ref[:, b, :])
        height = lat_ref.shape[0] // images
        move = mover(count, rows, b, start, length, height)
        return from_tokens + dot(move, lat_ref[b * height : (b + 1) * height])

    pieces = [states_of(b, 0, top) for b in range(images)]
    if rows.rest:
        pieces += [states_of(b, top, rows.rest) for b in range(images)]
    states = jnp.concatenate(pieces, axis=0)
    held[XS][...] = states.astype(bf16)
    done(XS)
    unit, _ = normed(states)
    h1 = (unit * gains_ref[0, 0:1, :] + biases_ref[0]).astype(bf16)
    held[H1][...] = h1
    done(H1)
    qkv = held[QKV]
    wi = held[W_IN]
    wait(W_IN)
    qkv[0:queries, 0:width] = (dot(h1[:queries], wi[:, :width]) + biases_ref[1]).astype(bf16)
    if rows.rest:
        qkv[queries:, 0:width] = jnp.zeros((rows.total - queries, width), bf16)
    qkv[:, width : 2 * width] = dot(h1, wi[:, width : 2 * width]).astype(bf16)
    qkv[:, 2 * width :] = (dot(h1, wi[:, 2 * width :]) + biases_ref[2]).astype(bf16)
    done(QKV)
    sides, masks = lane_sides()

    @pl.loop(0, PAIRS, unroll=UNROLL)
    def _(pair):
        lo = pl.multiple_of(pair * LANES, LANES)
        for b in range(images):
            q = qkv[b * top : (b + 1) * top, pl.ds(lo, LANES)]
            k = key_rows(qkv, b, pl.ds(width + lo, LANES), rows)
            v = key_rows(qkv, b, pl.ds(2 * width + lo, LANES), rows)
            at = iota((1, rows.keys), 1).astype(f32)
            if rows.first:
                usable = at < count[b : b + 1, :]
            else:
                usable = at < float(rows.patches)
            raw = dot_nt(two_heads(q, masks), k)
            logits = jnp.where(usable, raw * scale, -1e30)
            grown = jnp.exp(logits - jnp.max(logits, axis=-1, keepdims=True))
            p = (grown * (1.0 / jnp.sum(grown, axis=-1, keepdims=True))).astype(bf16)
            held[P][b * PAIRS + pair] = p
            mixed = dot(p, v)
            held[O][b * top : (b + 1) * top, pl.ds(lo, LANES)] = jnp.where(
                sides[0], mixed[:top], mixed[top:]
            ).astype(bf16)

    done(P)
    done(O)
    wait(W_OUT)
    a = dot(held[O][...], held[W_OUT][...]) + biases_ref[3]
    held[A][...] = a.astype(bf16)
    done(A)
    usable_rows = valid_rows(count, rows)
    x1 = states[:queries] + gains_ref[0, 1:2, :] * a * usable_rows
    held[X1][...] = x1
    done(X1)
    unit, _ = normed(x1)
    h2 = (unit * gains_ref[0, 2:3, :] + biases_ref[4]).astype(bf16)
    held[H2][...] = h2
    done(H2)
    wait(W_UP)
    y = jnp.zeros((queries, width), f32)
    for start in range(0, held[W_UP].shape[1], TILE):
        cols = slice(start, start + TILE)
        u = dot(h2, held[W_UP][:, cols]) + small[UP_BIAS][:, cols]
        below, density = gelu_parts(u)
        gl = (u * below).astype(bf16)
        held[GL][:, cols] = gl
        held[GP][:, cols] = (below + u * density).astype(bf16)
        done(GL, cols)
        done(GP, cols)
        wait(W_DOWN)
        y = y + dot(gl, held[W_DOWN][cols, :])
    done(GL_SEND)
    y = y + small[DOWN_BIAS][...]
    held[Y][...] = y.astype(bf16)
    done(Y)
    return (x1 + gains_ref[0, 3:4, :] * y * usable_rows).astype(bf16)


def part_shards(where_ref, values, keep, send, at):
    low_first = bit_of(where_ref, 0) == 0
    size = values.shape[1] // 16
    lanes = slice(at, at + 8 * size)
    height = values.shape[0]
    for own in range(2):
        picked = [values[:, j * size : (j + 1) * size] for j in range(own, 16, 2)]
        picked = jnp.concatenate(picked, axis=1)
        if own == 0:
            keep[:, lanes] = picked
        else:
            even = keep[:, lanes]
            keep[:, lanes] = jnp.where(low_first, even, picked)
            send[:height, lanes] = jnp.where(low_first, picked, even)


def backward_part(rows, order, where_ref, small, held, wait, done, dx_ref, ret_buf):
    cot_ref, gains_ref = small[COT], small[GAINS]
    flag, place, count = order
    images, top, queries = rows.images, rows.top, rows.queries
    hidden, width = held[W_DOWN].shape
    scale = HEAD_DIM**-0.5
    usable_rows = valid_rows(count, rows)
    vec = held[VEC]
    vec[...] = jnp.zeros(vec.shape, f32)
    pieces = []
    for b in range(images):
        chosen = (pick(place, b, 0, top) * flag[b : b + 1, :]).astype(bf16)
        piece = dot(chosen, cot_ref[0, :, b, :])
        if rows.first:
            piece = piece + small[RETURNED][b * top : (b + 1) * top].astype(f32)
        pieces.append(piece)
    grad = jnp.concatenate(pieces, axis=0)
    dy = (grad * gains_ref[0, 3:4, :] * usable_rows).astype(bf16)
    held[DY][...] = dy
    done(DY)
    if rows.first:
        part_shards(where_ref, held[DY], held[KEEP_DY], held[SEND_DY], 0)
        done(KEEP_DY)
        done(SEND_DY)
    wait(Y)
    vec[3:4, :] = total(grad * held[Y][...].astype(f32))
    vec[9:10, :] = total(dy.astype(f32))

    wait(W_DOWN)
    wait(GP)
    for step in range(hidden // TILE):
        cols = slice(step * TILE, (step + 1) * TILE)
        dgl = dot_nt(dy, held[W_DOWN][cols, :])
        du = (dgl * held[GP][:, cols].astype(f32)).astype(bf16)
        vec[10 + step : 11 + step, :] = total(du.astype(f32))
        held[DU][:, cols] = du
    done(DU)
    wait(W_UP)
    dh2 = dot_nt(held[DU][...], held[W_UP][...])

    wait(X1)
    unit, spread = normed(held[X1][...])
    vec[2:3, :] = total(dh2 * unit)
    vec[8:9, :] = total(dh2)
    dx1 = grad + norm_back(dh2, unit, spread, gains_ref[0, 2:3, :])
    da = (dx1 * gains_ref[0, 1:2, :] * usable_rows).astype(bf16)
    wait(A)
    vec[1:2, :] = total(dx1 * held[A][...].astype(f32) * usable_rows)
    vec[7:8, :] = total(da.astype(f32))
    held[DA][...] = da
    done(DA)
    do_ref = held[DO]
    wait(W_OUT)
    do_ref[...] = dot_nt(da, held[W_OUT][...]).astype(bf16)
    qkv, dqkv = held[QKV], held[DQKV]
    sides, masks = lane_sides()
    if rows.rest:
        dqkv[queries:, 0:width] = jnp.zeros((rows.total - queries, width), bf16)
    wait(QKV)
    wait(P)

    @pl.loop(0, PAIRS, unroll=UNROLL_BACK)
    def _(pair):
        lo = pl.multiple_of(pair * LANES, LANES)
        for b in range(images):
            q = qkv[b * top : (b + 1) * top, pl.ds(lo, LANES)]
            k = key_rows(qkv, b, pl.ds(width + lo, LANES), rows)
            v = key_rows(qkv, b, pl.ds(2 * width + lo, LANES), rows)
            do = two_heads(do_ref[b * top : (b + 1) * top, pl.ds(lo, LANES)], masks)
            p = held[P][b * PAIRS + pair]
            wide = p.astype(f32)
            dp = dot_nt(do, v)
            inner = jnp.sum(wide * dp, axis=-1, keepdims=True)
            draw = (wide * (dp - inner) * scale).astype(bf16)
            mixed = dot(draw, k)
            dq = jnp.where(sides[0], mixed[:top], mixed[top:])
            dk = dot_tn(draw, two_heads(q, masks))
            dv = dot_tn(p, do)
            for at, part in enumerate((dq, dk, dv)):
                part = part.astype(bf16)
                lanes = pl.ds(at * width + lo, LANES)
                dqkv[b * top : (b + 1) * top, lanes] = part[:top]
                if rows.rest and at > 0:
                    start = queries + b * rows.rest
                    dqkv[start : start + rows.rest, lanes] = part[top:]

    done(DQKV)
    if rows.first:
        part_shards(where_ref, dqkv, held[KEEP_IO], held[SEND_IO], 0)
        part_shards(where_ref, held[DA], held[KEEP_IO], held[SEND_IO], dqkv.shape[1] // 2)
        done(KEEP_IO)
    wait(W_IN)
    dh1 = jnp.zeros((rows.total, width), f32)
    for at in range(3):
        cols = slice(at * width, (at + 1) * width)
        dh1 = dh1 + dot_nt(dqkv[:, cols], held[W_IN][:, cols])
    wait(XS)
    unit, spread = normed(held[XS][...].astype(f32))
    dx = norm_back(dh1, unit, spread, gains_ref[0, 0:1, :])
    if rows.rest:
        rest = dx[queries:].astype(bf16)
    dx = dx[:queries] + dx1
    dx_ref[...] = dx
    if not rows.first:
        high = dx.astype(bf16)
        for b in range(images):
            height = ret_buf.shape[0] // images
            move = mover(count, rows, b, 0, rows.keys, height)
            part = slice(b * top, (b + 1) * top)
            tail = slice(b * rows.rest, (b + 1) * rows.rest)
            back = dot_tn(move[:top], high[part]) + dot_tn(move[top:], rest[tail])
            ret_buf[b * height : (b + 1) * height] = back.astype(bf16)
    vec[0:1, :] = total(dh1 * unit)
    vec[4:5, :] = total(dh1)
    vec[5:6, :] = total(dqkv[:, 0:width].astype(f32))
    vec[6:7, :] = total(dqkv[:, 2 * width :].astype(f32))
    done(VEC)
    if rows.first:
        held[SEND_IO][queries:, :width] = vec[...].astype(bf16)
        held[SEND_IO][queries:, width:] = jnp.zeros((16, width), bf16)
        done(SEND_IO)


class Flow:
    def __init__(self, held, sems, source):
        self.held = held
        self.source = source
        self.copies = Copies(sems)
        self.gets = {}
        self.later = {}
        self.puts = []

    def fetch(self, *names, after=None):
        if after is not None:
            self.later[after] = names
            return
        for name in names:
            ref = self.source[name]
            ref = ref.at[0] if name in WEIGHTS else ref
            self.gets[name] = self.copies.start(ref, self.held[name])

    def wait(self, name):
        if name in self.gets:
            self.gets.pop(name).wait()
            self.fetch(*self.later.pop(name, ()))

    def put(self, source, target):
        self.puts.append(self.copies.start(source, target))

    def finish(self):
        while self.gets:
            self.wait(next(iter(self.gets)))
        for copy in self.puts:
            copy.wait()


FORWARD_SMALL = (MASK, TOKENS, LATENT, GAINS, BIASES, UP_BIAS, DOWN_BIAS)
SECOND_SMALL = FORWARD_SMALL + (COT,)
BACK_SMALL = (MASK, COT, RETURNED, GAINS)
FIRST_HELD = WEIGHTS + SAVED
FIRST_OUTS = (XS, QKV, P, A, X1, H2, GP, GL, Y, HO)
SECOND_HELD = SAVED + (DA, DQKV, DY, DU, DO)
SECOND_OUTS = (H1, O, GL, SEND_DOWN, KEEP_UP, SEND_UP, DA, DQKV)
BACK_IN = WEIGHTS + (XS, QKV, P, A, X1, GP, Y)
BACK_OUTS = (KEEP_DY, SEND_DY, KEEP_UP, SEND_DU, KEEP_IO)
BACK_HELD = BACK_IN + (DA, DQKV, DO, DY, DU, KEEP_DY, SEND_DY, KEEP_IO)


def take_from(refs):
    def take(names):
        taken = dict(zip(names, refs))
        del refs[: len(names)]
        return taken

    return take


def part_du(flow, where_ref, keep, send):
    du = flow.held[DU]
    size = du.shape[1] // 8
    bit = bit_of(where_ref, 1)
    for target, own in ((keep, bit), (send, 1 - bit)):
        for z in range(4):
            start = pl.multiple_of((2 * z + own) * size, size)
            flow.put(du.at[:, pl.ds(start, size)], target.at[:, pl.ds(z * size, size)])


def other_half(where_ref, half):
    return pl.ds(pl.multiple_of((1 - bit_of(where_ref, 0)) * half, half), half)


def first_kernel(rows, where_ref, *refs):
    refs = list(refs)
    take = take_from(refs)
    small, weights = take(FORWARD_SMALL), take(WEIGHTS)
    x2_out, outs = refs.pop(0), take(FIRST_OUTS)
    held = take(FIRST_HELD)
    x2_buf, sems = refs

    @pl.when(active(where_ref, rows))
    def _():
        flow = Flow(held, sems, weights)
        flow.fetch(W_IN, W_OUT)
        flow.fetch(W_UP, W_DOWN, after=W_IN)
        order = sort_rows(small[MASK], rows)
        width = held[O].shape[1]

        def done(name, cols=None):
            if cols is not None:
                flow.put(held[name].at[:, cols], outs[name].at[:, cols])
            elif name in (H1, O):
                start = 0 if name == H1 else width
                flow.put(held[name], outs[HO].at[:, pl.ds(start, width)])
            elif name in outs:
                flow.put(held[name], outs[name])

        x2_buf[...] = forward_part(rows, order, small, held, flow.wait, done)
        flow.put(x2_buf, x2_out)
        flow.finish()


def hold_kernel(rows, where_ref, *refs):
    *refs, sems = refs
    half = len(refs) // 2

    @pl.when(active(where_ref, rows))
    def _():
        copies = Copies(sems)
        started = []
        for source, target in zip(refs[:half], refs[half:]):
            source = source.at[0] if len(source.shape) > len(target.shape) else source
            started.append(copies.start(source, target))
        for copy in started:
            copy.wait()


def hold(rows, where, arrays):
    return pl.pallas_call(
        functools.partial(hold_kernel, rows),
        out_shape=[jax.ShapeDtypeStruct(a.shape[-2:], a.dtype) for a in arrays],
        in_specs=[SMEM] + [ANY] * len(arrays),
        out_specs=[VMEM] * len(arrays),
        scratch_shapes=[pltpu.SemaphoreType.DMA((len(arrays),))],
        compiler_params=pltpu.CompilerParams(vmem_limit_bytes=18 * MIB),
        cost_estimate=cost(30, 3000),
        name="hold",
    )(where, *arrays)


def big_call(kernel, operands, in_specs, direct, outs, scratch, name, micros):
    return pl.pallas_call(
        kernel,
        out_shape=direct + outs,
        in_specs=in_specs,
        out_specs=[VMEM] * len(direct) + [ANY] * len(outs),
        scratch_shapes=scratch,
        compiler_params=pltpu.CompilerParams(vmem_limit_bytes=(32 if micros == 3000 else 56) * MIB),
        cost_estimate=cost(micros),
        name=name,
    )(*operands)


def shaped(shapes, names, make):
    return [make(*shapes[name]) for name in names]


def first_block(rows, where, small, weights):
    width, hidden = weights[2].shape[1:]
    shapes = kept_shapes(rows, width, hidden)
    results = big_call(
        functools.partial(first_kernel, rows),
        [where] + [small[name] for name in FORWARD_SMALL] + list(weights),
        [SMEM] + [VMEM] * len(FORWARD_SMALL) + [ANY] * 4,
        [],
        [jax.ShapeDtypeStruct((rows.queries, width), bf16)]
        + shaped(shapes, FIRST_OUTS, jax.ShapeDtypeStruct),
        shaped(shapes, FIRST_HELD, pltpu.VMEM)
        + [pltpu.VMEM((rows.queries, width), bf16), pltpu.SemaphoreType.DMA((48,))],
        "first_block",
        1500,
    )
    return results[0], dict(zip(FIRST_OUTS, results[1:]))


def second_kernel(rows, where_ref, *refs):
    refs = list(refs)
    take = take_from(refs)
    small, resident = take(SECOND_SMALL), take(WEIGHTS)
    ret_out, dx_out, x2_out, vec_out = (refs.pop(0) for _ in range(4))
    outs = take(SECOND_OUTS)
    held = take(SECOND_HELD)
    held.update(resident)
    held[VEC] = vec_out
    (sems,) = refs

    @pl.when(active(where_ref, rows))
    def _():
        flow = Flow(held, sems, resident)
        order = sort_rows(small[MASK], rows)
        half = held[DU].shape[1] // 2
        width = held[DY].shape[1]

        def done(name, cols=None):
            if cols is not None:
                if name in outs:
                    flow.put(held[name].at[:, cols], outs[name].at[:, cols])
            elif name == GL_SEND:
                flow.put(
                    held[GL].at[:, other_half(where_ref, half)],
                    outs[SEND_DOWN].at[:, pl.ds(0, half)],
                )
            elif name == H2:
                flow.put(held[H2], outs[SEND_UP].at[:, pl.ds(half, width)])
            elif name == DY:
                flow.put(held[DY], outs[SEND_DOWN].at[:, pl.ds(half, width)])
            elif name == DU:
                part_du(flow, where_ref, outs[KEEP_UP], outs[SEND_UP])
            elif name in outs:
                flow.put(held[name], outs[name])

        x2_out[...] = forward_part(rows, order, small, held, flow.wait, done)
        backward_part(rows, order, where_ref, small, held, flow.wait, done, dx_out, ret_out)
        flow.finish()


def second_block(rows, where, small, weights, resident, back_rows):
    width, hidden = weights[2].shape[1:]
    shapes = kept_shapes(rows, width, hidden)
    results = big_call(
        functools.partial(second_kernel, rows),
        [where] + [small[name] for name in SECOND_SMALL] + list(resident),
        [SMEM] + [VMEM] * (len(SECOND_SMALL) + 4),
        [
            jax.ShapeDtypeStruct((back_rows, width), bf16),
            jax.ShapeDtypeStruct((rows.queries, width), f32),
            jax.ShapeDtypeStruct((rows.queries, width), bf16),
            jax.ShapeDtypeStruct((16, width), f32),
        ],
        shaped(shapes, SECOND_OUTS, jax.ShapeDtypeStruct),
        shaped(shapes, SECOND_HELD, pltpu.VMEM) + [pltpu.SemaphoreType.DMA((48,))],
        "second_block",
        3000,
    )
    ret, dx, x2, vec = results[:4]
    return ret, dx, x2, {**dict(zip(SECOND_OUTS, results[4:])), VEC: vec}


def back_kernel(rows, where_ref, *refs):
    refs = list(refs)
    take = take_from(refs)
    small, source = take(BACK_SMALL), take(BACK_IN)
    dx_out, vec_out, send_out = (refs.pop(0) for _ in range(3))
    outs = take(BACK_OUTS)
    held = take(BACK_HELD)
    held[VEC], held[SEND_IO] = vec_out, send_out
    (sems,) = refs

    @pl.when(active(where_ref, rows))
    def _():
        flow = Flow(held, sems, source)
        flow.fetch(Y, W_DOWN, GP)
        flow.fetch(W_UP, X1, after=W_DOWN)
        flow.fetch(A, W_OUT, QKV, P, W_IN, XS, after=W_UP)

        def done(name):
            if name == DU:
                part_du(flow, where_ref, outs[KEEP_UP], outs[SEND_DU])
            elif name in outs:
                flow.put(held[name], outs[name])

        backward_part(
            rows,
            sort_rows(small[MASK], rows),
            where_ref,
            small,
            held,
            flow.wait,
            done,
            dx_out,
            None,
        )
        flow.finish()


def back_block(rows, where, small, weights, saved):
    width, hidden = weights[2].shape[1:]
    shapes = kept_shapes(rows, width, hidden)
    values = {**saved, **dict(zip(WEIGHTS, weights))}
    operands = [where] + [small[name] for name in BACK_SMALL]
    operands += [values[name] for name in BACK_IN]
    results = big_call(
        functools.partial(back_kernel, rows),
        operands,
        [SMEM] + [VMEM] * len(BACK_SMALL) + [ANY] * len(BACK_IN),
        [jax.ShapeDtypeStruct((rows.queries, width), f32)]
        + shaped(shapes, (VEC, SEND_IO), jax.ShapeDtypeStruct),
        shaped(shapes, BACK_OUTS, jax.ShapeDtypeStruct),
        shaped(shapes, BACK_HELD, pltpu.VMEM) + [pltpu.SemaphoreType.DMA((48,))],
        "back_block",
        2000,
    )
    return results[0], {**dict(zip((VEC, SEND_IO) + BACK_OUTS, results[1:]))}


class Order:
    def __init__(self, where):
        self.where = where
        self.last = None

    def call(self, kernel, rows, ins, outs, name, scratch=()):
        def body(where_ref, *refs):
            refs = list(refs)
            if extra:
                del refs[len(ins)]

            @pl.when(active(where_ref, rows))
            def _():
                kernel(where_ref, *refs)

        extra = [] if self.last is None else [self.last]
        results = pl.pallas_call(
            body,
            out_shape=outs,
            in_specs=[SMEM] + [VMEM] * len(ins) + [ANY] * len(extra),
            out_specs=[VMEM] * len(outs),
            scratch_shapes=list(scratch),
            compiler_params=pltpu.CompilerParams(vmem_limit_bytes=30 * MIB),
            cost_estimate=cost(30, 3000),
            name=name,
        )(self.where, *ins, *extra)
        self.last = results[-1]
        return results

    def gate(self, value):
        def body(value_ref, last_ref, out_ref):
            pass

        self.last = pl.pallas_call(
            body,
            out_shape=jax.ShapeDtypeStruct(value.shape, value.dtype),
            in_specs=[ANY] * 2,
            out_specs=ANY,
            input_output_aliases={0: 0},
            cost_estimate=cost(30, 3000),
            name="gate",
        )(value, self.last)
        return self.last


def vec_rows(vec_ref, d, lean):
    width = vec_ref.shape[1]
    long = 4 * lean
    at = long * d % width
    row = 10 + long * d // width
    block = jnp.zeros((16, width), f32)
    first = jnp.concatenate(
        [vec_ref[0:10, d * lean : (d + 1) * lean], jnp.zeros((10, width - lean), f32)], axis=1
    )
    second = jnp.concatenate(
        [vec_ref[row : row + 1, at : at + long], jnp.zeros((1, width - long), f32)], axis=1
    )
    return jnp.concatenate([first, second, block[11:]], axis=0)


def in_kernel(where_ref, dqkv_ref, h1_ref, da_ref, o_ref, vec_ref, *refs):
    keep_z, send_z, keep_y, send_y, buf = refs
    width = h1_ref.shape[1]
    lean, tall = width // 16, dqkv_ref.shape[1] // 16
    tile = dot_tn(da_ref[...], o_ref[...]).astype(bf16)
    for d in range(16):
        buf[d, :lean] = tile[d * lean : (d + 1) * lean]
    half = dqkv_ref.shape[1] // 2
    for step in range(2):
        tile = dot_tn(dqkv_ref[:, step * half : (step + 1) * half], h1_ref[...]).astype(bf16)
        for d in range(8):
            buf[8 * step + d, lean : lean + tall] = tile[d * tall : (d + 1) * tall]
    for d in range(16):
        buf[d, lean + tall :] = vec_rows(vec_ref, d, lean).astype(bf16)
    cut = keep_z.shape[1]
    y, z = bit_of(where_ref, 1), bit_of(where_ref, 2)
    for slot in range(8):
        high, other = slot >> 1, slot & 1
        keep_y[slot] = buf[4 * high + other + 2 * y, cut:]
        send_y[slot] = buf[4 * high + other + 2 * (1 - y), cut:]
        keep_z[slot] = buf[8 * other + high + 4 * z, :cut]
        send_z[slot] = buf[8 * other + high + 4 * (1 - z), :cut]


def in_back(order, rows, state):
    operands = [state[name] for name in (DQKV, H1, DA, O, VEC)]
    width = operands[1].shape[1]
    height, cut = width // 4 + 16, width // 8 + 16
    outs = [jax.ShapeDtypeStruct((8, size, width), bf16) for size in (cut, height - cut)]
    return order.call(
        in_kernel,
        rows,
        operands,
        [outs[0], outs[0], outs[1], outs[1]],
        "in_grad",
        [pltpu.VMEM((16, height, width), bf16)],
    )


def in_first_kernel(where_ref, own_ref, ho_ref, got_ref, got_ho_ref, vec_ref, keep, send, buf, sums):
    queries, width = own_ref.shape[0], vec_ref.shape[1]
    lean, tall = width // 16, 3 * width // 16
    edge = 8 * tall
    for lanes, part, height, at in (
        (slice(0, edge), slice(0, width), tall, lean),
        (slice(edge, 2 * width), slice(width, 2 * width), lean, 0),
    ):
        tile = joined(
            own_ref[:, lanes], got_ref[:queries, lanes], ho_ref[:, part], got_ho_ref[:, part]
        )
        for d in range(8):
            buf[d, at : at + height] = tile[d * height : (d + 1) * height]
    sums[...] = vec_ref[...] + got_ref[queries:, :width].astype(f32)
    low = bit_of(where_ref, 0) == 0
    for d in range(8):
        mine = jnp.where(low, vec_rows(sums, 2 * d, lean), vec_rows(sums, 2 * d + 1, lean))
        buf[d, lean + tall :] = mine.astype(bf16)
    bit = bit_of(where_ref, 1)
    for z in range(4):
        keep[z] = buf[2 * z + bit]
        send[z] = buf[2 * z + 1 - bit]


def in_first(order, rows, own, ho, got, got_ho, vec):
    width = vec.shape[1]
    shape = (width // 4 + 16, width)
    return order.call(
        in_first_kernel,
        rows,
        [own, ho, got, got_ho, vec],
        [jax.ShapeDtypeStruct((4,) + shape, bf16)] * 2,
        "in_grad",
        [pltpu.VMEM((8,) + shape, bf16), pltpu.VMEM(vec.shape, f32)],
    )


def joined(left, left_got, right, right_got):
    left = jnp.concatenate([left, left_got], axis=0)
    right = jnp.concatenate([right, right_got], axis=0)
    return dot_tn(left, right).astype(bf16)


def down_first_kernel(where_ref, dy, got_dy, gl, got_gl, keep, send, buf):
    height = buf.shape[1]
    width = keep.shape[2]
    tile = joined(dy[...], got_dy[...], gl[...], got_gl[...])
    for d in range(8):
        buf[d] = tile[d * height : (d + 1) * height]
    y = bit_of(where_ref, 1)
    for z in range(4):
        for part in range(4):
            rows = slice(part * height, (part + 1) * height)
            cols = slice(part * width, (part + 1) * width)
            keep[z, rows] = buf[2 * z + y, :, cols]
            send[z, rows] = buf[2 * z + 1 - y, :, cols]


def down_first(order, rows, ins, width):
    shape = (width // 16, ins[2].shape[1])
    outs = [jax.ShapeDtypeStruct((4, 4 * shape[0], width), bf16)] * 2
    scratch = [pltpu.VMEM((8,) + shape, bf16)]
    return order.call(down_first_kernel, rows, ins, outs, "down_grad", scratch)


def down_grad_kernel(where_ref, gl, own, got, keep, send, buf):
    height, half = buf.shape[1:]
    width = keep.shape[2]
    mine = pl.multiple_of(bit_of(where_ref, 0) * half, half)
    tile = joined(own[:, half:], got[:, half:], gl[:, pl.ds(mine, half)], got[:, :half])
    for d in range(16):
        buf[d] = tile[d * height : (d + 1) * height]
    bit = bit_of(where_ref, 2)
    for slot in range(4):
        base = 8 * (slot & 1) + (slot & 2)
        for x in range(2):
            for side in range(2):
                start = (2 * x + side) * height
                part = slice(start, start + height)
                cols = slice(side * width, (side + 1) * width)
                keep[slot, part] = buf[base + x + 4 * bit, :, cols]
                send[slot, part] = buf[base + x + 4 * (1 - bit), :, cols]


def down_grad(order, rows, ins, width):
    half = ins[0].shape[1] // 2
    shape = (width // 16, half)
    outs = [jax.ShapeDtypeStruct((4, 4 * shape[0], width), bf16)] * 2
    scratch = [pltpu.VMEM((16,) + shape, bf16)]
    return order.call(down_grad_kernel, rows, ins, outs, "down_grad", scratch)


def up_grad_kernel(where_ref, *refs):
    *ins, keep, send, buf = refs
    height = buf.shape[1]
    half = 8 * height
    bit = bit_of(where_ref, 0)
    if len(ins) == 4:
        du, h2, got_du, got_h2 = (ref[...] for ref in ins)
    else:
        du, own, got = ins
        du, h2, got_du, got_h2 = du[...], own[:, half:], got[:, :half], got[:, half:]
    tile = joined(du, got_du, h2, got_h2)
    for d in range(8):
        buf[d] = tile[d * height : (d + 1) * height]
    for z in range(4):
        keep[z] = buf[2 * z + bit]
        send[z] = buf[2 * z + 1 - bit]


def up_grad(order, rows, ins, width):
    shape = (ins[0].shape[1] // 8, width)
    outs = [jax.ShapeDtypeStruct((4,) + shape, bf16)] * 2
    scratch = [pltpu.VMEM((8,) + shape, bf16)]
    return order.call(up_grad_kernel, rows, ins, outs, "up_grad", scratch)


def swap(value, phase, bit, count):
    pairs = [(phase * count + i, phase * count + (i ^ (1 << bit))) for i in range(count)]
    return lax.ppermute(value, ("section", "dp"), pairs)


def halve_kernel(position, where_ref, *refs):
    *terms, keep, send = refs
    bit = bit_of(where_ref, position)
    at = 0
    for left, right in zip(terms[::2], terms[1::2]):
        part = slice(at, at + left.shape[1])
        at += left.shape[1]
        for slot in range(keep.shape[0]):
            mine, other = 2 * slot + bit, 2 * slot + 1 - bit
            keep[slot, part] = left[mine].astype(f32) + right[mine].astype(f32)
            sent = left[other].astype(f32) + right[other].astype(f32)
            send[slot, part] = sent.astype(bf16)


def halve(order, rows, phase, position, terms, count):
    height = sum(term.shape[1] for term in terms[::2])
    shape = (terms[0].shape[0] // 2, height, terms[0].shape[2])
    keep, send = order.call(
        functools.partial(halve_kernel, position),
        rows,
        terms,
        [jax.ShapeDtypeStruct(shape, f32), jax.ShapeDtypeStruct(shape, bf16)],
        "halve",
    )
    return [keep, swap(send, phase, position, count)]


def unsort_kernel(rows, where_ref, mask_ref, x2_ref, dx_ref, result, grads):
    flag, place, _ = sort_rows(mask_ref, rows)
    for b in range(rows.images):
        part = slice(b * rows.top, (b + 1) * rows.top)
        chosen = (pick(place, b, 0, rows.top) * flag[b : b + 1, :]).astype(bf16)
        dx = dx_ref[part]
        high = dx.astype(bf16)
        low = (dx - high.astype(f32)).astype(bf16)
        result[0, :, b, :] = dot_tn(chosen, x2_ref[part]).astype(bf16)
        grads[0, :, b, :] = dot_tn(chosen, high) + dot_tn(chosen, low)


def unsort(order, rows, mask, x2, dx):
    shape = (1, rows.patches, rows.images, x2.shape[1])
    outs = [jax.ShapeDtypeStruct(shape, kind) for kind in (bf16, f32)]
    return order.call(
        functools.partial(unsort_kernel, rows), rows, [mask, x2, dx], outs, "unsort"
    )


def both_terms(refs):
    return refs[0][0].astype(f32) + refs[1][0].astype(f32)


def side_kernel(where_ref, left, right, keep, send):
    height = keep.shape[0]
    low = bit_of(where_ref, 0) == 0
    both = left[0, : 2 * height].astype(f32) + right[0, : 2 * height].astype(f32)
    keep[...] = jnp.where(low, both[:height], both[height:])
    send[...] = jnp.where(low, both[height:], both[:height]).astype(bf16)


def side(order, rows, terms, lean):
    shape = (2 * lean, terms[0].shape[2])
    outs = [jax.ShapeDtypeStruct(shape, f32), jax.ShapeDtypeStruct(shape, bf16)]
    return order.call(side_kernel, rows, terms, outs, "side")


def down_end_kernel(where_ref, keep, got, out):
    lean, width = keep.shape[0] // 2, keep.shape[1]
    x = bit_of(where_ref, 0)
    for part in range(2):
        source = slice(part * lean, (part + 1) * lean)
        for ref, own in ((keep, x), (got, 1 - x)):
            start = pl.multiple_of((2 * own + part) * width, width)
            out[0, :, pl.ds(start, width)] = ref[source].astype(f32)


def down_first_end_kernel(where_ref, left, right, out):
    lean, width = out.shape[1], left.shape[2]
    for part in range(4):
        source = slice(part * lean, (part + 1) * lean)
        both = left[0, source].astype(f32) + right[0, source].astype(f32)
        out[0, :, part * width : (part + 1) * width] = both


def up_end_kernel(where_ref, left, right, out):
    tall = out.shape[1]
    start = left.shape[1] - tall
    out[0] = left[0, start:].astype(f32) + right[0, start:].astype(f32)


def in_end_kernel(where_ref, *refs):
    *terms, in_out, out_out, gain_out, bias_out, upb_out, downb_out = refs
    both = jnp.concatenate(
        [both_terms(pair) for pair in zip(terms[::2], terms[1::2])], axis=0
    )
    lean, tall = out_out.shape[1], upb_out.shape[1]
    out_out[0] = both[:lean]
    in_out[0] = both[lean:tall]
    gain_out[0] = both[tall : tall + 4, :lean]
    bias_out[:, 0, :] = both[tall + 4 : tall + 9, :lean]
    downb_out[...] = both[tall + 9 : tall + 10, :lean]
    upb_out[...] = both[tall + 10 : tall + 11, :tall]


def end(order, kernel, rows, terms, shapes, name):
    outs = [jax.ShapeDtypeStruct(shape, f32) for shape in shapes]
    return order.call(kernel, rows, terms, outs, name)


def on_device(
    tokens,
    patch_mask,
    cotangent,
    in_weight,
    out_weight,
    up_weight,
    down_weight,
    gains,
    biases,
    up_bias,
    down_bias,
):
    weights = (in_weight, out_weight, up_weight, down_weight, gains, biases, up_bias, down_bias)
    images, patches, width = tokens.shape
    hidden = up_weight.shape[2]
    count = lax.axis_size("dp")
    section = lax.axis_index("section")
    place = lax.axis_index("dp")
    is_first = section == 0
    where = jnp.stack([section, place]).astype(jnp.int32)
    x, y = place & 1, (place >> 1) & 1
    small = count == 16
    rows = [Rows(True, images, patches), Rows(False, images, patches)]

    small_args = {
        MASK: patch_mask,
        TOKENS: jnp.swapaxes(tokens, 0, 1),
        LATENT: gains,
        GAINS: gains,
        BIASES: jnp.swapaxes(biases, 0, 1),
        UP_BIAS: up_bias,
        DOWN_BIAS: down_bias,
        COT: jnp.swapaxes(cotangent, 1, 2),
    }
    matrices = weights[:4]
    sent, kept_first = first_block(rows[0], where, small_args, matrices)
    small_args[LATENT] = lax.ppermute(sent, "section", [(0, 1)])
    early = ()
    if small:
        early = tuple(
            swap(kept_first[name], 0, bit, count)
            for name, bit in ((HO, 0), (H2, 1), (GL, 0))
        )
    resident = hold(rows[1], where, matrices)
    back, dx_second, x2_second, state_second = second_block(
        rows[1], where, small_args, matrices, resident, rows[0].queries
    )
    returned = lax.ppermute(back, "section", [(1, 0)])

    def first_back(returned, saved):
        return back_block(rows[0], where, {**small_args, RETURNED: returned}, matrices, saved)

    def sums(order, phase):
        layout = rows[phase]
        lean, tall = width // 16, hidden // 16

        def step(position, terms):
            return halve(order, layout, phase, position, terms, count)

        def cross(terms):
            keep, send = side(order, layout, terms, lean)
            return [keep, swap(send, phase, 0, count)]

        def up_end(terms):
            return end(order, up_end_kernel, layout, terms, [(1, tall, width)], "up_end")

        def down_end(terms):
            kernel = down_end_kernel if phase else down_first_end_kernel
            return end(order, kernel, layout, terms, [(1, lean, hidden)], "down_end")

        def in_end(terms):
            shapes = [(1, 3 * lean, width), (1, lean, width), (1, 4, lean), (5, 1, lean)]
            shapes += [(1, tall), (1, lean)]
            return end(order, in_end_kernel, layout, terms, shapes, "in_end")

        return step, cross, up_end, down_end, in_end

    if small:

        def first_rest(returned, early, sent, saved, x2, dx, state):
            dx, state = first_back(returned, saved)
            got_ho, got_h2, got_gl = early
            got_dy = swap(state[SEND_DY], 0, 0, count)
            got_du = swap(state[SEND_DU], 0, 1, count)
            order = Order(where)
            order.last = state[VEC]
            got_io = swap(order.gate(state[SEND_IO]), 0, 0, count)
            keep, send = down_first(
                order, rows[0], [state[KEEP_DY], got_dy, saved[GL], got_gl], width
            )
            down = [keep, swap(send, 0, 1, count)]
            keep, send = up_grad(
                order, rows[0], [state[KEEP_UP], saved[H2], got_du, got_h2], width
            )
            up = [keep, swap(send, 0, 0, count)]
            keep, send = in_first(
                order, rows[0], state[KEEP_IO], saved[HO], got_io, got_ho, state[VEC]
            )
            rest = [keep, swap(send, 0, 1, count)]

            step, cross, up_end, down_end, in_end = sums(order, 0)
            down = step(2, down)
            up = step(2, up)
            outputs = unsort(order, rows[0], patch_mask, sent, dx)
            rest = step(2, rest)
            down = step(3, down)
            up = step(3, up)
            rest = step(3, rest)
            up = up_end(up)
            down = down_end(down)
            rest = in_end(rest)
            return *outputs, *rest[:2], *up, *down, *rest[2:]

        def second_rest(returned, early, sent, saved, x2, dx, state):
            got_up = swap(state[SEND_UP], 1, 1, count)
            got_down = swap(state[SEND_DOWN], 1, 0, count)
            order = Order(where)
            keep_z, send_z, keep_y, send_y = in_back(order, rows[1], state)
            upper = [keep_z, swap(send_z, 1, 2, count)]
            lower = [keep_y, swap(send_y, 1, 1, count)]
            keep, send = up_grad(
                order, rows[1], [state[KEEP_UP], state[SEND_UP], got_up], width
            )
            up = [keep, swap(send, 1, 0, count)]
            keep, send = down_grad(
                order, rows[1], [state[GL], state[SEND_DOWN], got_down], width
            )
            down = [keep, swap(send, 1, 2, count)]
            step, cross, up_end, down_end, in_end = sums(order, 1)
            lower = step(0, lower)
            upper = step(3, upper)
            up = step(2, up)
            down = step(3, down)
            lower = step(2, lower)
            upper = step(0, upper)
            up = step(3, up)
            outputs = unsort(order, rows[1], patch_mask, x2, dx)
            down = step(1, down)
            lower = step(3, lower)
            upper = step(1, upper)
            down = cross(down)
            up = up_end(up)
            down = down_end(down)
            rest = in_end(upper + lower)
            return *outputs, *rest[:2], *up, *down, *rest[2:]

        done = lax.cond(
            is_first,
            first_rest,
            second_rest,
            returned,
            early,
            sent,
            kept_first,
            x2_second,
            dx_second,
            state_second,
        )
        return (
            *(jnp.swapaxes(values, 1, 2) for values in done[:6]),
            done[6],
            jnp.swapaxes(done[7], 0, 1),
            *done[8:],
        )

    dx_first, state_first = first_back(returned, kept_first)
    order = Order(where)
    outputs_second = unsort(order, rows[1], patch_mask, x2_second, dx_second)
    outputs_first = unsort(order, rows[0], patch_mask, sent, dx_first)
    half = hidden // 2

    def merged(keep, send):
        parts = [keep.reshape(-1, 4, half // 4), send.reshape(-1, 4, half // 4)]
        both = jnp.where(y == 0, jnp.stack(parts, axis=2), jnp.stack(parts[::-1], axis=2))
        return both.reshape(-1, hidden)

    io = []
    for at, size in ((0, 3 * width), (3 * width // 2, width)):
        keep = state_first[KEEP_IO][:, at : at + size // 2].reshape(-1, 8, size // 16)
        send = state_first[SEND_IO][: keep.shape[0], at : at + size // 2]
        parts = [keep, send.reshape(-1, 8, size // 16)]
        both = jnp.where(x == 0, jnp.stack(parts, axis=2), jnp.stack(parts[::-1], axis=2))
        io.append(both.reshape(-1, size))
    keep = state_first[KEEP_DY].reshape(-1, 8, width // 16)
    parts = [keep, state_first[SEND_DY].reshape(-1, 8, width // 16)]
    dy_first = jnp.where(x == 0, jnp.stack(parts, axis=2), jnp.stack(parts[::-1], axis=2))
    dy_first = dy_first.reshape(-1, width)
    ho = kept_first[HO]
    first = [
        (io[0], ho[:, :width]),
        (io[1], ho[:, width:]),
        (merged(state_first[KEEP_UP], state_first[SEND_DU]), kept_first[H2]),
        (dy_first, kept_first[GL]),
    ]
    send = state_second[SEND_UP]
    second = [
        (state_second[DQKV], state_second[H1]),
        (state_second[DA], state_second[O]),
        (merged(state_second[KEEP_UP], send[:, :half]), send[:, half:]),
        (state_second[SEND_DOWN][:, half:], state_second[GL]),
    ]
    grads = [
        [*outputs_second, state_second[VEC], *(dot_tn(*pair) for pair in second)],
        [*outputs_first, state_first[VEC], *(dot_tn(*pair) for pair in first)],
    ]
    result, token_grads, vec, *finals = [
        jnp.where(is_first, left, right) for left, right in zip(grads[1], grads[0])
    ]
    finals = [lax.psum_scatter(f, "dp", scatter_dimension=0, tiled=True) for f in finals]
    vec = lax.psum(vec, "dp")
    lean, tall = width // count, hidden // count
    up_vec = vec[10:14].reshape(1, hidden)
    vec = lax.dynamic_slice_in_dim(vec, place * lean, lean, 1)
    up_vec = lax.dynamic_slice_in_dim(up_vec, place * tall, tall, 1)
    return (
        jnp.swapaxes(result, 1, 2),
        jnp.swapaxes(token_grads, 1, 2),
        *(final.T[None] for final in finals),
        vec[0:4][None],
        vec[4:9][None],
        up_vec,
        vec[9:10],
    )


def solution(mesh):
    return jax.shard_map(
        on_device,
        mesh=mesh,
        in_specs=(
            PartitionSpec("dp", None, None),
            PartitionSpec("dp", None),
            PartitionSpec("section", "dp", None, None),
            PartitionSpec("section", None, None),
            PartitionSpec("section", None, None),
            PartitionSpec("section", None, None),
            PartitionSpec("section", None, None),
            PartitionSpec("section", None, None),
            PartitionSpec("section", None, None),
            PartitionSpec("section", None),
            PartitionSpec("section", None),
        ),
        out_specs=(
            PartitionSpec("section", "dp", None, None),
            PartitionSpec("section", "dp", None, None),
            PartitionSpec("section", None, "dp"),
            PartitionSpec("section", None, "dp"),
            PartitionSpec("section", None, "dp"),
            PartitionSpec("section", None, "dp"),
            PartitionSpec("section", None, "dp"),
            PartitionSpec("section", None, "dp"),
            PartitionSpec("section", "dp"),
            PartitionSpec("section", "dp"),
        ),
        check_vma=False,
    )
```
